128 devices in a mesh: dp: 32 (over y, z_lo, x), group: 4 (over z_hi, core).
Axes of the slice: x: 4, y: 4, z: 4 (z_hi: 2, z_lo: 2; z = z_hi * 2 + z_lo), core: 2. Of those that a mesh axis runs over, the one named last changes fastest.
Arguments:
- tokens: bfloat16 [2, 32, 1024, 1024], P(None, 'dp', 'group'), may hold values from -6 to 6
- segments: int32 [2, 32, 1024], P(None, 'dp'), may hold values from 0 to 1023, as said below
- cotangent: bfloat16 [2, 32, 1024, 1024], P(None, 'dp', 'group'), may hold values from -6 to 6
- norm_gain: bfloat16 [1024], replicated, may hold values from 0.5 to 1.5
- in_weight: bfloat16 [1024, 4384], replicated, may hold values from -0.1875 to 0.1875
- conv_kernel: bfloat16 [4, 2304], replicated, may hold values from -3 to 3
- conv_bias: bfloat16 [2304], replicated, may hold values from -0.5 to 0.5
- step_bias: bfloat16 [32], replicated, may hold values from -6.5 to -2.5
- decay_log: bfloat16 [32], replicated, may hold values from 0 to 2.796875
- skip_gain: bfloat16 [32], replicated, may hold values from 0.5 to 1.5
- gate_gain: bfloat16 [2048], replicated, may hold values from 0.5 to 1.5
- out_weight: bfloat16 [2048, 1024], replicated, may hold values from -0.125 to 0.125
- master: float32 [6602752], P('dp'), may hold values from -0.75 to 0.75
- moment_one: float32 [6602752], P('dp'), may hold values from -0.00390625 to 0.00390625
- moment_two: float32 [6602752], P('dp'), may hold values from 1e-08 to 1e-06
- step_count: int32 [1], replicated, may hold values from 1 to 8
Outputs:
- output: bfloat16 [2, 32, 1024, 1024], P(None, 'dp', 'group')
- input_grad: bfloat16 [2, 32, 1024, 1024], P(None, 'dp', 'group')
- flat_grad: float32 [6602752], P('dp')
- moment_one_new: float32 [6602752], P('dp')
- moment_two_new: float32 [6602752], P('dp')
- master_new: float32 [6602752], P('dp')
- weights_copy: bfloat16 [6602752], replicated
The draws below stay inside these ranges and needn't reach their ends.
Inputs may be any that keep to these rules, and one draw needn't show every extreme that they name: `segments`: within each sequence the numbers start at 0, never fall and rise by at most one from a token to the next; of every 4 consecutive sequences of a micro-batch (sequences 0 to 3, 4 to 7 and so on) one is a single document; in every micro-batch one of sequences 0 to 3 starts a new document at every token.
All inputs are finite; a program needn't handle non-finite values.
Results may differ from the reference program's by a relative error of at most 0.0067.
Values may be sent and summed in bfloat16 or wider, within the bound.
No kernel may reach another device: no remote copies, remote signals or barrier semaphores. Data moves between devices by JAX's collectives and lax.ppermute only.
A program may use at most 256 MiB of HBM per device.

```python
import math
import jax
import jax.numpy as jnp
from jax import lax

D = 1024
DI = 2048
HEADS = 32
HDIM = 64
STATE = 128
KCONV = 4
SPAN = 256
MICRO = 2
CH = 2304
PROJ = 4384
SEQS = 32
LENGTH = 1024
NPARAM = 6601056
FLAT = 6602752


def draw_segments(key, part):
    key = jax.random.fold_in(key, 7)
    level_key, flag_key, pick_key, force_key = jax.random.split(key, 4)
    quads = SEQS // 4
    levels = jax.random.randint(level_key, (MICRO, SEQS, 1), 0, 4)
    limits = jnp.array([2, 8, 24, 64], jnp.int32)[levels]
    dice_rolls = jax.random.randint(flag_key, (MICRO, SEQS, LENGTH), 0, 1024)
    starts = (dice_rolls < limits).astype(jnp.int32)
    chosen = jax.random.randint(pick_key, (MICRO, quads, 1, 1), 0, 4)
    retained = (jnp.arange(4).reshape(1, 1, 4, 1) != chosen).astype(jnp.int32)
    starts = (starts.reshape(MICRO, quads, 4, LENGTH) * retained).reshape(MICRO, SEQS, LENGTH)
    forced_offset = jax.random.randint(force_key, (MICRO, 1), 1, 4)
    forced = (chosen[:, 0, 0, 0][:, None] + forced_offset) % 4
    every_token = (jnp.arange(SEQS)[None, :] == forced)[:, :, None]
    starts = jnp.where(every_token, 1, starts)
    starts = starts.at[:, :, 0].set(0)
    return jnp.cumsum(starts, axis=-1).astype(jnp.int32)


def shard_levels(stream_key, extent, cuts, least, top_value):
    def one(position, parts):
        steps = jax.random.uniform(jax.random.fold_in(jax.random.fold_in(stream_key, 6), position), (parts,), jnp.float32, least / len(cuts), top_value / len(cuts))
        return jnp.repeat(jnp.exp(steps), extent[position] // parts).reshape((-1,) + (1,) * (len(extent) - position - 1))

    level = one(*cuts[0])
    for cut in cuts[1:]:
        level = level * one(*cut)
    return level


def scatter_about(key, shape, deviation, bound, shards=(), held_as=jnp.bfloat16):
    values = jax.random.normal(key, shape, jnp.float32) * deviation
    if len(shards) > 0:
        values = shard_levels(key, shape, shards, -0.22, 0.18) * values
    return jnp.clip(values, min=-bound, max=bound).astype(held_as)


def setup_inputs(seed: int = 0) -> dict:
    key_list = jax.random.split(jax.random.key(seed), 17)
    return {
        "tokens": scatter_about(key_list[0], (MICRO, SEQS, LENGTH, D), 1.0, 6.0, ((1, 32), (2, 4))),
        "segments": draw_segments(jax.random.fold_in(key_list[16], 71), 0),
        "cotangent": scatter_about(key_list[2], (MICRO, SEQS, LENGTH, D), 1.0, 6.0, ((1, 32), (2, 4))),
        "norm_gain": jnp.clip(1.0 + 0.1 * jax.random.normal(key_list[3], (D,), jnp.float32), 0.5, 1.5).astype(jnp.bfloat16),
        "in_weight": scatter_about(key_list[4], (D, PROJ), D ** -0.5, 0.1875),
        "conv_kernel": scatter_about(key_list[5], (KCONV, CH), KCONV ** -0.5, 3.0),
        "conv_bias": jnp.clip(jax.random.uniform(key_list[6], (CH,), jnp.float32, -0.5, 0.5), -0.5, 0.5).astype(jnp.bfloat16),
        "step_bias": jnp.clip(jax.random.uniform(key_list[7], (HEADS,), jnp.float32, -6.5, -2.5), -6.5, -2.5).astype(jnp.bfloat16),
        "decay_log": jnp.clip(jax.random.uniform(key_list[8], (HEADS,), jnp.float32, 0.0, 2.796875), 0.0, 2.796875).astype(jnp.bfloat16),
        "skip_gain": jnp.clip(jax.random.uniform(key_list[9], (HEADS,), jnp.float32, 0.5, 1.5), 0.5, 1.5).astype(jnp.bfloat16),
        "gate_gain": jnp.clip(1.0 + 0.1 * jax.random.normal(key_list[10], (DI,), jnp.float32), 0.5, 1.5).astype(jnp.bfloat16),
        "out_weight": scatter_about(key_list[11], (DI, D), DI ** -0.5, 0.125),
        "master": scatter_about(key_list[12], (FLAT,), 0.05, 0.75, ((0, 32),), jnp.float32),
        "moment_one": scatter_about(key_list[13], (FLAT,), 0.0003, 0.00390625, ((0, 32),), jnp.float32),
        "moment_two": jnp.clip(jnp.exp(math.log(9.999999974752427e-07) - 4.6051702 * jax.random.uniform(key_list[14], (FLAT,), jnp.float32) ** shard_levels(key_list[14], (FLAT,), ((0, 32),), -0.2, 0.2)), 9.99999993922529e-09, 9.999999974752427e-07),
        "step_count": jax.random.randint(key_list[15], (1,), 1, 9).astype(jnp.int32),
    }


EPSILON = 1e-05
BETA_ONE = 0.9
BETA_TWO = 0.95
ADAM_EPSILON = 1e-08
LEARN_RATE = 0.01
WEIGHT_DECAY = 0.1
MAX_NORM = 1.0
HIGHEST_PRECISION = lax.Precision.HIGHEST

@jax.custom_vjp
def low(v):
    return lax.optimization_barrier(v.astype(jnp.bfloat16)).astype(jnp.float32)

@jax.custom_vjp
def low_back(v):
    return v

def low_keep(v):
    return (low(v), None)

def low_pass(kept, grad):
    return (grad,)

def back_keep(v):
    return (v, None)

def back_low(kept, grad):
    return (low(grad),)
low.defvjp(low_keep, low_pass)
low_back.defvjp(back_keep, back_low)

def norm_piece(values, scaling):
    factor = lax.rsqrt(lax.optimization_barrier(jnp.mean(values * values, axis=-1, keepdims=True)) + EPSILON)
    return values * factor * scaling

def prepare(padded, raw_steps, kernel, shift_bias, step_shift, decay_rate, tap_mask):
    length = raw_steps.shape[0]
    summed = shift_bias + tap_mask[0][:, None] * padded[0:length] * kernel[0]
    for offset in range(1, kernel.shape[0]):
        summed = summed + tap_mask[offset][:, None] * padded[offset:offset + length] * kernel[offset]
    active = jax.nn.silu(summed)
    signal = active[:, :DI]
    write_map = active[:, DI:DI + STATE]
    read_map = active[:, DI + STATE:]
    step_size = jax.nn.softplus(raw_steps + step_shift)
    log_decay = -step_size * jnp.exp(decay_rate)
    inflow = (signal * jnp.repeat(step_size, HDIM, axis=1)).reshape(length, HEADS, HDIM)
    return (signal, inflow, write_map, read_map, log_decay)

def doc_masks(doc_ids, prior_id):
    places = jnp.arange(doc_ids.shape[0])
    same_doc = ((doc_ids[:, None] == doc_ids[None, :]) & (places[:, None] >= places[None, :])).astype(jnp.float32)
    carry_mask = (doc_ids == prior_id).astype(jnp.float32)
    end_mask = (doc_ids == doc_ids[-1]).astype(jnp.float32)
    total_mask = (doc_ids[-1] == prior_id).astype(jnp.float32)
    return (same_doc, carry_mask, end_mask, total_mask)

def mix_out(signal, inflow, write_map, read_map, cum_decay, state_in, gate_z, skip_gain, gate_gain, same_doc, carry_mask):
    spread = cum_decay[:, None, :] - cum_decay[None, :, :]
    inside = same_doc[:, :, None] > 0
    kernel = jnp.where(inside, jnp.exp(jnp.where(inside, spread, 0.0)), 0.0)
    intersection = jnp.dot(read_map, write_map.T, precision=HIGHEST_PRECISION)
    within = jnp.einsum('ijh,ij,jhp->ihp', kernel, intersection, inflow, precision=HIGHEST_PRECISION)
    entry = carry_mask[:, None] * jnp.exp(cum_decay)
    carried = jnp.einsum('is,hps->ihp', read_map, state_in, precision=HIGHEST_PRECISION) * entry[:, :, None]
    scanned = (within + carried).reshape(signal.shape) + signal * jnp.repeat(skip_gain, HDIM)
    gated = scanned * jax.nn.silu(gate_z)
    factor = lax.rsqrt(lax.optimization_barrier(jnp.mean(gated * gated, axis=-1, keepdims=True)) + EPSILON)
    return gated * factor * gate_gain

def mix_state(inflow, write_map, cum_decay, end_mask, total_mask):
    tail_weight = end_mask[:, None] * jnp.exp(cum_decay[-1][None, :] - cum_decay)
    local_state = jnp.einsum('jh,jhp,js->hps', tail_weight, inflow, write_map, precision=HIGHEST_PRECISION)
    through = total_mask * jnp.exp(cum_decay[-1])
    return (through, local_state)

def adam_update(clipped, master, moment_one, moment_two, step_count):
    first_moment = BETA_ONE * moment_one + (1.0 - BETA_ONE) * clipped
    second_moment = BETA_TWO * moment_two + (1.0 - BETA_TWO) * clipped * clipped
    step_real = step_count[0].astype(jnp.float32)
    first_hat = first_moment / (1.0 - jnp.power(BETA_ONE, step_real))
    second_hat = second_moment / (1.0 - jnp.power(BETA_TWO, step_real))
    updated = master - LEARN_RATE * (first_hat / (jnp.sqrt(second_hat) + ADAM_EPSILON) + WEIGHT_DECAY * master)
    return (first_moment, second_moment, updated)

def mixer(weights, inputs, doc_ids):
    norm_gain, in_weight, conv_kernel, conv_bias, step_bias, decay_log, skip_gain, gate_gain, out_weight = weights
    normed = low(norm_piece(inputs, norm_gain))
    projected = low_back(jnp.dot(normed, in_weight, precision=HIGHEST_PRECISION))
    gate_z = projected[:, :DI]
    conv_input = low(projected[:, DI:DI + CH])
    raw_steps = projected[:, DI + CH:]
    padded = jnp.concatenate([jnp.zeros((KCONV - 1, CH), jnp.float32), conv_input], axis=0)
    seg_padded = jnp.concatenate([jnp.full((KCONV - 1,), -1, jnp.int32), doc_ids])
    tap_mask = jnp.stack([seg_padded[offset:offset + LENGTH] == doc_ids for offset in range(KCONV)]).astype(jnp.float32)
    signal, inflow, write_map, read_map, log_decay = prepare(padded, raw_steps, conv_kernel, conv_bias, step_bias, decay_log, tap_mask)
    blocks = LENGTH // SPAN
    cum_decay = jnp.cumsum(log_decay.reshape(blocks, SPAN, HEADS), axis=1)
    prior_ids = seg_padded[KCONV - 2:KCONV - 2 + LENGTH:SPAN]
    blocked = (signal.reshape(blocks, SPAN, DI), inflow.reshape(blocks, SPAN, HEADS, HDIM), write_map.reshape(blocks, SPAN, STATE), read_map.reshape(blocks, SPAN, STATE), cum_decay, gate_z.reshape(blocks, SPAN, DI), doc_ids.reshape(blocks, SPAN), prior_ids)

    def advance(state, sequence):
        block_signal, block_inflow, block_write, block_read, block_decay, block_gate, block_ids, block_prior = sequence
        same_doc, carry_mask, end_mask, total_mask = doc_masks(block_ids, block_prior)
        gated_norm = mix_out(block_signal, block_inflow, block_write, block_read, block_decay, state, block_gate, skip_gain, gate_gain, same_doc, carry_mask)
        through, local_state = mix_state(block_inflow, block_write, block_decay, end_mask, total_mask)
        return (through[:, None, None] * state + local_state, gated_norm)
    initial = jnp.zeros((HEADS, HDIM, STATE), jnp.float32)
    gated_norm = lax.scan(jax.checkpoint(advance), initial, blocked)[1]
    branch = jnp.dot(low(gated_norm.reshape(LENGTH, DI)), out_weight, precision=HIGHEST_PRECISION)
    return inputs + branch

def reference(tokens, segments, cotangent, norm_gain, in_weight, conv_kernel, conv_bias, step_bias, decay_log, skip_gain, gate_gain, out_weight, master, moment_one, moment_two, step_count):
    weights = tuple((weight.astype(jnp.float32) for weight in (norm_gain, in_weight, conv_kernel, conv_bias, step_bias, decay_log, skip_gain, gate_gain, out_weight)))
    inputs = tokens.astype(jnp.float32).reshape(MICRO * SEQS, LENGTH, D)
    doc_ids = segments.reshape(MICRO * SEQS, LENGTH)

    def forward(weights, inputs):

        def advance(ignored, sequence):
            return (ignored, jax.checkpoint(mixer)(weights, sequence[0], sequence[1]))
        return lax.scan(advance, jnp.zeros((), jnp.float32), (inputs, doc_ids))[1]
    result, pullback = jax.vjp(forward, weights, inputs)
    weight_grads, input_grad = pullback(cotangent.astype(jnp.float32).reshape(result.shape))
    flat = jnp.concatenate([piece.reshape(-1) for piece in weight_grads] + [jnp.zeros((FLAT - NPARAM,), jnp.float32)])
    clip_factor = MAX_NORM / jnp.maximum(jnp.sqrt(jnp.sum(flat * flat)), MAX_NORM)
    first_moment, second_moment, updated = adam_update(flat * clip_factor, master, moment_one, moment_two, step_count)
    return (result.reshape(tokens.shape).astype(jnp.bfloat16), input_grad.reshape(tokens.shape).astype(jnp.bfloat16), flat, first_moment, second_moment, updated, updated.astype(jnp.bfloat16))
```

```python
import jax
import jax.numpy as jnp
from jax import lax
from jax.experimental import pallas as pl
from jax.experimental.pallas import tpu as pltpu
from jax.sharding import Mesh
from jax.sharding import PartitionSpec as P

D = 1024
DI = 2048
HEADS = 32
HDIM = 64
STATE = 128
KCONV = 4
CH = 2304
NPARAM = 6601056
DP = ("y", "zl", "x")
GROUP = ("zh", "core")


EPSILON = 1e-05
BETA_ONE = 0.9
BETA_TWO = 0.95
ADAM_EPSILON = 1e-08
LEARN_RATE = 0.01
WEIGHT_DECAY = 0.1
MAX_NORM = 1.0
HIGHEST_PRECISION = lax.Precision.HIGHEST


def from_behind(block, axis, distance):
    devices = range(lax.axis_size(axis))
    route = [(i - distance, i) for i in devices if i - distance in devices]
    return lax.ppermute(block, axis, route)


def carried_in(value, axis, join, neutral, backward):
    count, mine = (lax.axis_size(axis), lax.axis_index(axis))
    pieces = jax.tree.map(lambda part: lax.all_gather(part, axis), value)
    if backward:
        pieces = jax.tree.map(lambda part: part[::-1], pieces)
        mine = count - 1 - mine
    running = jax.tree.map(
        lambda part, zero: jnp.full_like(part, 0) + jnp.asarray(zero, part.dtype), value, neutral
    )

    def step(position, running):
        longer = join(running, jax.tree.map(lambda part: part[position], pieces))
        return jax.tree.map(lambda new, old: jnp.where(position < mine, new, old), longer, running)

    return lax.fori_loop(0, count - 1, step, running)


def sent_to_all(shard, axis):
    copies = jnp.broadcast_to(shard, (lax.axis_size(axis), *shard.shape))
    return lax.all_to_all(copies, axis, split_axis=0, concat_axis=0, tiled=True)


def over_copies(shard, axis):
    everything = sent_to_all(shard, axis)
    return jnp.sum(everything, axis=0)


LANES = 128
LINES = 51584
SHARD_LINES = 1612
IN_LINE = 8
MID_LINE = 35080
OUT_LINE = 35187
PIECE = 416
PARTS = ((0, 144), (144, 144), (288, 128))
TAIL_LINES = 51632
GROUP_LINES = 137
RING = {"x": ("x",), "y": ("y",), "z": ("zl", "zh")}
ROUTES = (("x", "z", "y"), ("y", "z", "x"), ("z", "x", "y"))


def ring_place(axis, i):
    i = i % 4
    return (i % 2) * 2 + i // 2 if axis == "z" else i


def from_offset(block, axis, distance):
    route = [(ring_place(axis, i + distance), ring_place(axis, i)) for i in range(4)]
    return lax.ppermute(block, RING[axis], route)


def swap_cores(block):
    return lax.ppermute(block, "core", [(0, 1), (1, 0)])


def position():
    z = 2 * lax.axis_index("zh") + lax.axis_index("zl")
    return jnp.stack([lax.axis_index("y"), z, lax.axis_index("x"), lax.axis_index("core")]).astype(jnp.int32)


def first_tile(shard):
    return (403 * shard) // 4


def pack_kernel(pos, left, right, gated, cot, gain_part, mid_part, *rest):
    keep, send = rest[:3], rest[3:6]
    flat, carry, edge, stage, sems = rest[6:]
    lane = lax.broadcasted_iota(jnp.int32, (256, LANES), 1)

    flat[0:IN_LINE, :] = gain_part[...]
    flat[MID_LINE : MID_LINE + 104, :] = mid_part[0:104, :]
    flat[MID_LINE + 104 : MID_LINE + 107, :] = mid_part[104:107, :]
    carry[...] = jnp.zeros_like(carry)
    for k in range(4):

        def put(tile, line, k=k):
            moved = pltpu.roll(tile, 32 * k, 1) if k else tile
            whole = jnp.where(lane < 32 * k, carry[...], moved) if k else moved
            flat[pl.ds(line, 256, stride=GROUP_LINES), :] = whole
            carry[...] = moved
            return whole

        def columns(j, _, k=k, put=put):
            block = right[:, pl.ds(pl.multiple_of(j * 512, 512), 512)]
            product = jnp.dot(left[k], block, preferred_element_type=jnp.float32)
            for t in range(4):
                put(product[:, t * LANES : (t + 1) * LANES], IN_LINE + 34 * k + 4 * j + t)
            return 0

        lax.fori_loop(0, 8, columns, 0)
        product = jnp.dot(left[k], right[:, 4096:4480], preferred_element_type=jnp.float32)
        for t in range(3):
            whole = put(product[:, t * LANES : (t + 1) * LANES], IN_LINE + 34 * k + 32 + t)
        carry[...] = whole

    edge[0:8, :] = mid_part[99:107, :]

    def rows(b, _):
        block = gated[pl.ds(pl.multiple_of(b * 256, 256), 256), :]
        product = jnp.dot(block, cot[...], preferred_element_type=jnp.float32)
        start = OUT_LINE + 2048 * b
        for t in range(7):
            flat[pl.ds(start + t, 256, stride=8), :] = product[:, t * LANES : (t + 1) * LANES]
        last = product[:, 7 * LANES :]
        edge[8:264, :] = last
        flat[pl.ds(start - 1, 256, stride=8), :] = jnp.where(lane < 96, edge[7:263, :], last)
        edge[0:8, :] = edge[256:264, :]
        return 0

    lax.fori_loop(0, 8, rows, 0)
    low = lax.broadcasted_iota(jnp.int32, (1, LANES), 1) < 96
    flat[OUT_LINE + 16383 : TAIL_LINES, :] = jnp.zeros((TAIL_LINES - OUT_LINE - 16383, LANES), jnp.float32)
    flat[OUT_LINE + 16383 : OUT_LINE + 16384, :] = jnp.where(low, edge[7:8, :], 0.0)

    my_y, my_z, my_x, my_core = pos[0], pos[1], pos[2], pos[3]

    def drain(slot):
        pltpu.make_async_copy(stage.at[slot], keep[0].at[pl.ds(0, PIECE)], sems.at[slot]).wait()

    def ship(i, _):
        slot = i % 2

        @pl.when(i >= 2)
        def _():
            drain(slot)

        shard, quarter = i // 4, i % 4
        line = 16 * first_tile(shard) + PIECE * quarter
        stage[slot] = flat[pl.ds(pl.multiple_of(line, 16), PIECE), :].astype(jnp.bfloat16)
        x, zl, y = shard % 4, (shard // 4) % 2, shard // 8
        z, core = 2 * (quarter // 2) + zl, quarter % 2
        off = {"y": (y - my_y + 4) % 4, "z": (z - my_z + 4) % 4, "x": (x - my_x + 4) % 4}
        for p, (start, size) in enumerate(PARTS):
            a, b, c = (off[axis] for axis in ROUTES[p])
            to = pl.ds(pl.multiple_of(((a * 4 + b) * 4 + c) * size, 16), size)
            source = stage.at[slot, pl.ds(start, size)]

            @pl.when(core == my_core)
            def _():
                pltpu.make_async_copy(source, keep[p].at[to], sems.at[slot]).start()

            @pl.when(core != my_core)
            def _():
                pltpu.make_async_copy(source, send[p].at[to], sems.at[slot]).start()

        return 0

    lax.fori_loop(0, 128, ship, 0)
    drain(0)
    drain(1)


def pack(pos, left, right, gated, cot, gain_part, mid_part):
    vmem, hbm = pl.BlockSpec(memory_space=pltpu.VMEM), pl.BlockSpec(memory_space=pl.ANY)
    shapes = [jax.ShapeDtypeStruct((64 * size, LANES), jnp.bfloat16) for _, size in PARTS]
    return pl.pallas_call(
        pack_kernel,
        out_shape=shapes + shapes,
        in_specs=[pl.BlockSpec(memory_space=pltpu.SMEM)] + [vmem] * 6,
        out_specs=[hbm] * 6,
        scratch_shapes=[
            pltpu.VMEM((TAIL_LINES, LANES), jnp.float32),
            pltpu.VMEM((256, LANES), jnp.float32),
            pltpu.VMEM((264, LANES), jnp.float32),
            pltpu.VMEM((2, PIECE, LANES), jnp.bfloat16),
            pltpu.SemaphoreType.DMA((2,)),
        ],
        compiler_params=pltpu.CompilerParams(vmem_limit_bytes=60 * 2**20),
        cost_estimate=pl.CostEstimate(flops=7_000_000_000, bytes_accessed=25_000_000, transcendentals=0),
        name="pack_gradients",
    )(pos, left, right, gated, cot, gain_part, mid_part)


def real(v):
    return v.astype(jnp.float32)


def low(v):
    return v.astype(jnp.bfloat16)


def reduce_pieces(keep, send):
    got = [swap_cores(block) for block in send]
    held = [low(real(mine) + real(other)) for mine, other in zip(keep, got)]

    def hop(block, axis, narrow):
        quarter = block.shape[0] // 4
        total = real(block[:quarter])
        moved = [to_offset(block[d * quarter : (d + 1) * quarter], axis, d) for d in range(1, 4)]
        for part in moved:
            total = total + real(part)
        return low(total) if narrow else total

    held = [hop(block, ROUTES[p][0], True) for p, block in enumerate(held)]
    n0, n1 = PARTS[0][1] * 4, PARTS[1][1] * 4
    both = jnp.concatenate(
        [part for d in range(4) for part in (held[0][d * n0 : (d + 1) * n0], held[1][d * n1 : (d + 1) * n1])]
    )
    both, third = hop(both, "z", True), hop(held[2], "x", True)
    n0, n2 = PARTS[0][1], PARTS[2][1]
    first, second = both[: 4 * n0], both[4 * n0 :]
    outer = jnp.concatenate(
        [part for d in range(4) for part in (first[d * n0 : (d + 1) * n0], third[d * n2 : (d + 1) * n2])]
    )
    outer, second = hop(outer, "y", False), hop(second, "x", False)
    return jnp.concatenate([outer[:n0], second, outer[n0:]])


def to_offset(block, axis, distance):
    route = [(ring_place(axis, i), ring_place(axis, i + distance)) for i in range(4)]
    return lax.ppermute(block, RING[axis], route)


def gather_pieces(piece):
    def spread(block, axis):
        return [block] + [from_offset(block, axis, d) for d in range(1, 4)]

    n0, n1, n2 = (size for _, size in PARTS)
    first, second, third = piece[:n0], piece[n0 : n0 + n1], piece[n0 + n1 :]
    outer = spread(jnp.concatenate([first, third]), "y")
    second = jnp.concatenate(spread(second, "x"))
    first = jnp.concatenate([block[:n0] for block in outer])
    third = jnp.concatenate([block[n0:] for block in outer])
    both = spread(jnp.concatenate([first, second]), "z")
    third = jnp.concatenate(spread(third, "x"))
    first = jnp.concatenate([block[: 4 * n0] for block in both])
    second = jnp.concatenate([block[4 * n0 :] for block in both])
    mine = spread(first, "x") + spread(second, "y") + spread(third, "z")
    return mine + [swap_cores(block) for block in mine]


def unpack_kernel(pos, *rest):
    sources, out = rest[:24], rest[24]
    tiles, sem = rest[25:]
    my_y, my_z, my_x, my_core = pos[0], pos[1], pos[2], pos[3]

    def place(p, static, outer, inner, core):
        off = dict(zip(ROUTES[p], (static, outer, inner)))
        y, z, x = (my_y + off["y"]) % 4, (my_z + off["z"]) % 4, (my_x + off["x"]) % 4
        shard = (y * 2 + z % 2) * 4 + x
        return shard, 2 * (z // 2) + core

    for p, (start, size) in enumerate(PARTS):
        for far in range(4):
            for other in range(2):
                source = sources[other * 12 + p * 4 + far]

                def move(i, _, p=p, far=far, other=other, source=source, start=start, size=size):
                    core = (my_core + other) % 2
                    shard, quarter = place(p, far, i // 4, i % 4, core)
                    line = pl.multiple_of(16 * first_tile(shard) + PIECE * quarter + start, 16)
                    here = pl.multiple_of(i * size, 16)
                    if p == 0:

                        @pl.when(quarter == 0)
                        def _():
                            pltpu.make_async_copy(
                                source.at[pl.ds(pl.multiple_of(here + 16, 16), size - 16)],
                                out.at[pl.ds(pl.multiple_of(line + 16, 16), size - 16)], sem
                            ).start()

                        @pl.when(quarter != 0)
                        def _():
                            pltpu.make_async_copy(source.at[pl.ds(here, size)], out.at[pl.ds(line, size)], sem).start()

                    elif p == 1:
                        pltpu.make_async_copy(source.at[pl.ds(here, size)], out.at[pl.ds(line, size)], sem).start()
                    else:

                        @pl.when(quarter == 3)
                        def _():
                            pltpu.make_async_copy(source.at[pl.ds(here, 80)], out.at[pl.ds(line, 80)], sem).start()

                        @pl.when(quarter != 3)
                        def _():
                            pltpu.make_async_copy(source.at[pl.ds(here, size)], out.at[pl.ds(line, size)], sem).start()

                    return 0

                lax.fori_loop(0, 16, move, 0)
    for far in range(4):
        for other in range(2):

            @pl.when((my_core + other) % 2 == 0)
            def _(far=far, other=other):
                def head(i, _):
                    shard, quarter = place(0, far, i // 4, i % 4, 0)

                    @pl.when(quarter == 0)
                    def _():
                        pltpu.make_async_copy(
                            sources[other * 12 + far].at[pl.ds(pl.multiple_of(i * 144, 16), 16)], tiles.at[0, shard], sem
                        ).start()

                    return 0

                lax.fori_loop(0, 16, head, 0)

            @pl.when((my_core + other) % 2 == 1)
            def _(far=far, other=other):
                def tail(i, _):
                    shard, quarter = place(2, far, i // 4, i % 4, 1)

                    @pl.when(quarter == 3)
                    def _():
                        x = shard % 4
                        skip = jnp.where((x == 1) | (x == 2), 80, 64)
                        pltpu.make_async_copy(
                            sources[other * 12 + 8 + far].at[pl.ds(pl.multiple_of(i * 128 + skip, 16), 16)],
                            tiles.at[1, shard],
                            sem,
                        ).start()

                    return 0

                lax.fori_loop(0, 16, tail, 0)
    moved = 128 * PIECE - 32 * 16 - 32 * 48
    pltpu.make_async_copy(out.at[pl.ds(0, moved)], out.at[pl.ds(0, moved)], sem).wait()
    pltpu.make_async_copy(tiles, tiles, sem).wait()
    row = lax.broadcasted_iota(jnp.int32, (16, LANES), 0)
    for shard in range(32):
        x = shard % 4
        if x:
            joined = jnp.where(row < (12 * x) % 16, real(tiles[1, shard - 1]), real(tiles[0, shard]))
            tiles[0, shard] = low(joined)
    for shard in range(32):
        pltpu.make_async_copy(tiles.at[0, shard], out.at[pl.ds(16 * ((403 * shard) // 4), 16)], sem).start()
    pltpu.make_async_copy(tiles.at[0], tiles.at[0], sem).wait()


def unpack(pos, pieces):
    hbm, vmem = pl.BlockSpec(memory_space=pl.ANY), pl.BlockSpec(memory_space=pltpu.VMEM)
    return pl.pallas_call(
        unpack_kernel,
        out_shape=jax.ShapeDtypeStruct((LINES, LANES), jnp.bfloat16),
        in_specs=[pl.BlockSpec(memory_space=pltpu.SMEM)] + [vmem] * 24,
        out_specs=hbm,
        scratch_shapes=[pltpu.VMEM((2, 32, 16, LANES), jnp.bfloat16), pltpu.SemaphoreType.DMA],
        compiler_params=pltpu.CompilerParams(vmem_limit_bytes=32 * 2**20),
        cost_estimate=pl.CostEstimate(flops=0, bytes_accessed=27_000_000, transcendentals=0),
        name="unpack_weights",
    )(pos, *pieces)


def norm_piece(values, scaling):
    factor = lax.rsqrt(jnp.mean(values * values, axis=-1, keepdims=True) + EPSILON)
    return values * factor * scaling


def prepare(padded, raw_steps, kernel, shift_bias, step_shift, decay_rate, tap_mask):
    length = raw_steps.shape[0]
    summed = shift_bias + tap_mask[0][:, None] * padded[0:length] * kernel[0]
    for offset in range(1, kernel.shape[0]):
        summed = (
            summed + tap_mask[offset][:, None] * padded[offset : offset + length] * kernel[offset]
        )
    active = jax.nn.silu(summed)
    signal = active[:, :DI]
    write_map = active[:, DI : DI + STATE]
    read_map = active[:, DI + STATE :]
    step_size = jax.nn.softplus(raw_steps + step_shift)
    log_decay = -step_size * jnp.exp(decay_rate)
    inflow = (signal * jnp.repeat(step_size, HDIM, axis=1)).reshape(length, HEADS, HDIM)
    return (signal, inflow, write_map, read_map, log_decay)


def doc_masks(doc_ids, prior_id):
    places = jnp.arange(doc_ids.shape[0])
    same_doc = (
        (doc_ids[:, None] == doc_ids[None, :]) & (places[:, None] >= places[None, :])
    ).astype(jnp.float32)
    carry_mask = (doc_ids == prior_id).astype(jnp.float32)
    end_mask = (doc_ids == doc_ids[-1]).astype(jnp.float32)
    total_mask = (doc_ids[-1] == prior_id).astype(jnp.float32)
    return (same_doc, carry_mask, end_mask, total_mask)


def mix_out(
    signal,
    inflow,
    write_map,
    read_map,
    cum_decay,
    state_in,
    gate_z,
    skip_gain,
    gate_gain,
    same_doc,
    carry_mask,
):
    spread = cum_decay[:, None, :] - cum_decay[None, :, :]
    inside = same_doc[:, :, None] > 0
    kernel = jnp.where(inside, jnp.exp(jnp.where(inside, spread, 0.0)), 0.0)
    intersection = jnp.dot(read_map, write_map.T, precision=HIGHEST_PRECISION)
    within = jnp.einsum(
        "ijh,ij,jhp->ihp", kernel, intersection, inflow, precision=HIGHEST_PRECISION
    )
    entry = carry_mask[:, None] * jnp.exp(cum_decay)
    carried = (
        jnp.einsum("is,hps->ihp", read_map, state_in, precision=HIGHEST_PRECISION)
        * entry[:, :, None]
    )
    scanned = (within + carried).reshape(signal.shape) + signal * jnp.repeat(skip_gain, HDIM)
    gated = scanned * jax.nn.silu(gate_z)
    factor = lax.rsqrt(jnp.mean(gated * gated, axis=-1, keepdims=True) + EPSILON)
    return gated * factor * gate_gain


def mix_state(inflow, write_map, cum_decay, end_mask, total_mask):
    tail_weight = end_mask[:, None] * jnp.exp(cum_decay[-1][None, :] - cum_decay)
    local_state = jnp.einsum(
        "jh,jhp,js->hps", tail_weight, inflow, write_map, precision=HIGHEST_PRECISION
    )
    through = total_mask * jnp.exp(cum_decay[-1])
    return (through, local_state)


def adam_update(clipped, master, moment_one, moment_two, step_count):
    first_moment = BETA_ONE * moment_one + (1.0 - BETA_ONE) * clipped
    second_moment = BETA_TWO * moment_two + (1.0 - BETA_TWO) * clipped * clipped
    step_real = step_count[0].astype(jnp.float32)
    first_hat = first_moment / (1.0 - jnp.power(BETA_ONE, step_real))
    second_hat = second_moment / (1.0 - jnp.power(BETA_TWO, step_real))
    updated = master - LEARN_RATE * (
        first_hat / (jnp.sqrt(second_hat) + ADAM_EPSILON) + WEIGHT_DECAY * master
    )
    return (first_moment, second_moment, updated)


def chain(earlier, later):
    first_decay, first_state = earlier
    second_decay, second_state = later
    return (first_decay * second_decay, second_decay[:, :, None, None] * first_state + second_state)


def back_chain(earlier, later):
    upper_decay, upper_grad = earlier
    lower_decay, lower_grad = later
    return (upper_decay * lower_decay, lower_grad + lower_decay[:, :, None, None] * upper_grad)


def contract_rows(left, right):
    return lax.dot_general(
        left, right, (((0,), (0,)), ((), ())), preferred_element_type=jnp.float32
    )


def contract_cols(left, right):
    return lax.dot_general(
        left, right, (((1,), (1,)), ((), ())), preferred_element_type=jnp.float32
    )


def shards(
    tokens,
    segments,
    cotangent,
    norm_gain,
    in_weight,
    conv_kernel,
    conv_bias,
    step_bias,
    decay_log,
    skip_gain,
    gate_gain,
    out_weight,
    master,
    moment_one,
    moment_two,
    step_count,
):
    micro_count = tokens.shape[0]
    seq_count = tokens.shape[1]
    span_len = tokens.shape[2]
    rim_width = KCONV - 1
    norm_real = norm_gain.astype(jnp.float32)
    kernel_real = conv_kernel.astype(jnp.float32)
    shifts_real = conv_bias.astype(jnp.float32)
    steps_real = step_bias.astype(jnp.float32)
    decays_real = decay_log.astype(jnp.float32)
    skips_real = skip_gain.astype(jnp.float32)
    gains_real = gate_gain.astype(jnp.float32)
    group_place = lax.axis_index(GROUP)
    filler = jnp.full((seq_count, rim_width), -1, jnp.int32)
    outputs = []
    input_grads = []
    totals = None
    factors = []
    for batch_index in range(micro_count):
        seg_window = lax.dynamic_slice_in_dim(
            jnp.concatenate([filler, segments[batch_index]], axis=1),
            group_place * span_len,
            span_len + rim_width,
            axis=1,
        )
        doc_ids = seg_window[:, rim_width:]
        prior_ids = seg_window[:, rim_width - 1]
        tap_mask = jnp.stack(
            [seg_window[:, offset : offset + span_len] == doc_ids for offset in range(KCONV)],
            axis=1,
        ).astype(jnp.float32)
        same_doc, carry_mask, end_mask, total_mask = jax.vmap(doc_masks)(doc_ids, prior_ids)
        rows_in = tokens[batch_index].reshape(-1, D).astype(jnp.float32)
        normed, norm_back = jax.vjp(norm_piece, rows_in, norm_real)
        normed_low = normed.astype(jnp.bfloat16)
        projected = jnp.dot(normed_low, in_weight, preferred_element_type=jnp.float32)
        gate_z = projected[:, :DI].reshape(seq_count, span_len, DI)
        conv_input = (
            projected[:, DI : DI + CH].astype(jnp.bfloat16).reshape(seq_count, span_len, CH)
        )
        raw_steps = projected[:, DI + CH :].reshape(seq_count, span_len, HEADS)
        received = from_behind(conv_input[:, span_len - rim_width :], GROUP, 1)
        padded = jnp.concatenate([received, conv_input], axis=1).astype(jnp.float32)

        def prep_all(padded, raw_steps, kernel, shift_bias, step_shift, decay_rate):
            signal, inflow, write_map, read_map, log_decay = jax.vmap(
                prepare, in_axes=(0, 0, None, None, None, None, 0)
            )(padded, raw_steps, kernel, shift_bias, step_shift, decay_rate, tap_mask)
            return (signal, inflow, write_map, read_map, jnp.cumsum(log_decay, axis=1))

        prepared, prep_back = jax.vjp(
            prep_all, padded, raw_steps, kernel_real, shifts_real, steps_real, decays_real
        )
        signal, inflow, write_map, read_map, cum_decay = prepared

        def state_all(inflow, write_map, cum_decay):
            return jax.vmap(mix_state)(inflow, write_map, cum_decay, end_mask, total_mask)

        (through, local_state), state_back = jax.vjp(state_all, inflow, write_map, cum_decay)
        identity_pair = (jnp.ones_like(through), jnp.zeros_like(local_state))
        state_in = carried_in((through, local_state), GROUP, chain, identity_pair, False)[1]

        def out_all(signal, inflow, write_map, read_map, cum_decay, state_in, gate_z, skips, gains):
            return jax.vmap(mix_out, in_axes=(0, 0, 0, 0, 0, 0, 0, None, None, 0, 0))(
                signal,
                inflow,
                write_map,
                read_map,
                cum_decay,
                state_in,
                gate_z,
                skips,
                gains,
                same_doc,
                carry_mask,
            )

        gated_norm, out_back = jax.vjp(
            out_all,
            signal,
            inflow,
            write_map,
            read_map,
            cum_decay,
            state_in,
            gate_z,
            skips_real,
            gains_real,
        )
        gated_low = gated_norm.reshape(-1, DI).astype(jnp.bfloat16)
        branch = jnp.dot(gated_low, out_weight, preferred_element_type=jnp.float32)
        outputs.append((rows_in + branch).astype(jnp.bfloat16).reshape(tokens.shape[1:]))
        upstream = cotangent[batch_index].reshape(-1, D)
        grad_mixed = contract_cols(upstream, out_weight).reshape(gated_norm.shape)
        (
            grad_signal,
            grad_inflow,
            grad_write,
            grad_read,
            grad_cum,
            grad_state,
            grad_gate,
            grad_skips,
            grad_gains,
        ) = out_back(grad_mixed)
        returned = carried_in((through, grad_state), GROUP, back_chain, identity_pair, True)[1]
        grad_through = jnp.sum(state_in * returned, axis=(2, 3))
        more_inflow, more_write, more_cum = state_back((grad_through, returned))
        grad_padded, grad_raw, grad_kernel, grad_shift, grad_stepb, grad_decay = prep_back(
            (
                grad_signal,
                grad_inflow + more_inflow,
                grad_write + more_write,
                grad_read,
                grad_cum + more_cum,
            )
        )
        rim_grads = from_behind(grad_padded[:, :rim_width], GROUP, -1)
        grad_conv = grad_padded[:, rim_width:] + jnp.concatenate(
            [jnp.zeros((seq_count, span_len - rim_width, CH), jnp.float32), rim_grads], axis=1
        )
        grad_projected = jnp.concatenate(
            [grad_gate.reshape(-1, DI), grad_conv.reshape(-1, CH), grad_raw.reshape(-1, HEADS)],
            axis=1,
        ).astype(jnp.bfloat16)
        grad_normed = contract_cols(grad_projected, in_weight)
        grad_rows, grad_norm_gain = norm_back(grad_normed)
        input_grads.append(
            (upstream.astype(jnp.float32) + grad_rows)
            .astype(jnp.bfloat16)
            .reshape(tokens.shape[1:])
        )
        current = (
            grad_norm_gain,
            grad_kernel,
            grad_shift,
            grad_stepb,
            grad_decay,
            grad_skips,
            grad_gains,
        )
        factors.append((normed_low, grad_projected, gated_low, upstream))
        totals = current if totals is None else jax.tree.map(jnp.add, totals, current)
    normed_low, grad_projected, gated_low, upstream = (jnp.concatenate(part) for part in zip(*factors))
    left = normed_low.T.reshape(D // 4, 4, -1).transpose(1, 0, 2)
    right = jnp.pad(grad_projected, ((0, 0), (0, 4608 - grad_projected.shape[1])))
    turned = jnp.concatenate([upstream[:, 32:], upstream[:, :32]], axis=1)
    middle = jnp.concatenate([piece.reshape(-1) for piece in totals[1:]] + [jnp.zeros((32 + 5 * LANES,), jnp.float32)])
    spot = position()
    packed = pack(spot, left, right, gated_low.T, turned, totals[0].reshape(-1, LANES), middle.reshape(-1, LANES))
    piece = reduce_pieces(packed[:3], packed[3:])
    window = lax.all_gather(piece, GROUP, axis=0, tiled=True)
    skew = (12 * lax.axis_index("x")) % 16
    shard = lax.dynamic_slice(window, (skew, 0), (SHARD_LINES, LANES)).reshape(-1)
    squares = over_copies(jnp.sum(shard * shard), DP)
    clip_factor = MAX_NORM / jnp.maximum(jnp.sqrt(squares), MAX_NORM)
    first_moment, second_moment, updated = adam_update(
        shard * clip_factor, master, moment_one, moment_two, step_count
    )
    blank = jnp.zeros_like(window)
    placed = low(lax.dynamic_update_slice(blank, updated.reshape(SHARD_LINES, LANES), (skew, 0)))
    mine = lax.dynamic_slice(placed, (PIECE * lax.axis_index(GROUP), 0), (PIECE, LANES))
    copies = unpack(spot, gather_pieces(mine)).reshape(-1)
    return (
        jnp.stack(outputs),
        jnp.stack(input_grads),
        shard,
        first_moment,
        second_moment,
        updated,
        copies,
    )


def solution(mesh):
    finer = Mesh(mesh.devices.reshape(4, 2, 4, 2, 2), ("y", "zl", "x", "zh", "core"))
    return jax.shard_map(
        shards,
        mesh=finer,
        in_specs=(
            P(None, DP, GROUP, None),
            P(None, DP, None),
            P(None, DP, GROUP, None),
            P(),
            P(),
            P(),
            P(),
            P(),
            P(),
            P(),
            P(),
            P(),
            P(DP),
            P(DP),
            P(DP),
            P(),
        ),
        out_specs=(
            P(None, DP, GROUP, None),
            P(None, DP, GROUP, None),
            P(DP),
            P(DP),
            P(DP),
            P(DP),
            P(),
        ),
        check_vma=False,
    )
```

```python
import functools

import jax
import jax.numpy as jnp
from jax import lax
from jax.experimental import pallas as pl
from jax.experimental.pallas import tpu as pltpu
from jax.sharding import Mesh
from jax.sharding import PartitionSpec as P

D = 1024
DI = 2048
HEADS = 32
HDIM = 64
STATE = 128
CH = 2304
DP = ("y", "zl", "x")
GROUP = ("zh", "core")


EPSILON = 1e-05
BETA_ONE = 0.9
BETA_TWO = 0.95
ADAM_EPSILON = 1e-08
LEARN_RATE = 0.01
WEIGHT_DECAY = 0.1
MAX_NORM = 1.0


def sent_to_all(shard, axis):
    copies = jnp.broadcast_to(shard, (lax.axis_size(axis), *shard.shape))
    return lax.all_to_all(copies, axis, split_axis=0, concat_axis=0, tiled=True)


def over_copies(shard, axis):
    everything = sent_to_all(shard, axis)
    return jnp.sum(everything, axis=0)


def norm_piece(values, scaling):
    factor = lax.rsqrt(jnp.mean(values * values, axis=-1, keepdims=True) + EPSILON)
    return values * factor * scaling


def adam_update(clipped, master, moment_one, moment_two, step_count):
    first_moment = BETA_ONE * moment_one + (1.0 - BETA_ONE) * clipped
    second_moment = BETA_TWO * moment_two + (1.0 - BETA_TWO) * clipped * clipped
    step_real = step_count[0].astype(jnp.float32)
    first_hat = first_moment / (1.0 - jnp.power(BETA_ONE, step_real))
    second_hat = second_moment / (1.0 - jnp.power(BETA_TWO, step_real))
    updated = master - LEARN_RATE * (
        first_hat / (jnp.sqrt(second_hat) + ADAM_EPSILON) + WEIGHT_DECAY * master
    )
    return (first_moment, second_moment, updated)


LANES = 128
LINES = 51584
SHARD_LINES = 1612
IN_LINE = 8
MID_LINE = 35080
OUT_LINE = 35187
PIECE = 416
SLOTS = 16
PARTS = ((0, 144), (144, 144), (288, 128))
TAIL_LINES = 51632
GROUP_LINES = 137
RING = {"x": ("x",), "y": ("y",), "z": ("zl", "zh")}
ROUTES = (("x", "z", "y"), ("y", "z", "X"), ("z", "x", "y"))


def ring_place(axis, i):
    i = i % 4
    return (i % 2) * 2 + i // 2 if axis == "z" else i


def from_offset(block, axis, distance):
    route = [(ring_place(axis, i + distance), ring_place(axis, i)) for i in range(4)]
    return lax.ppermute(block, RING[axis], route)


def swap_cores(block):
    return lax.ppermute(block, "core", [(0, 1), (1, 0)])


def position():
    return jnp.stack([lax.axis_index("y"), lax.axis_index("zl"), lax.axis_index("x"), lax.axis_index("core")]).astype(jnp.int32)


def first_tile(shard):
    return (403 * shard) // 4


def pack_kernel(pos, left, grad_gate, grad_ci, grad_raw, gated, cot, gain_part, mid_part, *rest):
    keep, send = rest[:3], rest[3:6]
    flat, carry, edge, stage, sems = rest[6:]
    lane = lax.broadcasted_iota(jnp.int32, (256, LANES), 1)

    flat[0:IN_LINE, :] = gain_part[...]
    flat[MID_LINE : MID_LINE + 104, :] = mid_part[0:104, :]
    flat[MID_LINE + 104 : MID_LINE + 107, :] = mid_part[104:107, :]
    def put(tile, k, line):
        moved = pltpu.roll(tile, 32 * k, 1) if k else tile
        whole = jnp.where(lane < 32 * k, carry[k], moved) if k else moved
        flat[pl.ds(IN_LINE + 34 * k + line, 256, stride=GROUP_LINES), :] = whole
        carry[k] = moved

    def columns(block, line, tiles):
        product = nt(left[...], block)
        for k in range(4):
            for t in range(tiles):
                put(product[256 * k : 256 * (k + 1), t * LANES : (t + 1) * LANES], k, line + t)

    def from_gate(j, _):
        columns(grad_gate[pl.ds(pl.multiple_of(j * 512, 512), 512), :], 4 * j, 4)
        return 0

    def from_conv(j, _):
        columns(grad_ci[pl.ds(pl.multiple_of(j * 512, 512), 512), :], 16 + 4 * j, 4)
        return 0

    lax.fori_loop(0, 4, from_gate, 0)
    lax.fori_loop(0, 4, from_conv, 0)
    heads = []
    for k in range(1, 4):
        heads.append(flat[pl.ds(IN_LINE + 34 * k, 256, stride=GROUP_LINES), :])
    columns(jnp.concatenate([grad_ci[2048:2304, :], grad_raw[...]], axis=0), 32, 3)
    for k in range(1, 4):
        at = pl.ds(IN_LINE + 34 * k, 256, stride=GROUP_LINES)
        flat[at, :] = jnp.where(lane < 32 * k, flat[at, :], heads[k - 1])

    edge[0:8, :] = mid_part[99:107, :]

    def rows(b, _):
        block = gated[pl.ds(pl.multiple_of(b * 256, 256), 256), :]
        product = jnp.dot(block, cot[...], preferred_element_type=jnp.float32)
        start = OUT_LINE + 2048 * b
        for t in range(7):
            flat[pl.ds(start + t, 256, stride=8), :] = product[:, t * LANES : (t + 1) * LANES]
        last = product[:, 7 * LANES :]
        edge[8:264, :] = last
        flat[pl.ds(start - 1, 256, stride=8), :] = jnp.where(lane < 96, edge[7:263, :], last)
        edge[0:8, :] = edge[256:264, :]
        return 0

    lax.fori_loop(0, 8, rows, 0)
    low = lax.broadcasted_iota(jnp.int32, (1, LANES), 1) < 96
    flat[OUT_LINE + 16383 : TAIL_LINES, :] = jnp.zeros((TAIL_LINES - OUT_LINE - 16383, LANES), jnp.float32)
    flat[OUT_LINE + 16383 : OUT_LINE + 16384, :] = jnp.where(low, edge[7:8, :], 0.0)

    my_y, my_x, my_core = pos[0], pos[2], pos[3]

    def drain(slot):
        pltpu.make_async_copy(stage.at[slot], keep[0].at[pl.ds(0, PIECE)], sems.at[slot]).wait()

    def ship(i, _):
        slot = i % SLOTS

        @pl.when(i >= SLOTS)
        def _():
            drain(slot)

        shard, quarter = i // 4, i % 4
        line = 16 * first_tile(shard) + PIECE * quarter
        stage[slot] = flat[pl.ds(pl.multiple_of(line, 16), PIECE), :].astype(jnp.bfloat16)
        x, zl, y = shard % 4, (shard // 4) % 2, shard // 8
        core = quarter % 2
        off = {"y": (y - my_y + 4) % 4, "z": 2 * zl + quarter // 2, "x": (x - my_x + 4) % 4, "X": x}
        for p, (start, size) in enumerate(PARTS):
            a, b, c = (off[axis] for axis in ROUTES[p])
            to = pl.ds(pl.multiple_of(((a * 4 + b) * 4 + c) * size, 16), size)
            source = stage.at[slot, pl.ds(start, size)]

            @pl.when(core == my_core)
            def _():
                pltpu.make_async_copy(source, keep[p].at[to], sems.at[slot]).start()

            @pl.when(core != my_core)
            def _():
                pltpu.make_async_copy(source, send[p].at[to], sems.at[slot]).start()

        return 0

    lax.fori_loop(0, 128, ship, 0)
    for slot in range(SLOTS):
        drain(slot)


def pack(pos, left, grad_gate, grad_ci, grad_raw, gated, cot, gain_part, mid_part):
    vmem, hbm = pl.BlockSpec(memory_space=pltpu.VMEM), pl.BlockSpec(memory_space=pl.ANY)
    shapes = [jax.ShapeDtypeStruct((64 * size, LANES), jnp.bfloat16) for _, size in PARTS]
    return pl.pallas_call(
        pack_kernel,
        out_shape=shapes + shapes,
        in_specs=[pl.BlockSpec(memory_space=pltpu.SMEM)] + [vmem] * 8,
        out_specs=[hbm] * 6,
        scratch_shapes=[
            pltpu.VMEM((TAIL_LINES, LANES), jnp.float32),
            pltpu.VMEM((4, 256, LANES), jnp.float32),
            pltpu.VMEM((264, LANES), jnp.float32),
            pltpu.VMEM((SLOTS, PIECE, LANES), jnp.bfloat16),
            pltpu.SemaphoreType.DMA((SLOTS,)),
        ],
        compiler_params=pltpu.CompilerParams(vmem_limit_bytes=60 * 2**20),
        cost_estimate=pl.CostEstimate(flops=7_000_000_000, bytes_accessed=25_000_000, transcendentals=0),
        name="pack_gradients",
    )(pos, left, grad_gate, grad_ci, grad_raw, gated, cot, gain_part, mid_part)


def real(v):
    return v.astype(jnp.float32)


def low(v):
    return v.astype(jnp.bfloat16)


def to_offset(block, axis, distance):
    route = [(ring_place(axis, i), ring_place(axis, i + distance)) for i in range(4)]
    return lax.ppermute(block, RING[axis], route)


def exchange(blocks, axis):
    blocks = blocks.reshape(4, -1, LANES)
    return lax.all_to_all(blocks, RING[axis], split_axis=0, concat_axis=0, tiled=True)


def quarters(block):
    return block.reshape(4, -1, LANES)


def ring_sum(block, axis):
    block = quarters(block)
    half = block.shape[1] // 32 * 16
    a, b = to_offset(block[2, :half], axis, 1), to_offset(block[2, half:], axis, 3)
    one = jnp.concatenate([low(real(block[1, :half]) + real(a)), block[1, half:]])
    three = jnp.concatenate([block[3, :half], low(real(block[3, half:]) + real(b))])
    return real(block[0]) + real(to_offset(one, axis, 1)) + real(to_offset(three, axis, 3))


def direct_sum(block, axis):
    block = quarters(block)
    moved = [to_offset(block[d], axis, d) for d in (1, 3, 2)]
    return real(block[0]) + real(moved[0]) + real(moved[1]) + real(moved[2])


def exchange_sum(block, axis):
    return jnp.sum(real(exchange(block, axis)), axis=0)


def reduce_pieces(keep, send):
    held = [None] * 3
    for p in (2, 0, 1):
        held[p] = low(real(keep[p]) + real(swap_cores(send[p])))
    third = low(exchange_sum(held[2], "z"))
    first, second = low(ring_sum(held[0], "x")), low(ring_sum(held[1], "y"))
    both = jnp.concatenate([quarters(first), quarters(second)], axis=1)
    both, third = low(exchange_sum(both, "z")), low(direct_sum(third, "x"))
    n0, n2 = PARTS[0][1], PARTS[2][1]
    first, second = both[: 4 * n0], both[4 * n0 :]
    outer = jnp.concatenate([quarters(first), quarters(third)], axis=1)
    second, outer = exchange_sum(second, "x"), direct_sum(outer, "y")
    return jnp.concatenate([outer[:n0], second, outer[n0:]])


def gather_pieces(piece):
    def spread(block, axis):
        return [block] + [from_offset(block, axis, d) for d in (1, 3, 2)]

    def in_order(parts):
        return jnp.concatenate([parts[0], parts[1], parts[3], parts[2]])

    def exchanged(block, axis):
        return exchange(jnp.broadcast_to(block, (4, *block.shape)), axis)

    n0, n1, n2 = (size for _, size in PARTS)
    first, second, third = piece[:n0], piece[n0 : n0 + n1], piece[n0 + n1 :]
    second = exchanged(second, "x").reshape(-1, LANES)
    outer = spread(jnp.concatenate([first, third]), "y")
    first = in_order([block[:n0] for block in outer])
    third = in_order([block[n0:] for block in outer])
    both = exchanged(jnp.concatenate([first, second]), "z")
    third = in_order(spread(third, "x"))
    first = both[:, : 4 * n0].reshape(-1, LANES)
    second = both[:, 4 * n0 :].reshape(-1, LANES)
    third = exchanged(third, "z").reshape(-1, LANES)

    def ring(block, axis):
        right, left = from_offset(block, axis, 3), from_offset(block, axis, 1)
        return right, left

    around = [ring(first, "x"), ring(second, "y")]
    mine = []
    for block, axis, (right, left) in zip((first, second), "xy", around):
        half = block.shape[0] // 2
        mine += [block, right, left, from_offset(right[:half], axis, 3), from_offset(left[half:], axis, 1)]
    mine.append(third)
    return mine + [swap_cores(block) for block in mine]


def unpack_kernel(pos, *rest):
    sources, out = rest[:22], rest[22]
    tiles, sem = rest[23:]
    my_y, my_x, my_core = pos[0], pos[2], pos[3]

    def place(p, a, b, c, core):
        off = dict(zip(ROUTES[p], (a, b, c)))
        y = (my_y + off["y"]) % 4
        x = off["X"] if p == 1 else (my_x + off["x"]) % 4
        return (y * 2 + off["z"] // 2) * 4 + x, 2 * (off["z"] % 2) + core

    table = []
    for p in range(2):
        for far, array, start, end in ((0, 0, 0, 16), (3, 1, 0, 16), (1, 2, 0, 16), (2, 3, 0, 8), (2, 4, 8, 16)):
            table.append((p, far, 5 * p + array, start, end))
    table += [(2, far, 10, 0, 16) for far in range(4)]

    def copy(source, here, line, size):
        here, line = pl.multiple_of(here, 16), pl.multiple_of(line, 16)
        pltpu.make_async_copy(source.at[pl.ds(here, size)], out.at[pl.ds(line, size)], sem).start()

    for other in range(2):
        core = (my_core + other) % 2
        for p, far, array, begin, end in table:
            source = sources[11 * other + array]
            start, size = PARTS[p]

            def move(i, _, p=p, far=far, source=source, begin=begin, start=start, size=size, core=core):
                shard, quarter = place(p, far, i // 4, i % 4, core)
                line = 16 * first_tile(shard) + PIECE * quarter + start
                here = (i - begin + (16 * far if p == 2 else 0)) * size
                if p == 0:

                    @pl.when(quarter == 0)
                    def _():
                        copy(source, here + 16, line + 16, size - 16)
                        pltpu.make_async_copy(
                            source.at[pl.ds(pl.multiple_of(here, 16), 16)], tiles.at[0, shard], sem
                        ).start()

                    @pl.when(quarter != 0)
                    def _():
                        copy(source, here, line, size)

                elif p == 1:
                    copy(source, here, line, size)
                else:

                    @pl.when(quarter == 3)
                    def _():
                        copy(source, here, line, 80)
                        x = shard % 4
                        skip = jnp.where((x == 1) | (x == 2), 80, 64)
                        pltpu.make_async_copy(
                            source.at[pl.ds(pl.multiple_of(here + skip, 16), 16)], tiles.at[1, shard], sem
                        ).start()

                    @pl.when(quarter != 3)
                    def _():
                        copy(source, here, line, size)

                return 0

            lax.fori_loop(begin, end, move, 0)
    moved = 128 * PIECE - 32 * 16 - 32 * 48
    pltpu.make_async_copy(out.at[pl.ds(0, moved)], out.at[pl.ds(0, moved)], sem).wait()
    pltpu.make_async_copy(tiles, tiles, sem).wait()
    row = lax.broadcasted_iota(jnp.int32, (16, LANES), 0)
    for shard in range(32):
        x = shard % 4
        if x:
            joined = jnp.where(row < (12 * x) % 16, real(tiles[1, shard - 1]), real(tiles[0, shard]))
            tiles[0, shard] = low(joined)
    for shard in range(32):
        pltpu.make_async_copy(tiles.at[0, shard], out.at[pl.ds(16 * ((403 * shard) // 4), 16)], sem).start()
    pltpu.make_async_copy(tiles.at[0], tiles.at[0], sem).wait()


def unpack(pos, pieces):
    hbm, vmem = pl.BlockSpec(memory_space=pl.ANY), pl.BlockSpec(memory_space=pltpu.VMEM)
    return pl.pallas_call(
        unpack_kernel,
        out_shape=jax.ShapeDtypeStruct((LINES, LANES), jnp.bfloat16),
        in_specs=[pl.BlockSpec(memory_space=pltpu.SMEM)] + [vmem] * 22,
        out_specs=hbm,
        scratch_shapes=[pltpu.VMEM((2, 32, 16, LANES), jnp.bfloat16), pltpu.SemaphoreType.DMA],
        compiler_params=pltpu.CompilerParams(vmem_limit_bytes=32 * 2**20),
        cost_estimate=pl.CostEstimate(flops=0, bytes_accessed=27_000_000, transcendentals=0),
        name="unpack_weights",
    )(pos, *pieces)


SPAN = 256
MICRO = 2
GROUPS = 8
ROWS = 256
F32 = jnp.float32


def nt(left, right, precision=None):
    return lax.dot_general(left, right, (((1,), (1,)), ((), ())), precision=precision, preferred_element_type=F32)


def tn(left, right, precision=None):
    return lax.dot_general(left, right, (((0,), (0,)), ((), ())), precision=precision, preferred_element_type=F32)


def nn(left, right, precision=None):
    return lax.dot_general(left, right, (((1,), (0,)), ((), ())), precision=precision, preferred_element_type=F32)


def sigmoid(v):
    return 0.5 + 0.5 * jnp.tanh(0.5 * v)


def iota(shape, dim):
    return lax.broadcasted_iota(jnp.int32, shape, dim)


def shifts(marks, first, length, step, offset):
    parts = []
    for d in range(1, 4):
        hit = iota((length, SPAN), 0) == iota((length, SPAN), 1) + step * d + offset
        parts.append(jnp.where(hit, marks[first + d - 1 : first + d, :], 0.0))
    return low(jnp.concatenate(parts, axis=1))


def by_head(ref, r):
    rows = [jnp.broadcast_to(ref[pl.ds(4 * r + k, 1), :], (HDIM, ref.shape[1])) for k in range(4)]
    return jnp.concatenate(rows, axis=0)


def put_head_sums(ref, r, block):
    for k in range(4):
        ref[pl.ds(4 * r + k, 1), :] = jnp.sum(block[k * HDIM : (k + 1) * HDIM], axis=0, keepdims=True)


def chunk(r):
    return pl.ds(pl.multiple_of(r * ROWS, ROWS), ROWS)


def prepare_kernel(
    ci, halo, taps, raw, steps, marks, conv, signal, inflow, maps, cum, step, cols, local, through, state, move, enter
):
    move[...] = shifts(marks, 0, SPAN, -1, 0)
    enter[...] = shifts(marks, 0, 16, -1, 3) * (iota((16, 3 * SPAN), 0) < 3).astype(jnp.bfloat16)
    step[...] = jax.nn.softplus(raw[...] + steps[:, 0:1])
    decay = -step[...] * steps[:, 1:2]
    upto = (iota((SPAN, SPAN), 0) <= iota((SPAN, SPAN), 1)).astype(F32)
    cum[...] = nn(decay, upto, lax.Precision.HIGHEST)
    column = lax.dot_general(
        upto, decay, (((0,), (1,)), ((), ())), precision=lax.Precision.HIGHEST, preferred_element_type=F32
    )
    for g in range(GROUPS):
        cols[g] = column[:, 4 * g : 4 * g + 4]
    ends = cum[:, SPAN - 1 : SPAN]
    state[...] = marks[7:8, :] * jnp.exp(ends - cum[...])
    through[0] = jnp.broadcast_to(marks[8:9, 0:1] * jnp.exp(ends), (HEADS, LANES))

    def convolve(r):
        x = ci[chunk(r), :]
        moved = nn(x, move[...]) + tn(halo[0, :, chunk(r)], enter[...])
        total = taps[chunk(r), 4:5] + real(x) * taps[chunk(r), 3:4]
        for d in range(1, 4):
            total = total + moved[:, (d - 1) * SPAN : d * SPAN] * taps[chunk(r), 3 - d : 4 - d]
        conv[chunk(r), :] = total
        return total * sigmoid(total)

    maps[...] = convolve(8)

    def channels(r, _):
        flow = convolve(r)
        signal[chunk(r), :] = flow
        x = flow * by_head(step, r)
        inflow[chunk(r), :] = low(x)
        tail = x * by_head(state, r)
        local[0, chunk(r), :] = low(nt(low(tail), low(maps[0:LANES, :])))
        return 0

    lax.fori_loop(0, 8, channels, 0)


def mixing(maps, docs, marks):
    products = tn(maps[0:LANES, :], maps[LANES:, :], lax.Precision.HIGHEST)
    inside = (docs[...] == marks[9:10, :]) & (iota((SPAN, SPAN), 0) <= iota((SPAN, SPAN), 1))
    return jnp.where(inside, products, 0.0)


def within_kernel(inflow, maps, cum, cols, docs, marks, out, table):
    @pl.when(pl.program_id(1) == 0)
    def _():
        table[...] = mixing(maps, docs, marks)

    half = SPAN // 2
    for h in range(4):
        row, col = cum[0, h : h + 1, :], cols[0, :, h : h + 1]
        upper = low(jnp.exp(jnp.minimum(row - col[:half], 0.0)) * table[:half, :])
        lower = low(jnp.exp(jnp.minimum(row[:, half:] - col[half:], 0.0)) * table[half:, half:])
        x = inflow[h * HDIM : (h + 1) * HDIM, :]
        y = nn(x[:, :half], upper)
        out[h * HDIM : (h + 1) * HDIM, :half] = y[:, :half]
        out[h * HDIM : (h + 1) * HDIM, half:] = y[:, half:] + nn(x[:, half:], lower)


def gate_kernel(
    inside, enter, maps, signal, gate, grad, cum, marks, coef,
    gated_low, grad_gate, grad_scan, carried_sum, skip_sum, gain_sum, grad_state, grad_read, scan, entry
):
    entry[...] = marks[6:7, :] * jnp.exp(cum[...])
    reads = low(maps[LANES:, :])

    @pl.when(pl.program_id(0) == 0)
    def _():
        gain_sum[...] = jnp.zeros_like(gain_sum)

    def forward(r, sums):
        carried = nn(enter[0, chunk(r), :], reads) * by_head(entry, r)
        total = inside[chunk(r), :] + carried + coef[chunk(r), 1:2] * signal[chunk(r), :]
        scan[chunk(r), :] = total
        z = gate[chunk(r), :]
        gated = total * (z * sigmoid(z))
        up = grad[chunk(r), :] * coef[chunk(r), 0:1]
        squares, cross = sums
        return (
            squares + jnp.sum(gated * gated, axis=0, keepdims=True),
            cross + jnp.sum(gated * up, axis=0, keepdims=True),
        )

    nothing = jnp.zeros((1, SPAN), F32)
    squares, cross = lax.fori_loop(0, 8, forward, (nothing, nothing))
    factor = lax.rsqrt(squares * (1.0 / DI) + EPSILON)
    pull = factor * factor * cross * (1.0 / DI)
    grad_read[...] = jnp.zeros_like(grad_read)

    def backward(r, _):
        heads = by_head(entry, r)
        state = enter[0, chunk(r), :]
        carried = nn(state, reads) * heads
        total = scan[chunk(r), :]
        z = gate[chunk(r), :]
        sig = sigmoid(z)
        soft = z * sig
        gated = total * soft
        scaled = gated * factor
        gain = coef[chunk(r), 0:1]
        given = grad[chunk(r), :]
        gated_low[chunk(r), :] = low(scaled * gain)
        share = given * scaled
        gain_sum[chunk(r), :] += share[:, :LANES] + share[:, LANES:]
        back = factor * (given * gain - gated * pull)
        grad_gate[chunk(r), :] = low(back * total * (sig * (1.0 + z * (1.0 - sig))))
        push = back * soft
        grad_scan[chunk(r), :] = push
        put_head_sums(carried_sum, r, push * carried)
        put_head_sums(skip_sum, r, push * signal[chunk(r), :])
        entering = low(push * heads)
        grad_state[0, chunk(r), :] = low(nt(entering, reads))
        grad_read[...] += tn(state, entering)
        return 0

    lax.fori_loop(0, 8, backward, 0)


def within_back_kernel(
    inflow, push, inside, maps, cum, cols, docs, marks, grad_inflow, decay_sum, grad_maps, table, grad_table
):
    g = pl.program_id(1)

    @pl.when(g == 0)
    def _():
        table[...] = mixing(maps, docs, marks)
        grad_table[...] = jnp.zeros_like(grad_table)

    half = SPAN // 2
    for h in range(4):
        rows = slice(h * HDIM, (h + 1) * HDIM)
        row, col = cum[0, h : h + 1, :], cols[0, :, h : h + 1]
        upper = jnp.exp(jnp.minimum(row - col[:half], 0.0))
        lower = jnp.exp(jnp.minimum(row[:, half:] - col[half:], 0.0))
        x, d = inflow[rows, :], low(push[rows, :])
        grad_table[:half, :] += upper * tn(x[:, :half], d)
        grad_table[half:, half:] += lower * tn(x[:, half:], d[:, half:])
        first = nt(d, low(upper * table[:half, :]))
        second = nt(d[:, half:], low(lower * table[half:, half:]))
        back = jnp.concatenate([first, second], axis=1)
        grad_inflow[rows, :] = back
        balance = real(d) * inside[rows, :] - real(x) * back
        decay_sum[0, h : h + 1, :] = jnp.sum(balance, axis=0, keepdims=True)

    @pl.when(g == GROUPS - 1)
    def _():
        inner = (docs[...] == marks[9:10, :]) & (iota((SPAN, SPAN), 0) <= iota((SPAN, SPAN), 1))
        spread = low(jnp.where(inner, grad_table[...], 0.0))
        grad_maps[0:LANES, :] = nt(low(maps[LANES:, :]), spread)
        grad_maps[LANES:, :] = nn(low(maps[0:LANES, :]), spread)


def state_back_kernel(
    leave, enter, conv, push, grad_inflow, maps, cum, step, raw, decay_sum, carried_sum, grad_maps, grad_read,
    steps, marks, coef, grad_conv, rim, grad_raw, bias_sum, rate_sum, tail, from_tail, from_step, crossing, grad_write
):
    ends = cum[:, SPAN - 1 : SPAN]
    tail[...] = marks[7:8, :] * jnp.exp(ends - cum[...])
    writes = low(maps[0:LANES, :])
    front = ((iota((16, SPAN), 1) == iota((16, SPAN), 0)) & (iota((16, SPAN), 0) < 3)).astype(jnp.bfloat16)
    grad_write[...] = grad_maps[0:LANES, :]

    def through_silu(r, c, sig, above):
        given = above * (sig * (1.0 + c * (1.0 - sig)))
        grad_conv[chunk(r), :] = given
        rim[0, :, chunk(r)] = low(nt(front, low(given)))

    def channels(r, _):
        c = conv[chunk(r), :]
        sig = sigmoid(c)
        signal = c * sig
        heads, tails = by_head(step, r), by_head(tail, r)
        x = signal * heads
        back = leave[0, chunk(r), :]
        ended = nn(back, writes) * tails
        whole = grad_inflow[chunk(r), :] + ended
        grad_write[...] += tn(back, low(x * tails))
        put_head_sums(from_tail, r, x * ended)
        put_head_sums(from_step, r, whole * signal)
        put_head_sums(crossing, r, real(back) * real(enter[0, chunk(r), :]))
        through_silu(r, c, sig, whole * heads + coef[chunk(r), 1:2] * push[chunk(r), :])
        return 0

    lax.fori_loop(0, 8, channels, 0)
    c = conv[chunk(8), :]
    through_silu(8, c, sigmoid(c), jnp.concatenate([grad_write[...], grad_maps[LANES:, :] + grad_read[...]], axis=0))
    last = iota((HEADS, SPAN), 1) == SPAN - 1
    passing = marks[8:9, 0:1] * jnp.exp(ends) * jnp.sum(crossing[...], axis=1, keepdims=True)
    tails = jnp.sum(from_tail[...], axis=1, keepdims=True)
    total = decay_sum[...] + carried_sum[...] - from_tail[...] + jnp.where(last, tails + passing, 0.0)
    onward = (iota((SPAN, SPAN), 0) >= iota((SPAN, SPAN), 1)).astype(F32)
    grad_decay = nn(total, onward, lax.Precision.HIGHEST)
    rate = steps[:, 1:2]
    rate_sum[...] = -grad_decay * step[...] * rate
    grad_step = (from_step[...] - grad_decay * rate) * sigmoid(raw[...] + steps[:, 0:1])
    bias_sum[...] = grad_step
    grad_raw[0:HEADS, :] = low(grad_step)
    grad_raw[HEADS:, :] = jnp.zeros((LANES - HEADS, SPAN), jnp.bfloat16)


def conv_back_kernel(grad_conv, ci, rim, taps, marks, grad_ci, sums, move, enter):
    @pl.when(pl.program_id(0) == 0)
    def _():
        for m in range(MICRO):
            here = marks[:, m * SPAN : (m + 1) * SPAN]
            move[m] = shifts(here, 3, SPAN, 1, 0)
            enter[m] = shifts(here, 3, 16, 1, -SPAN) * (iota((16, 3 * SPAN), 0) < 3).astype(jnp.bfloat16)

    totals = [0.0] * 5
    for m in range(MICRO):
        part = slice(m * SPAN, (m + 1) * SPAN)
        given, x = grad_conv[:, part], real(ci[:, part])
        moved = nn(low(given), move[m]) + tn(rim[m], enter[m])
        back = given * taps[:, 3:4]
        totals[3] += given * x
        totals[4] += given
        for d in range(1, 4):
            sooner = moved[:, (d - 1) * SPAN : d * SPAN]
            back += sooner * taps[:, 3 - d : 4 - d]
            totals[3 - d] += sooner * x
        grad_ci[:, part] = low(back)
    count = jnp.zeros((ROWS, LANES), F32)
    for k in range(5):
        pick = (iota((SPAN, LANES), 1) == k).astype(jnp.bfloat16)
        count += nn(low(totals[k]), pick)
    sums[...] = count[:, 0:8]


def call(kernel, grid, ins, outs, scratch, cost, name):
    return pl.pallas_call(
        kernel,
        grid=grid,
        in_specs=[pl.BlockSpec(block, where) for _, block, where in ins],
        out_specs=[pl.BlockSpec(block, where) for _, _, block, where in outs],
        out_shape=[jax.ShapeDtypeStruct(shape, dtype) for shape, dtype, _, _ in outs],
        scratch_shapes=scratch,
        compiler_params=pltpu.CompilerParams(
            vmem_limit_bytes=56 * 2**20, dimension_semantics=("arbitrary",) * len(grid)
        ),
        cost_estimate=pl.CostEstimate(flops=cost, bytes_accessed=20_000_000, transcendentals=0),
        name=name,
    )(*[array for array, _, _ in ins])


def neighbours(value, source, target):
    return lax.ppermute(value, GROUP, [(source, target)])


def chained(local, through, order, beside):
    keep = real(jnp.repeat(through[:, :, 0], HDIM, axis=1))[:, :, None]
    one = neighbours(local, order[0], order[1])
    two = neighbours(low(keep * real(one) + real(local)), order[1], order[2])
    two, beside = lax.optimization_barrier((two, beside))
    three = neighbours(low(keep * real(two) + real(local)), order[2], order[3])
    return one + two + three, beside


def shards(
    tokens, segments, cotangent, norm_gain, in_weight, conv_kernel, conv_bias, step_bias, decay_log,
    skip_gain, gate_gain, out_weight, master, moment_one, moment_two, step_count
):
    width = MICRO * SPAN
    bf16 = jnp.bfloat16
    spot = position()
    place = lax.axis_index(GROUP)
    ids = segments[:, 0, :]
    window = jnp.pad(ids, ((0, 0), (3, 3)), constant_values=-1)
    window = lax.dynamic_slice(window, (0, place * SPAN), (MICRO, SPAN + 6))
    here = window[:, 3 : 3 + SPAN]
    before = [window[:, 3 - d : 3 - d + SPAN] == here for d in (1, 2, 3)]
    after = [window[:, 3 + d : 3 + d + SPAN] == here for d in (1, 2, 3)]
    prior, final = window[:, 2:3], here[:, SPAN - 1 :]
    rows = before + after + [here == prior, here == final, jnp.broadcast_to(final == prior, here.shape)]
    marks = jnp.stack([row.astype(F32) for row in rows] + [here.astype(F32)] + [jnp.zeros(here.shape, F32)] * 6)
    marks = marks.reshape(16, width)
    docs = here.astype(F32).reshape(width, 1)

    norm_real = real(norm_gain)
    rows_in = real(tokens.reshape(width, D))
    normed, norm_back = jax.vjp(norm_piece, rows_in, norm_real)
    normed_low = low(normed)
    rim_tokens = lax.ppermute(tokens[:, 0, SPAN - 3 :, :], GROUP, [(0, 1), (1, 2), (2, 3)])
    rim_low = low(norm_piece(real(rim_tokens).reshape(-1, D), norm_real))
    rim_low = jnp.pad(rim_low.reshape(MICRO, 3, D), ((0, 0), (0, 13), (0, 0)))
    turned_weight = in_weight.T
    conv_weight = turned_weight[DI : DI + CH]
    halo = low(nt(rim_low.reshape(-1, D), conv_weight)).reshape(MICRO, 16, CH)
    ci = low(nt(conv_weight, normed_low))
    raw = nt(turned_weight[DI + CH :], normed_low)
    gate = nt(turned_weight[:DI], normed_low)
    upstream = cotangent.reshape(width, D)
    grad_mixed = nt(out_weight, upstream)

    taps = jnp.concatenate([real(conv_kernel), real(conv_bias)[None], jnp.zeros((3, CH), F32)]).T
    steps = jnp.stack([real(step_bias), jnp.exp(real(decay_log))] + [jnp.zeros((HEADS,), F32)] * 6, axis=1)
    coef = jnp.stack([real(gate_gain), jnp.repeat(real(skip_gain), HDIM)] + [jnp.zeros((DI,), F32)] * 6, axis=1)

    one, two = (MICRO,), (MICRO, GROUPS)
    by_m, by_gm = lambda m: (0, m), lambda m, g: (g, m)
    whole, first = lambda m: (0, 0), lambda m: (m, 0, 0)
    mark_in, mark_in2 = (marks, (16, SPAN), by_m), (marks, (16, SPAN), lambda m, g: (0, m))

    conv, signal, inflow, maps, cum, step, cols, local, through = call(
        prepare_kernel, one,
        [(ci, (CH, SPAN), by_m), (halo, (1, 16, CH), first), (taps, (CH, 8), whole), (raw, (HEADS, SPAN), by_m),
         (steps, (HEADS, 8), whole), mark_in],
        [((CH, width), F32, (CH, SPAN), by_m), ((DI, width), F32, (DI, SPAN), by_m),
         ((DI, width), bf16, (DI, SPAN), by_m), ((2 * STATE, width), F32, (2 * STATE, SPAN), by_m), ((HEADS, width), F32, (HEADS, SPAN), by_m),
         ((HEADS, width), F32, (HEADS, SPAN), by_m), ((GROUPS, width, 4), F32, (GROUPS, SPAN, 4), lambda m: (0, m, 0)),
         ((MICRO, DI, STATE), bf16, (1, DI, STATE), first), ((MICRO, HEADS, LANES), F32, (1, HEADS, LANES), first)],
        [pltpu.VMEM((HEADS, SPAN), F32), pltpu.VMEM((SPAN, 3 * SPAN), bf16), pltpu.VMEM((16, 3 * SPAN), bf16)],
        10**9, "convolve_and_prepare",
    )
    cum_groups = cum.reshape(GROUPS, 4, width)
    head_ins = [
        (maps, (2 * STATE, SPAN), lambda m, g: (0, m)),
        (cum_groups, (1, 4, SPAN), lambda m, g: (g, 0, m)),
        (cols, (1, SPAN, 4), lambda m, g: (g, m, 0)),
        (docs, (SPAN, 1), lambda m, g: (m, 0)),
        mark_in2,
    ]
    quad = (4 * HDIM, SPAN)
    table = pltpu.VMEM((SPAN, SPAN), F32)
    (inside,) = call(
        within_kernel, two, [(inflow, quad, by_gm)] + head_ins, [((DI, width), F32, quad, by_gm)], [table],
        4 * 10**9, "within_blocks",
    )

    enter, (inside, gate, grad_mixed) = chained(local, through, (0, 1, 2, 3), (inside, gate, grad_mixed))

    tall = (DI, SPAN)
    state_block = (1, DI, STATE)
    gated_low, grad_gate, push, carried_sum, skip_sum, gain_sum, grad_state, grad_read = call(
        gate_kernel, one,
        [(inside, tall, by_m), (enter, state_block, first), (maps, (2 * STATE, SPAN), by_m), (signal, tall, by_m),
         (gate, tall, by_m), (grad_mixed, tall, by_m), (cum, (HEADS, SPAN), by_m), mark_in, (coef, (DI, 8), whole)],
        [((DI, width), bf16, tall, by_m), ((DI, width), bf16, tall, by_m), ((DI, width), F32, tall, by_m),
         ((HEADS, width), F32, (HEADS, SPAN), by_m), ((HEADS, width), F32, (HEADS, SPAN), by_m),
         ((DI, LANES), F32, (DI, LANES), whole), ((MICRO, DI, STATE), bf16, state_block, first),
         ((STATE, width), F32, (STATE, SPAN), by_m)],
        [pltpu.VMEM((DI, SPAN), F32), pltpu.VMEM((HEADS, SPAN), F32)], 2 * 10**9, "gate_and_back",
    )
    grad_inflow, decay_sum, grad_maps = call(
        within_back_kernel, two,
        [(inflow, quad, by_gm), (push, quad, by_gm), (inside, quad, by_gm)] + head_ins,
        [((DI, width), F32, quad, by_gm), ((GROUPS, 4, width), F32, (1, 4, SPAN), lambda m, g: (g, 0, m)),
         ((2 * STATE, width), F32, (2 * STATE, SPAN), lambda m, g: (0, m))],
        [table, table], 8 * 10**9, "within_blocks_back",
    )

    leave, (grad_inflow, decay_sum, grad_maps) = chained(
        grad_state, through, (3, 2, 1, 0), (grad_inflow, decay_sum, grad_maps)
    )

    few = (HEADS, SPAN)
    grad_conv, rim, grad_raw, bias_sum, rate_sum = call(
        state_back_kernel, one,
        [(leave, state_block, first), (enter, state_block, first), (conv, (CH, SPAN), by_m), (push, tall, by_m),
         (grad_inflow, tall, by_m), (maps, (2 * STATE, SPAN), by_m), (cum, few, by_m), (step, few, by_m), (raw, few, by_m),
         (decay_sum.reshape(HEADS, width), few, by_m), (carried_sum, few, by_m), (grad_maps, (2 * STATE, SPAN), by_m),
         (grad_read, (STATE, SPAN), by_m), (steps, (HEADS, 8), whole), mark_in, (coef, (DI, 8), whole)],
        [((CH, width), F32, (CH, SPAN), by_m), ((MICRO, 16, CH), bf16, (1, 16, CH), first),
         ((LANES, width), bf16, (LANES, SPAN), by_m), ((HEADS, width), F32, few, by_m), ((HEADS, width), F32, few, by_m)],
        [pltpu.VMEM(few, F32), pltpu.VMEM(few, F32), pltpu.VMEM(few, F32), pltpu.VMEM((HEADS, LANES), F32),
         pltpu.VMEM((STATE, SPAN), F32)], 10**9, "state_and_silu_back",
    )
    next_rim = lax.ppermute(rim, GROUP, [(1, 0), (2, 1), (3, 2)])

    by_r = lambda r: (r, 0)
    grad_ci, tap_sums = call(
        conv_back_kernel, (CH // ROWS,),
        [(grad_conv, (ROWS, width), by_r), (ci, (ROWS, width), by_r), (next_rim, (MICRO, 16, ROWS), lambda r: (0, 0, r)),
         (taps, (ROWS, 8), by_r), (marks, (16, width), lambda r: (0, 0))],
        [((CH, width), bf16, (ROWS, width), by_r), ((CH, 8), F32, (ROWS, 8), by_r)],
        [pltpu.VMEM((MICRO, SPAN, 3 * SPAN), bf16), pltpu.VMEM((MICRO, 16, 3 * SPAN), bf16)], 10**8, "convolution_back",
    )

    grad_normed = (
        tn(grad_gate, turned_weight[:DI]) + tn(grad_ci, conv_weight) + tn(grad_raw[:HEADS], turned_weight[DI + CH :])
    )
    grad_rows, grad_norm_gain = norm_back(grad_normed)
    input_grad = low(real(upstream) + grad_rows).reshape(tokens.shape)
    output = low(rows_in + tn(gated_low, out_weight)).reshape(tokens.shape)

    left = normed_low.T.reshape(D // 4, 4, width).transpose(1, 0, 2).reshape(D, width)
    turned = jnp.concatenate([upstream[:, 32:], upstream[:, :32]], axis=1)
    middle = [tap_sums[:, :5].T.reshape(-1), jnp.sum(bias_sum, axis=1), jnp.sum(rate_sum, axis=1)]
    middle += [jnp.sum(skip_sum, axis=1), jnp.sum(gain_sum, axis=1), jnp.zeros((32 + 5 * LANES,), F32)]
    middle = jnp.concatenate(middle).reshape(-1, LANES)
    packed = pack(spot, left, grad_gate, grad_ci, grad_raw, gated_low, turned, grad_norm_gain.reshape(-1, LANES), middle)
    piece = reduce_pieces(packed[:3], packed[3:])
    window = lax.all_gather(piece, GROUP, axis=0, tiled=True)
    skew = (12 * lax.axis_index("x")) % 16
    shard = lax.dynamic_slice(window, (skew, 0), (SHARD_LINES, LANES)).reshape(-1)
    squares = over_copies(jnp.sum(shard * shard), DP)
    clip_factor = MAX_NORM / jnp.maximum(jnp.sqrt(squares), MAX_NORM)
    first_moment, second_moment, updated = adam_update(
        shard * clip_factor, master, moment_one, moment_two, step_count
    )
    blank = jnp.zeros_like(window)
    placed = low(lax.dynamic_update_slice(blank, updated.reshape(SHARD_LINES, LANES), (skew, 0)))
    mine = lax.dynamic_slice(placed, (PIECE * place, 0), (PIECE, LANES))
    copies = unpack(spot, gather_pieces(mine)).reshape(-1)
    return (output, input_grad, shard, first_moment, second_moment, updated, copies)


def solution(mesh):
    finer = Mesh(mesh.devices.reshape(4, 2, 4, 2, 2), ("y", "zl", "x", "zh", "core"))
    return jax.shard_map(
        shards,
        mesh=finer,
        in_specs=(
            P(None, DP, GROUP, None),
            P(None, DP, None),
            P(None, DP, GROUP, None),
            P(),
            P(),
            P(),
            P(),
            P(),
            P(),
            P(),
            P(),
            P(),
            P(DP),
            P(DP),
            P(DP),
            P(),
        ),
        out_specs=(
            P(None, DP, GROUP, None),
            P(None, DP, GROUP, None),
            P(DP),
            P(DP),
            P(DP),
            P(DP),
            P(),
        ),
        check_vma=False,
    )
```

```python
import functools

import jax
import jax.numpy as jnp
from jax import lax
from jax.experimental import pallas as pl
from jax.experimental.pallas import tpu as pltpu
from jax.sharding import Mesh
from jax.sharding import PartitionSpec as P

D = 1024
DI = 2048
HEADS = 32
HDIM = 64
STATE = 128
CH = 2304
DP = ("y", "zl", "x")
GROUP = ("zh", "core")
EVERY = DP + GROUP


EPSILON = 1e-05
BETA_ONE = 0.9
BETA_TWO = 0.95
ADAM_EPSILON = 1e-08
LEARN_RATE = 0.01
WEIGHT_DECAY = 0.1
MAX_NORM = 1.0


def sent_to_all(shard, axis):
    copies = jnp.broadcast_to(shard, (lax.axis_size(axis), *shard.shape))
    return lax.all_to_all(copies, axis, split_axis=0, concat_axis=0, tiled=True)


def norm_piece(values, scaling):
    factor = lax.rsqrt(jnp.mean(values * values, axis=-1, keepdims=True) + EPSILON)
    return values * factor * scaling


def adam_step(clipped, master, moment_one, moment_two, first_scale, second_scale):
    first_moment = BETA_ONE * moment_one + (1.0 - BETA_ONE) * clipped
    second_moment = BETA_TWO * moment_two + (1.0 - BETA_TWO) * clipped * clipped
    first_hat, second_hat = first_moment * first_scale, second_moment * second_scale
    updated = master - LEARN_RATE * (first_hat / (jnp.sqrt(second_hat) + ADAM_EPSILON) + WEIGHT_DECAY * master)
    return (first_moment, second_moment, updated)


LANES = 128
LINES = 51584
SHARD_LINES = 1612
IN_LINE = 8
MID_LINE = 35080
OUT_LINE = 35187
PIECE = 416
SLOTS = 16
PARTS = ((0, 144), (144, 144), (288, 128))
TAIL_LINES = 51632
GROUP_LINES = 137
RING = {"x": ("x",), "y": ("y",), "z": ("zl", "zh")}
ROUTES = (("x", "y", "z"), ("y", "x", "z"), ("Z", "y", "x"))


def ring_place(axis, i):
    i = i % 4
    return (i % 2) * 2 + i // 2 if axis == "z" else i


def from_offset(block, axis, distance):
    route = [(ring_place(axis, i + distance), ring_place(axis, i)) for i in range(4)]
    return lax.ppermute(block, RING[axis], route)


def swap_cores(block):
    return lax.ppermute(block, "core", [(0, 1), (1, 0)])


def position():
    z = 2 * lax.axis_index("zh") + lax.axis_index("zl")
    return jnp.stack([lax.axis_index("y"), z, lax.axis_index("x"), lax.axis_index("core")]).astype(jnp.int32)


def first_tile(shard):
    return (403 * shard) >> 2


def pack_kernel(pos, mid_part, *rest):
    sources, keep, send = rest[:6], rest[6:9], rest[9:12]
    flat, carry, edge, stage, sems = rest[12:17]
    left, grad_gate, grad_ci, grad_raw, gated, cot = held = rest[17:23]
    loads = [pltpu.make_async_copy(source, here, rest[23].at[k]) for k, (source, here) in enumerate(zip(sources, held))]
    for k in (4, 5, 0, 1, 2, 3):
        loads[k].start()
    lane = lax.broadcasted_iota(jnp.int32, (256, LANES), 1)

    flat[0:IN_LINE, :] = jnp.zeros((IN_LINE, LANES), jnp.float32)
    flat[MID_LINE : MID_LINE + 104, :] = mid_part[0:104, :]
    flat[MID_LINE + 104 : MID_LINE + 107, :] = mid_part[104:107, :]
    edge[0:8, :] = mid_part[99:107, :]

    def rows(b, _):
        block = gated[pl.ds(pl.multiple_of(b * 256, 256), 256), :]
        product = jnp.dot(block, cot[...], preferred_element_type=jnp.float32)
        start = OUT_LINE + 2048 * b
        for t in range(7):
            flat[pl.ds(start + t, 256, stride=8), :] = product[:, t * LANES : (t + 1) * LANES]
        last = product[:, 7 * LANES :]
        edge[8:264, :] = last
        flat[pl.ds(start - 1, 256, stride=8), :] = jnp.where(lane < 96, edge[7:263, :], last)
        edge[0:8, :] = edge[256:264, :]
        return 0

    loads[4].wait()
    loads[5].wait()
    lax.fori_loop(0, 8, rows, 0)
    low = lax.broadcasted_iota(jnp.int32, (1, LANES), 1) < 96
    flat[OUT_LINE + 16383 : TAIL_LINES, :] = jnp.zeros((TAIL_LINES - OUT_LINE - 16383, LANES), jnp.float32)
    flat[OUT_LINE + 16383 : OUT_LINE + 16384, :] = jnp.where(low, edge[7:8, :], 0.0)

    my_y, my_z, my_x, my_core = pos[0], pos[1], pos[2], pos[3]

    def drain(slot):
        pltpu.make_async_copy(stage.at[slot], keep[0].at[pl.ds(0, PIECE)], sems.at[slot]).wait()

    def ship(n, _):
        i = (n + 88) & 127
        slot = n & (SLOTS - 1)

        @pl.when(n >= SLOTS)
        def _():
            drain(slot)

        shard, quarter = i >> 2, i & 3
        line = 16 * first_tile(shard) + PIECE * quarter
        stage[slot] = flat[pl.ds(pl.multiple_of(line, 16), PIECE), :].astype(jnp.bfloat16)
        x, zl, y = shard & 3, (shard >> 2) & 1, shard >> 3
        core = quarter & 1
        z = 2 * (quarter >> 1) + zl
        off = {"y": (y - my_y) & 3, "z": (z - my_z) & 3, "x": (x - my_x) & 3, "Z": 2 * zl + (quarter >> 1)}
        for p, (start, size) in enumerate(PARTS):
            a, b, c = (off[axis] for axis in ROUTES[p])
            to = pl.ds(pl.multiple_of(((a * 4 + b) * 4 + c) * size, 16), size)
            source = stage.at[slot, pl.ds(start, size)]

            @pl.when(core == my_core)
            def _():
                pltpu.make_async_copy(source, keep[p].at[to], sems.at[slot]).start()

            @pl.when(core != my_core)
            def _():
                pltpu.make_async_copy(source, send[p].at[to], sems.at[slot]).start()

        return 0

    lax.fori_loop(0, 40, ship, 0)

    def put(tile, k, line):
        moved = pltpu.roll(tile, 32 * k, 1) if k else tile
        whole = jnp.where(lane < 32 * k, carry[k], moved) if k else moved
        flat[pl.ds(IN_LINE + 34 * k + line, 256, stride=GROUP_LINES), :] = whole
        carry[k] = moved

    def columns(block, line, tiles):
        product = nt(left[...], block)
        for k in range(4):
            for t in range(tiles):
                put(product[256 * k : 256 * (k + 1), t * LANES : (t + 1) * LANES], k, line + t)

    def from_gate(j, _):
        columns(grad_gate[pl.ds(pl.multiple_of(j * 512, 512), 512), :], 4 * j, 4)
        return 0

    def from_conv(j, _):
        columns(grad_ci[pl.ds(pl.multiple_of(j * 512, 512), 512), :], 16 + 4 * j, 4)
        return 0

    loads[0].wait()
    loads[1].wait()
    lax.fori_loop(0, 4, from_gate, 0)
    loads[2].wait()
    loads[3].wait()
    lax.fori_loop(0, 4, from_conv, 0)
    heads = []
    for k in range(1, 4):
        heads.append(flat[pl.ds(IN_LINE + 34 * k, 256, stride=GROUP_LINES), :])
    columns(jnp.concatenate([grad_ci[2048:2304, :], grad_raw[...]], axis=0), 32, 3)
    for k in range(1, 4):
        at = pl.ds(IN_LINE + 34 * k, 256, stride=GROUP_LINES)
        flat[at, :] = jnp.where(lane < 32 * k, flat[at, :], heads[k - 1])

    lax.fori_loop(40, 128, ship, 0)
    for slot in range(SLOTS):
        drain(slot)


def pack(pos, left, grad_gate, grad_ci, grad_raw, gated, cot, mid_part):
    vmem, hbm = pl.BlockSpec(memory_space=pltpu.VMEM), pl.BlockSpec(memory_space=pl.ANY)
    shapes = [jax.ShapeDtypeStruct((64 * size, LANES), jnp.bfloat16) for _, size in PARTS]
    return pl.pallas_call(
        pack_kernel,
        out_shape=shapes + shapes,
        in_specs=[pl.BlockSpec(memory_space=pltpu.SMEM)] + [vmem] + [hbm] * 6,
        out_specs=[hbm] * 6,
        scratch_shapes=[
            pltpu.VMEM((TAIL_LINES, LANES), jnp.float32),
            pltpu.VMEM((4, 256, LANES), jnp.float32),
            pltpu.VMEM((264, LANES), jnp.float32),
            pltpu.VMEM((SLOTS, PIECE, LANES), jnp.bfloat16),
            pltpu.SemaphoreType.DMA((SLOTS,)),
        ]
        + [pltpu.VMEM(v.shape, v.dtype) for v in (left, grad_gate, grad_ci, grad_raw, gated, cot)]
        + [pltpu.SemaphoreType.DMA((6,))],
        compiler_params=pltpu.CompilerParams(vmem_limit_bytes=60 * 2**20),
        cost_estimate=pl.CostEstimate(flops=7_000_000_000, bytes_accessed=25_000_000, transcendentals=0),
        name="pack_gradients",
    )(pos, mid_part, left, grad_gate, grad_ci, grad_raw, gated, cot)


def real(v):
    return v.astype(jnp.float32)


def low(v):
    return v.astype(jnp.bfloat16)


def to_offset(block, axis, distance):
    route = [(ring_place(axis, i), ring_place(axis, i + distance)) for i in range(4)]
    return lax.ppermute(block, RING[axis], route)


def exchange(blocks, axis):
    blocks = blocks.reshape(4, -1, LANES)
    return lax.all_to_all(blocks, RING[axis], split_axis=0, concat_axis=0, tiled=True)


def quarters(block):
    return block.reshape(4, -1, LANES)


def ring_sum(block, axis):
    block = quarters(block)
    half = block.shape[1] // 32 * 16
    a, b = to_offset(block[2, :half], axis, 1), to_offset(block[2, half:], axis, 3)
    one = jnp.concatenate([low(real(block[1, :half]) + real(a)), block[1, half:]])
    three = jnp.concatenate([block[3, :half], low(real(block[3, half:]) + real(b))])
    return real(block[0]) + real(to_offset(one, axis, 1)) + real(to_offset(three, axis, 3))


def direct_sum(block, axis):
    block = quarters(block)
    moved = [to_offset(block[d], axis, d) for d in (1, 3, 2)]
    return real(block[0]) + real(moved[0]) + real(moved[1]) + real(moved[2])


def exchange_sum(block, axis):
    return jnp.sum(real(exchange(block, axis)), axis=0)


def reduce_pieces(keep, send, gain_grad, beside, given):
    held = [None] * 3
    for p in (2, 0, 1):
        held[p] = low(real(keep[p]) + real(swap_cores(send[p])))
    gain_grad = low(gain_grad + swap_cores(gain_grad))
    x, y, z = lax.axis_index("x"), lax.axis_index("y"), 2 * lax.axis_index("zh") + lax.axis_index("zl")
    block = 16 * (-x & 3) + 4 * (-y & 3) + (-z & 3)
    lines = jnp.arange(16)[:, None]
    mine = (lines < IN_LINE) & (lax.axis_index("core") == 0)
    start = (block * PARTS[0][1], 0)
    tile = lax.dynamic_slice(held[0], start, (16, LANES))
    tile = jnp.where(mine, jnp.pad(gain_grad, ((0, 16 - IN_LINE), (0, 0))), tile)
    held[0] = lax.dynamic_update_slice(held[0], tile, start)
    third = exchange(held[2], "z")
    ends, given = lax.optimization_barrier((held[:2], given))
    first, second = low(ring_sum(ends[0], "x")), low(ring_sum(ends[1], "y"))
    third = low(jnp.sum(real(third), axis=0))
    (first, second, third), done = lax.optimization_barrier(((first, second, third), beside(given)))
    n0, n1, n2 = (size for _, size in PARTS)
    outer = jnp.concatenate([quarters(first), quarters(third)], axis=1).reshape(-1, LANES)
    outer, second = low(direct_sum(outer, "y")), low(direct_sum(second, "x"))
    first, third = outer[: 4 * n0], outer[4 * n0 :]
    both = jnp.concatenate([quarters(first), quarters(second)], axis=1).reshape(-1, LANES)
    both, third = direct_sum(both, "z"), direct_sum(third, "x")
    return jnp.concatenate([both, third]), done


def gather_pieces(piece):
    def spread(block, axis):
        return [block] + [from_offset(block, axis, d) for d in (1, 3, 2)]

    def in_order(parts):
        return jnp.concatenate([parts[0], parts[1], parts[3], parts[2]])

    n0, n1, n2 = (size for _, size in PARTS)
    both, third = spread(piece[: n0 + n1], "z"), in_order(spread(piece[n0 + n1 :], "x"))
    first = in_order([block[:n0] for block in both])
    second = in_order([block[n0:] for block in both])
    outer = spread(jnp.concatenate([first, third]), "y")
    second = in_order(spread(second, "x"))
    first = in_order([block[: 4 * n0] for block in outer])
    third = in_order([block[4 * n0 :] for block in outer])
    third = exchange(jnp.broadcast_to(third, (4, *third.shape)), "z").reshape(-1, LANES)
    ends = (first, "x"), (second, "y")
    mine = [[block] for block, _ in ends]
    for d in (1, 3, 2):
        for blocks, (block, axis) in zip(mine, ends):
            blocks.append(from_offset(block, axis, d))
    mine = mine[0] + mine[1] + [third]
    return mine + [swap_cores(block) for block in mine]


def unpack_kernel(pos, *rest):
    sources, out = rest[:18], rest[18]
    whole, edges, sem = rest[19:]
    my_y, my_z, my_x, my_core = pos[0], pos[1], pos[2], pos[3]
    row = lax.broadcasted_iota(jnp.int32, (16, LANES), 0)

    def put(source, here, line, size):
        whole[pl.ds(pl.multiple_of(line, 16), size), :] = source[pl.ds(pl.multiple_of(here, 16), size), :]

    def at(far_y, z, x, core):
        shard = (((my_y + far_y) & 3) << 3) + ((z & 1) << 2) + x
        line = first_tile(shard) << 4
        return shard & 7, line, line + PIECE * (2 * (z >> 1) + core)

    rows_of_y = 8 * SHARD_LINES
    for far_y in range(4):
        for other in range(2):
            core = (my_core + other) & 1
            for array, far_x in enumerate((0, 1, 3, 2)):
                source = sources[9 * other + array]

                def first(i, _, source=source, far_x=far_x, far_y=far_y, core=core):
                    z, x = (my_z + i) & 3, (my_x + far_x) & 3
                    shard, start, line = at(far_y, z, x, core)
                    here = (4 * far_y + i) * 144
                    put(source, here + 16, line + 16, 128)

                    @pl.when(line == start)
                    def _():
                        edges[0, shard] = source[pl.ds(pl.multiple_of(here, 16), 16), :]

                    @pl.when(line != start)
                    def _():
                        put(source, here, line, 16)

                    return 0

                lax.fori_loop(0, 4, first, 0, unroll=True)
            source = sources[9 * other + 4 + (0, 1, 3, 2).index(far_y)]

            def second(i, _, source=source, far_y=far_y, core=core):
                x, z = (my_x + (i >> 2)) & 3, (my_z + (i & 3)) & 3
                _, _, line = at(far_y, z, x, core)
                put(source, i * 144, line + 144, 144)
                return 0

            lax.fori_loop(0, 16, second, 0, unroll=4)
            source = sources[9 * other + 8]

            def third(i, _, source=source, far_y=far_y, core=core):
                z, x = 2 * ((i >> 2) & 1) + (i >> 3), (my_x + (i & 3)) & 3
                shard, start, line = at(far_y, z, x, core)
                here = (16 * (i >> 2) + 4 * far_y + (i & 3)) * 128
                put(source, here, line + 288, 80)

                @pl.when(line == start + 3 * PIECE)
                def _():
                    skip = jnp.where((x == 1) | (x == 2), 80, 64)
                    edges[1, shard] = source[pl.ds(pl.multiple_of(here + skip, 16), 16), :]

                @pl.when(line != start + 3 * PIECE)
                def _():
                    put(source, here + 80, line + 368, 48)

                return 0

            lax.fori_loop(0, 16, third, 0, unroll=4)
        base = pl.multiple_of(rows_of_y * ((my_y + far_y) & 3), 16)
        for shard in range(8):
            x = shard % 4
            tile = real(edges[0, shard])
            if x:
                tile = jnp.where(row < (12 * x) % 16, real(edges[1, shard - 1]), tile)
            whole[pl.ds(pl.multiple_of(base + 16 * ((403 * shard) // 4), 16), 16), :] = low(tile)
        pltpu.make_async_copy(whole.at[pl.ds(base, rows_of_y)], out.at[pl.ds(base, rows_of_y)], sem.at[far_y]).start()
    for far_y in range(4):
        pltpu.make_async_copy(whole.at[pl.ds(0, rows_of_y)], out.at[pl.ds(0, rows_of_y)], sem.at[far_y]).wait()


def unpack(pos, pieces):
    hbm, vmem = pl.BlockSpec(memory_space=pl.ANY), pl.BlockSpec(memory_space=pltpu.VMEM)
    return pl.pallas_call(
        unpack_kernel,
        out_shape=jax.ShapeDtypeStruct((LINES, LANES), jnp.bfloat16),
        in_specs=[pl.BlockSpec(memory_space=pltpu.SMEM)] + [vmem] * 18,
        out_specs=hbm,
        scratch_shapes=[
            pltpu.VMEM((LINES, LANES), jnp.bfloat16),
            pltpu.VMEM((2, 8, 16, LANES), jnp.bfloat16),
            pltpu.SemaphoreType.DMA((4,)),
        ],
        compiler_params=pltpu.CompilerParams(vmem_limit_bytes=48 * 2**20),
        cost_estimate=pl.CostEstimate(flops=0, bytes_accessed=27_000_000, transcendentals=0),
        name="unpack_weights",
    )(pos, *pieces)


def own_update_kernel(where, scales, squares, piece, master, moment_one, moment_two, out):
    start, turn = where[0], where[1]
    total = jnp.sum(squares[...], axis=1, keepdims=True)
    clipped = piece[...] * (MAX_NORM / jnp.maximum(jnp.sqrt(total), MAX_NORM))

    def lines(ref):
        return pltpu.roll(ref[pl.ds(start, PIECE), :], turn, 0)

    out[...] = low(adam_step(clipped, lines(master), lines(moment_one), lines(moment_two), scales[0], scales[1])[2])


def own_update(offset, scales, squares, piece, master, moment_one, moment_two):
    start = jnp.clip(offset, 0, SHARD_LINES - PIECE)
    where = jnp.stack([start, (start - offset + PIECE) % PIECE]).astype(jnp.int32)
    smem, vmem = pl.BlockSpec(memory_space=pltpu.SMEM), pl.BlockSpec(memory_space=pltpu.VMEM)
    return pl.pallas_call(
        own_update_kernel,
        out_shape=jax.ShapeDtypeStruct((PIECE, LANES), jnp.bfloat16),
        in_specs=[smem, smem] + [vmem] * 5,
        out_specs=vmem,
        compiler_params=pltpu.CompilerParams(vmem_limit_bytes=16 * 2**20),
        name="own_update",
    )(where, scales, squares, piece, *[v.reshape(SHARD_LINES, LANES) for v in (master, moment_one, moment_two)])


SPAN = 256
MICRO = 2
GROUPS = 8
ROWS = 256
F32 = jnp.float32


def nt(left, right, precision=None):
    return lax.dot_general(left, right, (((1,), (1,)), ((), ())), precision=precision, preferred_element_type=F32)


def tn(left, right, precision=None):
    return lax.dot_general(left, right, (((0,), (0,)), ((), ())), precision=precision, preferred_element_type=F32)


def nn(left, right, precision=None):
    return lax.dot_general(left, right, (((1,), (0,)), ((), ())), precision=precision, preferred_element_type=F32)


def sigmoid(v):
    return 0.5 + 0.5 * jnp.tanh(0.5 * v)


def iota(shape, dim):
    return lax.broadcasted_iota(jnp.int32, shape, dim)


def shifts(marks, first, length, step, offset):
    parts = []
    for d in range(1, 4):
        hit = iota((length, SPAN), 0) == iota((length, SPAN), 1) + step * d + offset
        parts.append(jnp.where(hit, marks[first + d - 1 : first + d, :], 0.0))
    return low(jnp.concatenate(parts, axis=1))


def by_head(ref, r):
    rows = [jnp.broadcast_to(ref[pl.ds(4 * r + k, 1), :], (HDIM, ref.shape[1])) for k in range(4)]
    return jnp.concatenate(rows, axis=0)


def put_head_sums(ref, r, block):
    for k in range(4):
        ref[pl.ds(4 * r + k, 1), :] = jnp.sum(block[k * HDIM : (k + 1) * HDIM], axis=0, keepdims=True)


def chunk(r):
    return pl.ds(pl.multiple_of(r * ROWS, ROWS), ROWS)


def prepare_kernel(
    weight, step_weight, normed, rim, taps, steps, marks,
    ci, conv, signal, inflow, maps, raw, cum, step, cols, local, through, state, move, enter
):
    r = pl.program_id(0)
    parts = [slice(m * SPAN, (m + 1) * SPAN) for m in range(MICRO)]

    @pl.when(r == 0)
    def _():
        raw[...] = nt(step_weight[...], normed[...])
        step[...] = jax.nn.softplus(raw[...] + steps[:, 0:1])
        upto = (iota((SPAN, SPAN), 0) <= iota((SPAN, SPAN), 1)).astype(F32)
        for m, part in enumerate(parts):
            here = marks[:, part]
            move[m] = shifts(here, 0, SPAN, -1, 0)
            enter[m] = shifts(here, 0, 16, -1, 3) * (iota((16, 3 * SPAN), 0) < 3).astype(jnp.bfloat16)
            decay = -step[:, part] * steps[:, 1:2]
            total = nn(decay, upto, lax.Precision.HIGHEST)
            cum[:, part] = total
            column = lax.dot_general(
                upto, decay, (((0,), (1,)), ((), ())), precision=lax.Precision.HIGHEST, preferred_element_type=F32
            )
            for g in range(GROUPS):
                cols[g, part, :] = column[:, 4 * g : 4 * g + 4]
            ends = total[:, SPAN - 1 :]
            state[:, part] = here[7:8, :] * jnp.exp(ends - total)
            through[m] = jnp.broadcast_to(here[8:9, 0:1] * jnp.exp(ends), (HEADS, LANES))

    x = low(nt(weight[...], normed[...]))
    ci[...] = x
    halo = low(nt(weight[...], rim[...]))
    flows = []
    for m, part in enumerate(parts):
        moved = nn(x[:, part], move[m]) + nn(halo[:, 16 * m : 16 * m + 16], enter[m])
        total = taps[:, 4:5] + real(x[:, part]) * taps[:, 3:4]
        for d in range(1, 4):
            total = total + moved[:, (d - 1) * SPAN : d * SPAN] * taps[:, 3 - d : 4 - d]
        conv[:, part] = total
        flows.append(total * sigmoid(total))

    @pl.when(r == 0)
    def _():
        for flow, part in zip(flows, parts):
            maps[:, part] = flow

    @pl.when(r > 0)
    def _():
        for m, (flow, part) in enumerate(zip(flows, parts)):
            signal[:, part] = flow
            heads = by_head(step, r - 1)[:, part]
            tails = by_head(state, r - 1)[:, part]
            flow = flow * heads
            inflow[:, part] = low(flow)
            local[m] = low(nt(low(flow * tails), low(maps[0:LANES, part])))


def turn_kernel(normed, upstream, left, cot, turned):
    for t in range(4):
        part = slice(t * LANES, (t + 1) * LANES)
        turned[...] = jnp.transpose(real(normed[part, :]))
        for k in range(4):
            left[256 * k : 256 * (k + 1), part] = low(turned[pl.ds(k, 256, stride=4), :])
    cot[...] = low(pltpu.roll(real(upstream[...]), D - 32, 1))


def mixing(maps, docs, marks):
    products = tn(maps[0:LANES, :], maps[LANES:, :], lax.Precision.HIGHEST)
    inside = (docs[...] == marks[9:10, :]) & (iota((SPAN, SPAN), 0) <= iota((SPAN, SPAN), 1))
    return jnp.where(inside, products, 0.0)


def within_kernel(inflow, maps, cum, cols, docs, marks, out, table):
    table[...] = mixing(maps, docs, marks)
    half = SPAN // 2

    def heads(g, _):
        results = []
        x4 = inflow[chunk(g), :]
        for h in range(4):
            row, col = cum[pl.ds(4 * g + h, 1), :], cols[g, :, h : h + 1]
            upper = low(jnp.exp(jnp.minimum(row - col[:half], 0.0)) * table[:half, :])
            lower = low(jnp.exp(jnp.minimum(row[:, half:] - col[half:], 0.0)) * table[half:, half:])
            x = x4[h * HDIM : (h + 1) * HDIM, :]
            y = nn(x[:, :half], upper)
            results.append(jnp.concatenate([y[:, :half], y[:, half:] + nn(x[:, half:], lower)], axis=1))
        out[chunk(g), :] = jnp.concatenate(results, axis=0)
        return 0

    lax.fori_loop(0, GROUPS, heads, 0)


def gate_kernel(
    inside, enter, last, maps, signal, gate, grad, cum, marks, coef,
    gated_low, grad_gate, grad_scan, carried_sum, skip_sum, gain_sum, grad_state, grad_read, scan, entry
):
    entry[...] = marks[6:7, :] * jnp.exp(cum[...])
    reads = low(maps[LANES:, :])

    @pl.when(pl.program_id(0) == 0)
    def _():
        gain_sum[...] = jnp.zeros_like(gain_sum)

    def forward(r, sums):
        carried = nn(enter[0, chunk(r), :] + last[0, chunk(r), :], reads) * by_head(entry, r)
        total = inside[chunk(r), :] + carried + coef[chunk(r), 1:2] * signal[chunk(r), :]
        scan[chunk(r), :] = total
        z = gate[chunk(r), :]
        gated = total * (z * sigmoid(z))
        up = grad[chunk(r), :] * coef[chunk(r), 0:1]
        squares, cross = sums
        return (
            squares + jnp.sum(gated * gated, axis=0, keepdims=True),
            cross + jnp.sum(gated * up, axis=0, keepdims=True),
        )

    nothing = jnp.zeros((1, SPAN), F32)
    squares, cross = lax.fori_loop(0, 8, forward, (nothing, nothing))
    factor = lax.rsqrt(squares * (1.0 / DI) + EPSILON)
    pull = factor * factor * cross * (1.0 / DI)
    grad_read[...] = jnp.zeros_like(grad_read)

    def backward(r, _):
        heads = by_head(entry, r)
        state = enter[0, chunk(r), :] + last[0, chunk(r), :]
        carried = nn(state, reads) * heads
        total = scan[chunk(r), :]
        z = gate[chunk(r), :]
        sig = sigmoid(z)
        soft = z * sig
        gated = total * soft
        scaled = gated * factor
        gain = coef[chunk(r), 0:1]
        given = grad[chunk(r), :]
        gated_low[chunk(r), :] = low(scaled * gain)
        share = given * scaled
        gain_sum[chunk(r), :] += share[:, :LANES] + share[:, LANES:]
        back = factor * (given * gain - gated * pull)
        grad_gate[chunk(r), :] = low(back * total * (sig * (1.0 + z * (1.0 - sig))))
        push = back * soft
        grad_scan[chunk(r), :] = push
        put_head_sums(carried_sum, r, push * carried)
        put_head_sums(skip_sum, r, push * signal[chunk(r), :])
        entering = low(push * heads)
        grad_state[0, chunk(r), :] = low(nt(entering, reads))
        grad_read[...] += tn(state, entering)
        return 0

    lax.fori_loop(0, 8, backward, 0)


def within_back_kernel(
    inflow, push, inside, maps, cum, cols, docs, marks, grad_inflow, decay_sum, grad_maps, table, grad_table
):
    table[...] = mixing(maps, docs, marks)
    grad_table[...] = jnp.zeros_like(grad_table)
    half = SPAN // 2

    def heads(g, _):
        x4, d4, results = inflow[chunk(g), :], low(push[chunk(g), :]), []
        above, below = 0.0, 0.0
        for h in range(4):
            rows = slice(h * HDIM, (h + 1) * HDIM)
            row, col = cum[pl.ds(4 * g + h, 1), :], cols[g, :, h : h + 1]
            upper = jnp.exp(jnp.minimum(row - col[:half], 0.0))
            lower = jnp.exp(jnp.minimum(row[:, half:] - col[half:], 0.0))
            x, d = x4[rows, :], d4[rows, :]
            above += upper * tn(x[:, :half], d)
            below += lower * tn(x[:, half:], d[:, half:])
            first = nt(d, low(upper * table[:half, :]))
            second = nt(d[:, half:], low(lower * table[half:, half:]))
            results.append(jnp.concatenate([first, second], axis=1))
        grad_table[:half, :] += above
        grad_table[half:, half:] += below
        back = jnp.concatenate(results, axis=0)
        grad_inflow[chunk(g), :] = back
        put_head_sums(decay_sum, g, real(d4) * inside[chunk(g), :] - real(x4) * back)
        return 0

    lax.fori_loop(0, GROUPS, heads, 0)
    inner = (docs[...] == marks[9:10, :]) & (iota((SPAN, SPAN), 0) <= iota((SPAN, SPAN), 1))
    spread = low(jnp.where(inner, grad_table[...], 0.0))
    grad_maps[0:LANES, :] = nt(low(maps[LANES:, :]), spread)
    grad_maps[LANES:, :] = nn(low(maps[0:LANES, :]), spread)


def state_back_kernel(
    leave, leave_last, enter, enter_last, conv, push, grad_inflow, maps, cum, step, raw, decay_sum, carried_sum, grad_maps, grad_read,
    steps, marks, coef, grad_conv, rim, grad_raw, bias_sum, rate_sum, tail, from_tail, from_step, crossing, grad_write
):
    ends = cum[:, SPAN - 1 : SPAN]
    tail[...] = marks[7:8, :] * jnp.exp(ends - cum[...])
    writes = low(maps[0:LANES, :])
    front = ((iota((16, SPAN), 1) == iota((16, SPAN), 0)) & (iota((16, SPAN), 0) < 3)).astype(jnp.bfloat16)
    grad_write[...] = grad_maps[0:LANES, :]

    def through_silu(r, c, sig, above):
        given = above * (sig * (1.0 + c * (1.0 - sig)))
        grad_conv[chunk(r), :] = given
        rim[0, :, chunk(r)] = low(nt(front, low(given)))

    def channels(r, _):
        c = conv[chunk(r), :]
        sig = sigmoid(c)
        signal = c * sig
        heads, tails = by_head(step, r), by_head(tail, r)
        x = signal * heads
        back = leave[0, chunk(r), :] + leave_last[0, chunk(r), :]
        ended = nn(back, writes) * tails
        whole = grad_inflow[chunk(r), :] + ended
        grad_write[...] += tn(back, low(x * tails))
        put_head_sums(from_tail, r, x * ended)
        put_head_sums(from_step, r, whole * signal)
        put_head_sums(crossing, r, real(back) * real(enter[0, chunk(r), :] + enter_last[0, chunk(r), :]))
        through_silu(r, c, sig, whole * heads + coef[chunk(r), 1:2] * push[chunk(r), :])
        return 0

    lax.fori_loop(0, 8, channels, 0)
    c = conv[chunk(8), :]
    through_silu(8, c, sigmoid(c), jnp.concatenate([grad_write[...], grad_maps[LANES:, :] + grad_read[...]], axis=0))
    last = iota((HEADS, SPAN), 1) == SPAN - 1
    passing = marks[8:9, 0:1] * jnp.exp(ends) * jnp.sum(crossing[...], axis=1, keepdims=True)
    tails = jnp.sum(from_tail[...], axis=1, keepdims=True)
    total = decay_sum[...] + carried_sum[...] - from_tail[...] + jnp.where(last, tails + passing, 0.0)
    onward = (iota((SPAN, SPAN), 0) >= iota((SPAN, SPAN), 1)).astype(F32)
    grad_decay = nn(total, onward, lax.Precision.HIGHEST)
    rate = steps[:, 1:2]
    rate_sum[...] = -grad_decay * step[...] * rate
    grad_step = (from_step[...] - grad_decay * rate) * sigmoid(raw[...] + steps[:, 0:1])
    bias_sum[...] = grad_step
    grad_raw[0:HEADS, :] = low(grad_step)
    grad_raw[HEADS:, :] = jnp.zeros((LANES - HEADS, SPAN), jnp.bfloat16)


def conv_back_kernel(grad_conv, ci, rim, taps, marks, grad_ci, sums, move, enter):
    @pl.when(pl.program_id(0) == 0)
    def _():
        for m in range(MICRO):
            here = marks[:, m * SPAN : (m + 1) * SPAN]
            move[m] = shifts(here, 3, SPAN, 1, 0)
            enter[m] = shifts(here, 3, 16, 1, -SPAN) * (iota((16, 3 * SPAN), 0) < 3).astype(jnp.bfloat16)

    totals = [0.0] * 5
    for m in range(MICRO):
        part = slice(m * SPAN, (m + 1) * SPAN)
        given, x = grad_conv[:, part], real(ci[:, part])
        moved = nn(low(given), move[m]) + tn(rim[m], enter[m])
        back = given * taps[:, 3:4]
        totals[3] += given * x
        totals[4] += given
        for d in range(1, 4):
            sooner = moved[:, (d - 1) * SPAN : d * SPAN]
            back += sooner * taps[:, 3 - d : 4 - d]
            totals[3 - d] += sooner * x
        grad_ci[:, part] = low(back)
    count = jnp.zeros((ROWS, LANES), F32)
    for k in range(5):
        pick = (iota((SPAN, LANES), 1) == k).astype(jnp.bfloat16)
        count += nn(low(totals[k]), pick)
    sums[...] = count[:, 0:8]


def call(kernel, grid, ins, outs, scratch, cost, name):
    return pl.pallas_call(
        kernel,
        grid=grid,
        in_specs=[pl.BlockSpec(block, where) for _, block, where in ins],
        out_specs=[pl.BlockSpec(block, where) for _, _, block, where in outs],
        out_shape=[jax.ShapeDtypeStruct(shape, dtype) for shape, dtype, _, _ in outs],
        scratch_shapes=scratch,
        compiler_params=pltpu.CompilerParams(
            vmem_limit_bytes=56 * 2**20, dimension_semantics=("arbitrary",) * len(grid)
        ),
        cost_estimate=pl.CostEstimate(flops=cost, bytes_accessed=20_000_000, transcendentals=0),
        name=name,
    )(*[array for array, _, _ in ins])


def neighbours(value, source, target):
    return lax.ppermute(value, GROUP, [(source, target)])


def chained(local, through, order, beside):
    by_heads = (MICRO, HEADS, HDIM, STATE)

    def joined(arrived):
        total = through[:, :, None, :] * real(arrived).reshape(by_heads) + real(local).reshape(by_heads)
        return low(total).reshape(local.shape)

    one = neighbours(local, order[0], order[1])
    two = neighbours(joined(one), order[1], order[2])
    two, beside = lax.optimization_barrier((two, beside))
    three = neighbours(joined(two), order[2], order[3])
    return (one + two, three), beside


def shards(
    tokens, segments, cotangent, norm_gain, in_weight, conv_kernel, conv_bias, step_bias, decay_log,
    skip_gain, gate_gain, out_weight, master, moment_one, moment_two, step_count
):
    width = MICRO * SPAN
    bf16 = jnp.bfloat16
    spot = position()
    place = lax.axis_index(GROUP)
    ids = segments[:, 0, :]
    window = jnp.pad(ids, ((0, 0), (3, 3)), constant_values=-1)
    window = lax.dynamic_slice(window, (0, place * SPAN), (MICRO, SPAN + 6))
    here = window[:, 3 : 3 + SPAN]
    before = [window[:, 3 - d : 3 - d + SPAN] == here for d in (1, 2, 3)]
    after = [window[:, 3 + d : 3 + d + SPAN] == here for d in (1, 2, 3)]
    prior, final = window[:, 2:3], here[:, SPAN - 1 :]
    rows = before + after + [here == prior, here == final, jnp.broadcast_to(final == prior, here.shape)]
    marks = jnp.stack([row.astype(F32) for row in rows] + [here.astype(F32)] + [jnp.zeros(here.shape, F32)] * 6)
    marks = marks.reshape(16, width)
    docs = here.astype(F32).reshape(width, 1)

    norm_real = real(norm_gain)
    rows_in = real(tokens.reshape(width, D))
    normed, norm_back = jax.vjp(norm_piece, rows_in, norm_real)
    normed_low = low(normed)
    rim_tokens = lax.ppermute(tokens[:, 0, SPAN - 3 :, :], GROUP, [(0, 1), (1, 2), (2, 3)])
    rim_low = low(norm_piece(real(rim_tokens).reshape(-1, D), norm_real))
    rim_low = jnp.pad(rim_low.reshape(MICRO, 3, D), ((0, 0), (0, 13), (0, 0)))
    turned_weight = in_weight.T
    conv_weight = turned_weight[DI : DI + CH]
    gate = nt(turned_weight[:DI], normed_low)
    upstream = cotangent.reshape(width, D)
    grad_mixed = nt(out_weight, upstream)

    taps = jnp.concatenate([real(conv_kernel), real(conv_bias)[None], jnp.zeros((3, CH), F32)]).T
    steps = jnp.stack([real(step_bias), jnp.exp(real(decay_log))] + [jnp.zeros((HEADS,), F32)] * 6, axis=1)
    coef = jnp.stack([real(gate_gain), jnp.repeat(real(skip_gain), HDIM)] + [jnp.zeros((DI,), F32)] * 6, axis=1)

    one = (MICRO,)
    by_m = lambda m: (0, m)
    whole, first = lambda m: (0, 0), lambda m: (m, 0, 0)
    mark_in = (marks, (16, SPAN), by_m)

    whole1, head_rows = lambda r: (0, 0), lambda r: (jnp.maximum(r - 1, 0), 0)
    rows_of = lambda r: jnp.where(r == 0, GROUPS, r - 1)
    by_rows = lambda r: (rows_of(r), 0)
    lot = (HEADS, width)
    ci, conv, signal, inflow, maps, raw, cum, step, cols, local, through = call(
        prepare_kernel, (CH // ROWS,),
        [(turned_weight, (ROWS, D), lambda r: (GROUPS + rows_of(r), 0)),
         (turned_weight, (HEADS, D), lambda r: ((DI + CH) // HEADS, 0)), (normed_low, (width, D), whole1),
         (rim_low.reshape(-1, D), (32, D), whole1), (taps, (ROWS, 8), by_rows), (steps, (HEADS, 8), whole1),
         (marks, (16, width), whole1)],
        [((CH, width), bf16, (ROWS, width), by_rows), ((CH, width), F32, (ROWS, width), by_rows),
         ((DI, width), F32, (ROWS, width), head_rows), ((DI, width), bf16, (ROWS, width), head_rows),
         ((2 * STATE, width), F32, (2 * STATE, width), whole1), (lot, F32, lot, whole1), (lot, F32, lot, whole1),
         (lot, F32, lot, whole1), ((GROUPS, width, 4), F32, (GROUPS, width, 4), lambda r: (0, 0, 0)),
         ((MICRO, DI, STATE), bf16, (MICRO, ROWS, STATE), lambda r: (0, jnp.maximum(r - 1, 0), 0)),
         ((MICRO, HEADS, LANES), F32, (MICRO, HEADS, LANES), lambda r: (0, 0, 0))],
        [pltpu.VMEM(lot, F32), pltpu.VMEM((MICRO, SPAN, 3 * SPAN), bf16), pltpu.VMEM((MICRO, 16, 3 * SPAN), bf16)],
        10**9, "project_and_convolve",
    )

    tall, few = (DI, SPAN), (HEADS, SPAN)
    state_block = (1, DI, STATE)
    head_ins = [
        (maps, (2 * STATE, SPAN), by_m),
        (cum, few, by_m),
        (cols, (GROUPS, SPAN, 4), lambda m: (0, m, 0)),
        (docs, (SPAN, 1), lambda m: (m, 0)),
        mark_in,
    ]
    table = pltpu.VMEM((SPAN, SPAN), F32)
    (inside,) = call(
        within_kernel, one, [(inflow, tall, by_m)] + head_ins, [((DI, width), F32, tall, by_m)], [table],
        4 * 10**9, "within_blocks",
    )
    enter, (inside, gate, grad_mixed) = chained(local, through, (0, 1, 2, 3), (inside, gate, grad_mixed))

    gated_low, grad_gate, push, carried_sum, skip_sum, gain_sum, grad_state, grad_read = call(
        gate_kernel, one,
        [(inside, tall, by_m), (enter[0], state_block, first), (enter[1], state_block, first), (maps, (2 * STATE, SPAN), by_m), (signal, tall, by_m),
         (gate, tall, by_m), (grad_mixed, tall, by_m), (cum, (HEADS, SPAN), by_m), mark_in, (coef, (DI, 8), whole)],
        [((DI, width), bf16, tall, by_m), ((DI, width), bf16, tall, by_m), ((DI, width), F32, tall, by_m),
         ((HEADS, width), F32, (HEADS, SPAN), by_m), ((HEADS, width), F32, (HEADS, SPAN), by_m),
         ((DI, LANES), F32, (DI, LANES), whole), ((MICRO, DI, STATE), bf16, state_block, first),
         ((STATE, width), F32, (STATE, SPAN), by_m)],
        [pltpu.VMEM((DI, SPAN), F32), pltpu.VMEM((HEADS, SPAN), F32)], 2 * 10**9, "gate_and_back",
    )
    grad_inflow, decay_sum, grad_maps = call(
        within_back_kernel, one, [(inflow, tall, by_m), (push, tall, by_m), (inside, tall, by_m)] + head_ins,
        [((DI, width), F32, tall, by_m), ((HEADS, width), F32, few, by_m),
         ((2 * STATE, width), F32, (2 * STATE, SPAN), by_m)],
        [table, table], 8 * 10**9, "within_blocks_back",
    )
    left, cot = call(
        turn_kernel, (1,), [(normed_low, (width, D), whole), (upstream, (width, D), whole)],
        [((D, width), bf16, (D, width), whole), ((width, D), bf16, (width, D), whole)],
        [pltpu.VMEM((D, LANES), F32)], 10**6, "turn",
    )
    leave, (grad_inflow, decay_sum, grad_maps, left, cot) = chained(
        grad_state, through, (3, 2, 1, 0), (grad_inflow, decay_sum, grad_maps, left, cot)
    )

    grad_conv, rim, grad_raw, bias_sum, rate_sum = call(
        state_back_kernel, one,
        [(leave[0], state_block, first), (leave[1], state_block, first), (enter[0], state_block, first),
         (enter[1], state_block, first), (conv, (CH, SPAN), by_m), (push, tall, by_m),
         (grad_inflow, tall, by_m), (maps, (2 * STATE, SPAN), by_m), (cum, few, by_m), (step, few, by_m), (raw, few, by_m),
         (decay_sum, few, by_m), (carried_sum, few, by_m), (grad_maps, (2 * STATE, SPAN), by_m),
         (grad_read, (STATE, SPAN), by_m), (steps, (HEADS, 8), whole), mark_in, (coef, (DI, 8), whole)],
        [((CH, width), F32, (CH, SPAN), by_m), ((MICRO, 16, CH), bf16, (1, 16, CH), first),
         ((LANES, width), bf16, (LANES, SPAN), by_m), ((HEADS, width), F32, few, by_m), ((HEADS, width), F32, few, by_m)],
        [pltpu.VMEM(few, F32), pltpu.VMEM(few, F32), pltpu.VMEM(few, F32), pltpu.VMEM((HEADS, LANES), F32),
         pltpu.VMEM((STATE, SPAN), F32)], 10**9, "state_and_silu_back",
    )
    next_rim = lax.ppermute(rim, GROUP, [(1, 0), (2, 1), (3, 2)])
    early = tn(grad_gate, turned_weight[:DI])
    next_rim, early = lax.optimization_barrier((next_rim, early))

    by_r = lambda r: (r, 0)
    grad_ci, tap_sums = call(
        conv_back_kernel, (CH // ROWS,),
        [(grad_conv, (ROWS, width), by_r), (ci, (ROWS, width), by_r), (next_rim, (MICRO, 16, ROWS), lambda r: (0, 0, r)),
         (taps, (ROWS, 8), by_r), (marks, (16, width), lambda r: (0, 0))],
        [((CH, width), bf16, (ROWS, width), by_r), ((CH, 8), F32, (ROWS, 8), by_r)],
        [pltpu.VMEM((MICRO, SPAN, 3 * SPAN), bf16), pltpu.VMEM((MICRO, 16, 3 * SPAN), bf16)], 10**8, "convolution_back",
    )

    middle = [tap_sums[:, :5].T.reshape(-1), jnp.sum(bias_sum, axis=1), jnp.sum(rate_sum, axis=1)]
    middle += [jnp.sum(skip_sum, axis=1), jnp.sum(gain_sum, axis=1), jnp.zeros((32 + 5 * LANES,), F32)]
    middle = jnp.concatenate(middle).reshape(-1, LANES)
    packed = pack(spot, left, grad_gate, grad_ci, grad_raw, gated_low, cot, middle)
    packed, late = lax.optimization_barrier((packed, (grad_gate, grad_ci, grad_raw)))
    grad_normed = early + tn(late[1], conv_weight) + tn(late[2][:HEADS], turned_weight[DI + CH :])
    grad_rows, grad_norm_gain = norm_back(grad_normed)

    def finish(inputs):
        gated_low, grad_rows = inputs
        output = low(rows_in + tn(gated_low, out_weight)).reshape(tokens.shape)
        return output, low(real(upstream) + grad_rows).reshape(tokens.shape)

    piece, (output, input_grad) = reduce_pieces(
        packed[:3], packed[3:], grad_norm_gain.reshape(-1, LANES), finish, (gated_low, grad_rows)
    )

    skew = (12 * lax.axis_index("x")) % 16
    offset = PIECE * place - skew
    line = offset + iota((PIECE, 1), 0)
    own = jnp.where((line >= 0) & (line < SHARD_LINES), piece, 0.0)
    squares = sent_to_all(jnp.sum(own * own).reshape(1, 1), EVERY).reshape(1, -1)
    core, high = lax.axis_index("core") == 0, lax.axis_index("zh") == 0
    pair = [piece, swap_cores(piece)]
    pair = jnp.concatenate([jnp.where(core, *pair), jnp.where(core, *pair[::-1])])
    both = [pair, lax.ppermute(pair, "zh", [(0, 1), (1, 0)])]
    step_real = real(step_count[0])
    scales = jnp.stack([1.0 / (1.0 - jnp.power(BETA_ONE, step_real)), 1.0 / (1.0 - jnp.power(BETA_TWO, step_real))])
    both, squares = lax.optimization_barrier((both, squares))
    mine = own_update(offset, scales, squares, piece, master, moment_one, moment_two)

    window = jnp.concatenate([jnp.where(high, *both), jnp.where(high, *both[::-1])])
    shard = lax.dynamic_slice(window, (skew, 0), (SHARD_LINES, LANES)).reshape(-1)
    clip_factor = MAX_NORM / jnp.maximum(jnp.sqrt(jnp.sum(squares)), MAX_NORM)
    results = adam_step(shard * clip_factor, master, moment_one, moment_two, scales[0], scales[1])
    pieces, (shard, results) = lax.optimization_barrier((gather_pieces(mine), (shard, results)))
    copies = unpack(spot, pieces).reshape(-1)
    return (output, input_grad, shard, *results, copies)


def solution(mesh):
    finer = Mesh(mesh.devices.reshape(4, 2, 4, 2, 2), ("y", "zl", "x", "zh", "core"))
    return jax.shard_map(
        shards,
        mesh=finer,
        in_specs=(
            P(None, DP, GROUP, None),
            P(None, DP, None),
            P(None, DP, GROUP, None),
            P(),
            P(),
            P(),
            P(),
            P(),
            P(),
            P(),
            P(),
            P(),
            P(DP),
            P(DP),
            P(DP),
            P(),
        ),
        out_specs=(
            P(None, DP, GROUP, None),
            P(None, DP, GROUP, None),
            P(DP),
            P(DP),
            P(DP),
            P(DP),
            P(),
        ),
        check_vma=False,
    )
```

```python
import functools

import jax
import jax.numpy as jnp
from jax import lax
from jax.experimental import pallas as pl
from jax.experimental.pallas import tpu as pltpu
from jax.sharding import Mesh
from jax.sharding import PartitionSpec as P

D = 1024
DI = 2048
HEADS = 32
HDIM = 64
STATE = 128
CH = 2304
DP = ("y", "zl", "x")
GROUP = ("zh", "core")
EVERY = DP + GROUP


EPSILON = 1e-05
BETA_ONE = 0.9
BETA_TWO = 0.95
ADAM_EPSILON = 1e-08
LEARN_RATE = 0.01
WEIGHT_DECAY = 0.1
MAX_NORM = 1.0


def sent_to_all(shard, axis):
    copies = jnp.broadcast_to(shard, (lax.axis_size(axis), *shard.shape))
    return lax.all_to_all(copies, axis, split_axis=0, concat_axis=0, tiled=True)


def norm_piece(values, scaling):
    factor = lax.rsqrt(jnp.mean(values * values, axis=-1, keepdims=True) + EPSILON)
    return values * factor * scaling


def adam_step(clipped, master, moment_one, moment_two, first_scale, second_scale):
    first_moment = BETA_ONE * moment_one + (1.0 - BETA_ONE) * clipped
    second_moment = BETA_TWO * moment_two + (1.0 - BETA_TWO) * clipped * clipped
    first_hat, second_hat = first_moment * first_scale, second_moment * second_scale
    updated = master - LEARN_RATE * (first_hat / (jnp.sqrt(second_hat) + ADAM_EPSILON) + WEIGHT_DECAY * master)
    return (first_moment, second_moment, updated)


LANES = 128
LINES = 51584
SHARD_LINES = 1612
IN_LINE = 8
MID_LINE = 35080
OUT_LINE = 35187
PIECE = 416
SLOTS = 16
PARTS = ((0, 208), (208, 208))
TAIL_LINES = 51632
GROUP_LINES = 137
RING = {"x": ("x",), "y": ("y",), "z": ("zl", "zh")}
ROUTES = (("x", "y", "z"), ("y", "x", "z"))


def ring_place(axis, i):
    i = i % 4
    return (i % 2) * 2 + i // 2 if axis == "z" else i


def from_offset(block, axis, distance):
    route = [(ring_place(axis, i + distance), ring_place(axis, i)) for i in range(4)]
    return lax.ppermute(block, RING[axis], route)


def swap_cores(block):
    return lax.ppermute(block, "core", [(0, 1), (1, 0)])


def position():
    z = 2 * lax.axis_index("zh") + lax.axis_index("zl")
    return jnp.stack([lax.axis_index("y"), z, lax.axis_index("x"), lax.axis_index("core")]).astype(jnp.int32)


def first_tile(shard):
    return (403 * shard) >> 2


def pack_kernel(pos, mid_part, *rest):
    sources, keep, send = rest[:6], rest[6:8], rest[8:10]
    flat, carry, edge, stage, sems = rest[10:15]
    left, grad_gate, grad_ci, grad_raw, gated, cot = held = rest[15:21]
    loads = [pltpu.make_async_copy(source, here, rest[21].at[k]) for k, (source, here) in enumerate(zip(sources, held))]
    for k in (4, 5, 0, 1, 2, 3):
        loads[k].start()
    lane = lax.broadcasted_iota(jnp.int32, (256, LANES), 1)

    flat[0:IN_LINE, :] = jnp.zeros((IN_LINE, LANES), jnp.float32)
    flat[MID_LINE : MID_LINE + 104, :] = mid_part[0:104, :]
    flat[MID_LINE + 104 : MID_LINE + 107, :] = mid_part[104:107, :]
    edge[0:8, :] = mid_part[99:107, :]

    def rows(b, _):
        block = gated[pl.ds(pl.multiple_of(b * 256, 256), 256), :]
        product = jnp.dot(block, cot[...], preferred_element_type=jnp.float32)
        start = OUT_LINE + 2048 * b
        for t in range(7):
            flat[pl.ds(start + t, 256, stride=8), :] = product[:, t * LANES : (t + 1) * LANES]
        last = product[:, 7 * LANES :]
        edge[8:264, :] = last
        flat[pl.ds(start - 1, 256, stride=8), :] = jnp.where(lane < 96, edge[7:263, :], last)
        edge[0:8, :] = edge[256:264, :]
        return 0

    loads[4].wait()
    loads[5].wait()
    lax.fori_loop(0, 8, rows, 0)
    low = lax.broadcasted_iota(jnp.int32, (1, LANES), 1) < 96
    flat[OUT_LINE + 16383 : TAIL_LINES, :] = jnp.zeros((TAIL_LINES - OUT_LINE - 16383, LANES), jnp.float32)
    flat[OUT_LINE + 16383 : OUT_LINE + 16384, :] = jnp.where(low, edge[7:8, :], 0.0)

    my_y, my_z, my_x, my_core = pos[0], pos[1], pos[2], pos[3]

    def drain(slot):
        pltpu.make_async_copy(stage.at[slot], keep[0].at[pl.ds(0, PIECE)], sems.at[slot]).wait()

    def ship(n, _):
        i = (n + 88) & 127
        slot = n & (SLOTS - 1)

        @pl.when(n >= SLOTS)
        def _():
            drain(slot)

        shard, quarter = i >> 2, i & 3
        line = 16 * first_tile(shard) + PIECE * quarter
        stage[slot] = flat[pl.ds(pl.multiple_of(line, 16), PIECE), :].astype(jnp.bfloat16)
        x, zl, y = shard & 3, (shard >> 2) & 1, shard >> 3
        core = quarter & 1
        z = 2 * (quarter >> 1) + zl
        off = {"y": (y - my_y) & 3, "z": (z - my_z) & 3, "x": (x - my_x) & 3}
        for p, (start, size) in enumerate(PARTS):
            a, b, c = (off[axis] for axis in ROUTES[p])
            to = pl.ds(pl.multiple_of(((a * 4 + b) * 4 + c) * size, 16), size)
            source = stage.at[slot, pl.ds(start, size)]

            @pl.when(core == my_core)
            def _():
                pltpu.make_async_copy(source, keep[p].at[to], sems.at[slot]).start()

            @pl.when(core != my_core)
            def _():
                pltpu.make_async_copy(source, send[p].at[to], sems.at[slot]).start()

        return 0

    lax.fori_loop(0, 40, ship, 0)

    def put(tile, k, line):
        moved = pltpu.roll(tile, 32 * k, 1) if k else tile
        whole = jnp.where(lane < 32 * k, carry[k], moved) if k else moved
        flat[pl.ds(IN_LINE + 34 * k + line, 256, stride=GROUP_LINES), :] = whole
        carry[k] = moved

    def columns(block, line, tiles):
        product = nt(left[...], block)
        for k in range(4):
            for t in range(tiles):
                put(product[256 * k : 256 * (k + 1), t * LANES : (t + 1) * LANES], k, line + t)

    def from_gate(j, _):
        columns(grad_gate[pl.ds(pl.multiple_of(j * 512, 512), 512), :], 4 * j, 4)
        return 0

    def from_conv(j, _):
        columns(grad_ci[pl.ds(pl.multiple_of(j * 512, 512), 512), :], 16 + 4 * j, 4)
        return 0

    loads[0].wait()
    loads[1].wait()
    lax.fori_loop(0, 4, from_gate, 0)
    loads[2].wait()
    loads[3].wait()
    lax.fori_loop(0, 4, from_conv, 0)
    heads = []
    for k in range(1, 4):
        heads.append(flat[pl.ds(IN_LINE + 34 * k, 256, stride=GROUP_LINES), :])
    columns(jnp.concatenate([grad_ci[2048:2304, :], grad_raw[...]], axis=0), 32, 3)
    for k in range(1, 4):
        at = pl.ds(IN_LINE + 34 * k, 256, stride=GROUP_LINES)
        flat[at, :] = jnp.where(lane < 32 * k, flat[at, :], heads[k - 1])

    lax.fori_loop(40, 128, ship, 0)
    for slot in range(SLOTS):
        drain(slot)


def pack(pos, left, grad_gate, grad_ci, grad_raw, gated, cot, mid_part):
    vmem, hbm = pl.BlockSpec(memory_space=pltpu.VMEM), pl.BlockSpec(memory_space=pl.ANY)
    shapes = [jax.ShapeDtypeStruct((64 * size, LANES), jnp.bfloat16) for _, size in PARTS]
    return pl.pallas_call(
        pack_kernel,
        out_shape=shapes + shapes,
        in_specs=[pl.BlockSpec(memory_space=pltpu.SMEM)] + [vmem] + [hbm] * 6,
        out_specs=[hbm] * 4,
        scratch_shapes=[
            pltpu.VMEM((TAIL_LINES, LANES), jnp.float32),
            pltpu.VMEM((4, 256, LANES), jnp.float32),
            pltpu.VMEM((264, LANES), jnp.float32),
            pltpu.VMEM((SLOTS, PIECE, LANES), jnp.bfloat16),
            pltpu.SemaphoreType.DMA((SLOTS,)),
        ]
        + [pltpu.VMEM(v.shape, v.dtype) for v in (left, grad_gate, grad_ci, grad_raw, gated, cot)]
        + [pltpu.SemaphoreType.DMA((6,))],
        compiler_params=pltpu.CompilerParams(vmem_limit_bytes=60 * 2**20),
        cost_estimate=pl.CostEstimate(flops=7_000_000_000, bytes_accessed=25_000_000, transcendentals=0),
        name="pack_gradients",
    )(pos, mid_part, left, grad_gate, grad_ci, grad_raw, gated, cot)


def real(v):
    return v.astype(jnp.float32)


def low(v):
    return v.astype(jnp.bfloat16)


def to_offset(block, axis, distance):
    route = [(ring_place(axis, i), ring_place(axis, i + distance)) for i in range(4)]
    return lax.ppermute(block, RING[axis], route)


def quarters(block):
    return block.reshape(4, -1, LANES)


def ring_sum(block, axis):
    block = quarters(block)
    half = block.shape[1] // 32 * 16
    a, b = to_offset(block[2, :half], axis, 1), to_offset(block[2, half:], axis, 3)
    one = jnp.concatenate([low(real(block[1, :half]) + real(a)), block[1, half:]])
    three = jnp.concatenate([block[3, :half], low(real(block[3, half:]) + real(b))])
    return real(block[0]) + real(to_offset(one, axis, 1)) + real(to_offset(three, axis, 3))


def direct_sum(block, axis):
    block = quarters(block)
    moved = [to_offset(block[d], axis, d) for d in (1, 3, 2)]
    return real(block[0]) + real(moved[0]) + real(moved[1]) + real(moved[2])


def reduce_pieces(keep, send, gain_grad, beside, given):
    held = [low(real(mine) + real(swap_cores(other))) for mine, other in zip(keep, send)]
    gain_grad = low(gain_grad + swap_cores(gain_grad))
    x, y, z = lax.axis_index("x"), lax.axis_index("y"), 2 * lax.axis_index("zh") + lax.axis_index("zl")
    block = 16 * (-x & 3) + 4 * (-y & 3) + (-z & 3)
    lines = jnp.arange(16)[:, None]
    mine = (lines < IN_LINE) & (lax.axis_index("core") == 0)
    start = (block * PARTS[0][1], 0)
    tile = lax.dynamic_slice(held[0], start, (16, LANES))
    tile = jnp.where(mine, jnp.pad(gain_grad, ((0, 16 - IN_LINE), (0, 0))), tile)
    held[0] = lax.dynamic_update_slice(held[0], tile, start)
    held, given = lax.optimization_barrier((held, given))
    first, second = low(ring_sum(held[0], "x")), low(ring_sum(held[1], "y"))
    (first, second), done = lax.optimization_barrier(((first, second), beside(given)))
    first, second = low(direct_sum(first, "y")), low(direct_sum(second, "x"))
    both = jnp.concatenate([quarters(first), quarters(second)], axis=1).reshape(-1, LANES)
    return direct_sum(both, "z"), done


def join_kernel(*refs):
    *blocks, first, second = refs
    for out, parts in ((first, blocks[: len(blocks) // 2]), (second, blocks[len(blocks) // 2 :])):
        start = 0
        for block in parts:
            out[start : start + block.shape[0], :] = block[...]
            start += block.shape[0]


def join(first, second):
    vmem = pl.BlockSpec(memory_space=pltpu.VMEM)
    rows = [sum(block.shape[0] for block in parts) for parts in (first, second)]
    return pl.pallas_call(
        join_kernel,
        out_shape=[jax.ShapeDtypeStruct((n, LANES), jnp.bfloat16) for n in rows],
        in_specs=[vmem] * (len(first) + len(second)),
        out_specs=[vmem] * 2,
        compiler_params=pltpu.CompilerParams(vmem_limit_bytes=8 * 2**20),
        name="join",
    )(*first, *second)


def gather_pieces(piece, beside, given):
    def spread(block, axis):
        return [block] + [from_offset(block, axis, d) for d in (1, 3, 2)]

    def in_order(parts):
        return [parts[0], parts[1], parts[3], parts[2]]

    n = PARTS[0][1]
    both = spread(piece, "z")
    both = in_order(both)
    first = spread(jnp.concatenate([block[:n] for block in both]), "y")
    second = spread(jnp.concatenate([block[n:] for block in both]), "x")
    first, second = join(in_order(first), in_order(second))
    ends = [(first, "x"), (second, "y")]
    sides = [[from_offset(block, axis, d) for d in (1, 3)] for block, axis in ends]
    swapped = [swap_cores(block) for block, _ in ends]
    swapped, given = lax.optimization_barrier((swapped, given))
    sides, swapped, done = lax.optimization_barrier((sides, swapped, beside(given)))
    mine, other = [], []
    for (block, axis), (left, right), first in zip(ends, sides, swapped):
        half = block.shape[0] // 2
        halves = [from_offset(right[:half], axis, 3), from_offset(left[half:], axis, 1)]
        mine += [block, left, right, *halves]
        left, right, halves = lax.optimization_barrier((left, right, halves))
        other += [first] + [swap_cores(part) for part in (left, right, *halves)]
    return mine + other, done


def unpack_kernel(pos, *rest):
    sources, out = rest[:20], rest[20]
    whole, edges, sem = rest[21:]
    my_y, my_z, my_x, my_core = pos[0], pos[1], pos[2], pos[3]
    row = lax.broadcasted_iota(jnp.int32, (16, LANES), 0)

    def put(source, here, line, size):
        whole[pl.ds(pl.multiple_of(line, 16), size), :] = source[pl.ds(pl.multiple_of(here, 16), size), :]

    def at(far_y, z, x, core):
        shard = (((my_y + far_y) & 3) << 3) + ((z & 1) << 2) + x
        line = first_tile(shard) << 4
        return shard & 7, line, line + PIECE * (2 * (z >> 1) + core)

    rows_of_y = 8 * SHARD_LINES
    for far_y in range(4):
        for other in range(2):
            core = (my_core + other) & 1
            for array, far_x in enumerate((0, 1, 3, 2)):
                array = 4 if array == 3 and far_y >= 2 else array
                source = sources[10 * other + array]

                def first(i, _, source=source, far_x=far_x, far_y=far_y, core=core, array=array):
                    z, x = (my_z + i) & 3, (my_x + far_x) & 3
                    shard, start, line = at(far_y, z, x, core)
                    here = (4 * (far_y - 2 * (array == 4)) + i) * 208
                    put(source, here + 16, line + 16, 192)

                    @pl.when(line == start)
                    def _():
                        edges[0, shard] = source[pl.ds(pl.multiple_of(here, 16), 16), :]

                    @pl.when(line != start)
                    def _():
                        put(source, here, line, 16)

                    return 0

                lax.fori_loop(0, 4, first, 0, unroll=True)

            array = (0, 1, 3, 2)[far_y]
            for skip, array in ((0, array), (8, array)) if array < 3 else ((0, 3), (8, 4)):
                source = sources[10 * other + 5 + array]

                def second(i, _, source=source, far_y=far_y, core=core, skip=skip, array=array):
                    x, z = (my_x + ((i + skip) >> 2)) & 3, (my_z + (i & 3)) & 3
                    shard, start, line = at(far_y, z, x, core)
                    here = (i + (skip if array < 3 else 0)) * 208
                    put(source, here, line + 208, 160)

                    @pl.when(line == start + 3 * PIECE)
                    def _():
                        last = jnp.where((x == 1) | (x == 2), 160, 144)
                        edges[1, shard] = source[pl.ds(pl.multiple_of(here + last, 16), 16), :]

                    @pl.when(line != start + 3 * PIECE)
                    def _():
                        put(source, here + 160, line + 368, 48)

                    return 0

                lax.fori_loop(0, 8, second, 0, unroll=4)
        base = pl.multiple_of(rows_of_y * ((my_y + far_y) & 3), 16)
        for shard in range(8):
            x = shard % 4
            tile = real(edges[0, shard])
            if x:
                tile = jnp.where(row < (12 * x) % 16, real(edges[1, shard - 1]), tile)
            whole[pl.ds(pl.multiple_of(base + 16 * ((403 * shard) // 4), 16), 16), :] = low(tile)
        pltpu.make_async_copy(whole.at[pl.ds(base, rows_of_y)], out.at[pl.ds(base, rows_of_y)], sem.at[far_y]).start()
    for far_y in range(4):
        pltpu.make_async_copy(whole.at[pl.ds(0, rows_of_y)], out.at[pl.ds(0, rows_of_y)], sem.at[far_y]).wait()


def unpack(pos, pieces):
    hbm, vmem = pl.BlockSpec(memory_space=pl.ANY), pl.BlockSpec(memory_space=pltpu.VMEM)
    return pl.pallas_call(
        unpack_kernel,
        out_shape=jax.ShapeDtypeStruct((LINES, LANES), jnp.bfloat16),
        in_specs=[pl.BlockSpec(memory_space=pltpu.SMEM)] + [vmem] * 20,
        out_specs=hbm,
        scratch_shapes=[
            pltpu.VMEM((LINES, LANES), jnp.bfloat16),
            pltpu.VMEM((2, 8, 16, LANES), jnp.bfloat16),
            pltpu.SemaphoreType.DMA((4,)),
        ],
        compiler_params=pltpu.CompilerParams(vmem_limit_bytes=48 * 2**20),
        cost_estimate=pl.CostEstimate(flops=0, bytes_accessed=27_000_000, transcendentals=0),
        name="unpack_weights",
    )(pos, *pieces)


def own_update_kernel(where, scales, squares, piece, master, moment_one, moment_two, out):
    start, turn = where[0], where[1]
    total = jnp.sum(squares[...], axis=1, keepdims=True)
    clipped = piece[...] * (MAX_NORM / jnp.maximum(jnp.sqrt(total), MAX_NORM))

    def lines(ref):
        return pltpu.roll(ref[pl.ds(start, PIECE), :], turn, 0)

    out[...] = low(adam_step(clipped, lines(master), lines(moment_one), lines(moment_two), scales[0], scales[1])[2])


def own_update(offset, scales, squares, piece, master, moment_one, moment_two):
    start = jnp.clip(offset, 0, SHARD_LINES - PIECE)
    where = jnp.stack([start, (start - offset + PIECE) % PIECE]).astype(jnp.int32)
    smem, vmem = pl.BlockSpec(memory_space=pltpu.SMEM), pl.BlockSpec(memory_space=pltpu.VMEM)
    return pl.pallas_call(
        own_update_kernel,
        out_shape=jax.ShapeDtypeStruct((PIECE, LANES), jnp.bfloat16),
        in_specs=[smem, smem] + [vmem] * 5,
        out_specs=vmem,
        compiler_params=pltpu.CompilerParams(vmem_limit_bytes=16 * 2**20),
        name="own_update",
    )(where, scales, squares, piece, *[v.reshape(SHARD_LINES, LANES) for v in (master, moment_one, moment_two)])


SPAN = 256
MICRO = 2
GROUPS = 8
ROWS = 256
F32 = jnp.float32


def nt(left, right, precision=None):
    return lax.dot_general(left, right, (((1,), (1,)), ((), ())), precision=precision, preferred_element_type=F32)


def tn(left, right, precision=None):
    return lax.dot_general(left, right, (((0,), (0,)), ((), ())), precision=precision, preferred_element_type=F32)


def nn(left, right, precision=None):
    return lax.dot_general(left, right, (((1,), (0,)), ((), ())), precision=precision, preferred_element_type=F32)


def sigmoid(v):
    return 0.5 + 0.5 * jnp.tanh(0.5 * v)


def iota(shape, dim):
    return lax.broadcasted_iota(jnp.int32, shape, dim)


def shifts(marks, first, length, step, offset):
    parts = []
    for d in range(1, 4):
        hit = iota((length, SPAN), 0) == iota((length, SPAN), 1) + step * d + offset
        parts.append(jnp.where(hit, marks[first + d - 1 : first + d, :], 0.0))
    return low(jnp.concatenate(parts, axis=1))


def by_head(ref, r):
    rows = [jnp.broadcast_to(ref[pl.ds(4 * r + k, 1), :], (HDIM, ref.shape[1])) for k in range(4)]
    return jnp.concatenate(rows, axis=0)


def put_head_sums(ref, r, block):
    for k in range(4):
        ref[pl.ds(4 * r + k, 1), :] = jnp.sum(block[k * HDIM : (k + 1) * HDIM], axis=0, keepdims=True)


def chunk(r):
    return pl.ds(pl.multiple_of(r * ROWS, ROWS), ROWS)


def set_up_kernel(
    place, tokens, segments, gain, kernel, bias, heads, gate_gain, normed, marks, taps, steps, coef, table
):
    x = real(tokens[...])
    factor = lax.rsqrt(jnp.mean(x * x, axis=1, keepdims=True) + EPSILON)
    for t in range(D // LANES):
        part = slice(t * LANES, (t + 1) * LANES)
        normed[:, part] = low(x[:, part] * factor * real(gain[t : t + 1, :]))

    first = place[0] * SPAN
    lane = iota((1, SPAN), 1)
    for m in range(MICRO):
        part = slice(m * SPAN, (m + 1) * SPAN)
        here = segments[m, :, pl.ds(pl.multiple_of(first, SPAN), SPAN)]
        left = segments[m, :, pl.ds(pl.multiple_of(jnp.maximum(first - LANES, 0), LANES), LANES)]
        right = segments[m, :, pl.ds(pl.multiple_of(jnp.minimum(first + SPAN, 3 * SPAN), LANES), LANES)]
        here, left, right = real(here), real(left), real(right)
        left = jnp.where(place[0] > 0, left, -1.0)
        right = jnp.where(place[0] < 3, right, -1.0)
        left, right = jnp.concatenate([left, left], axis=1), jnp.concatenate([right, right], axis=1)
        rows = []
        for d in range(1, 4):
            before = jnp.where(lane < d, pltpu.roll(left, d, 1), pltpu.roll(here, d, 1))
            rows.append(before == here)
        for d in range(1, 4):
            after = pltpu.roll(here, SPAN - d, 1)
            rows.append(jnp.where(lane >= SPAN - d, pltpu.roll(right, SPAN - d, 1), after) == here)
        prior, final = left[:, LANES - 1 : LANES], here[:, SPAN - 1 :]
        rows += [here == prior, here == final, jnp.broadcast_to(final == prior, here.shape)]
        rows = [row.astype(F32) for row in rows] + [here] + [jnp.zeros((1, SPAN), F32)] * 6
        marks[:, part] = jnp.concatenate(rows, axis=0)

    def columns(rows):
        return jnp.transpose(jnp.concatenate(rows + [jnp.zeros((8 - len(rows), LANES), F32)], axis=0))

    for t in range(CH // LANES):
        part = slice(t * LANES, (t + 1) * LANES)
        rows = [real(kernel[k : k + 1, part]) for k in range(4)] + [real(bias[t : t + 1, :])]
        taps[part, :] = columns(rows)
    steps[...] = columns([heads[0:1, :], jnp.exp(heads[1:2, :])])[0:HEADS, :]
    pick = (iota((LANES, DI), 1) >> 6 == iota((LANES, DI), 0)).astype(F32)
    table[...] = nn(jnp.broadcast_to(heads[2:3, :], (8, LANES)), pick, lax.Precision.HIGHEST)
    for t in range(DI // LANES):
        part = slice(t * LANES, (t + 1) * LANES)
        coef[part, :] = columns([real(gate_gain[t : t + 1, :]), table[0:1, part]])


def products_kernel(gate_weight, out_weight, normed, cotangent, gate, grad_mixed):
    gate[...] = nt(gate_weight[...], normed[...])
    grad_mixed[...] = nt(out_weight[...], cotangent[...])


def prepare_kernel(
    weight, step_weight, normed, rim, gain, taps, steps, marks,
    ci, conv, signal, inflow, maps, raw, cum, step, cols, local, through, state, move, enter, edge
):
    r = pl.program_id(0)
    parts = [slice(m * SPAN, (m + 1) * SPAN) for m in range(MICRO)]

    @pl.when(r == 0)
    def _():
        x = real(rim[...])
        factor = lax.rsqrt(jnp.mean(x * x, axis=1, keepdims=True) + EPSILON)
        for t in range(D // LANES):
            part = slice(t * LANES, (t + 1) * LANES)
            edge[:, part] = low(x[:, part] * factor * real(gain[t : t + 1, :]))
        raw[...] = nt(step_weight[...], normed[...])
        step[...] = jax.nn.softplus(raw[...] + steps[:, 0:1])
        upto = (iota((SPAN, SPAN), 0) <= iota((SPAN, SPAN), 1)).astype(F32)
        for m, part in enumerate(parts):
            here = marks[:, part]
            move[m] = shifts(here, 0, SPAN, -1, 0)
            enter[m] = shifts(here, 0, 16, -1, 16)
            decay = -step[:, part] * steps[:, 1:2]
            total = nn(decay, upto, lax.Precision.HIGHEST)
            cum[:, part] = total
            column = lax.dot_general(
                upto, decay, (((0,), (1,)), ((), ())), precision=lax.Precision.HIGHEST, preferred_element_type=F32
            )
            for g in range(GROUPS):
                cols[g, part, :] = column[:, 4 * g : 4 * g + 4]
            ends = total[:, SPAN - 1 :]
            state[:, part] = here[7:8, :] * jnp.exp(ends - total)
            through[m] = jnp.broadcast_to(here[8:9, 0:1] * jnp.exp(ends), (HEADS, LANES))

    x = low(nt(weight[...], normed[...]))
    ci[...] = x
    halo = low(nt(weight[...], edge[...]))
    flows = []
    for m, part in enumerate(parts):
        moved = nn(x[:, part], move[m]) + nn(halo[:, 16 * m : 16 * m + 16], enter[m])
        total = taps[:, 4:5] + real(x[:, part]) * taps[:, 3:4]
        for d in range(1, 4):
            total = total + moved[:, (d - 1) * SPAN : d * SPAN] * taps[:, 3 - d : 4 - d]
        conv[:, part] = total
        flows.append(total * sigmoid(total))

    @pl.when(r == 0)
    def _():
        for flow, part in zip(flows, parts):
            maps[:, part] = flow

    @pl.when(r > 0)
    def _():
        for m, (flow, part) in enumerate(zip(flows, parts)):
            signal[:, part] = flow
            heads = by_head(step, r - 1)[:, part]
            tails = by_head(state, r - 1)[:, part]
            flow = flow * heads
            inflow[:, part] = low(flow)
            local[m] = low(nt(low(flow * tails), low(maps[0:LANES, part])))


def turn_kernel(normed, upstream, left, cot, turned):
    for t in range(4):
        part = slice(t * LANES, (t + 1) * LANES)
        turned[...] = jnp.transpose(real(normed[part, :]))
        for k in range(4):
            left[256 * k : 256 * (k + 1), part] = low(turned[pl.ds(k, 256, stride=4), :])
    cot[...] = low(pltpu.roll(real(upstream[...]), D - 32, 1))


def same_document(marks):
    column = jnp.transpose(jnp.broadcast_to(marks[9:10, :], (8, SPAN)))[:, 0:1]
    return (column == marks[9:10, :]) & (iota((SPAN, SPAN), 0) <= iota((SPAN, SPAN), 1))


def mixing(maps, marks):
    products = tn(maps[0:LANES, :], maps[LANES:, :], lax.Precision.HIGHEST)
    return jnp.where(same_document(marks), products, 0.0)


def within_kernel(inflow, maps, cum, cols, marks, out, table):
    table[...] = mixing(maps, marks)
    half = SPAN // 2

    def heads(g, _):
        results = []
        x4 = inflow[chunk(g), :]
        for h in range(4):
            row, col = cum[pl.ds(4 * g + h, 1), :], cols[g, :, h : h + 1]
            upper = low(jnp.exp(jnp.minimum(row - col[:half], 0.0)) * table[:half, :])
            lower = low(jnp.exp(jnp.minimum(row[:, half:] - col[half:], 0.0)) * table[half:, half:])
            x = x4[h * HDIM : (h + 1) * HDIM, :]
            y = nn(x[:, :half], upper)
            results.append(jnp.concatenate([y[:, :half], y[:, half:] + nn(x[:, half:], lower)], axis=1))
        out[chunk(g), :] = jnp.concatenate(results, axis=0)
        return 0

    lax.fori_loop(0, GROUPS, heads, 0)


def gate_kernel(
    inside, enter, last, maps, signal, gate, grad, cum, marks, coef,
    gated_low, grad_gate, grad_scan, carried_sum, skip_sum, gain_sum, grad_state, grad_read, scan, entry
):
    entry[...] = marks[6:7, :] * jnp.exp(cum[...])
    reads = low(maps[LANES:, :])

    @pl.when(pl.program_id(0) == 0)
    def _():
        gain_sum[...] = jnp.zeros_like(gain_sum)

    def forward(r, sums):
        carried = nn(enter[0, chunk(r), :] + last[0, chunk(r), :], reads) * by_head(entry, r)
        total = inside[chunk(r), :] + carried + coef[chunk(r), 1:2] * signal[chunk(r), :]
        scan[chunk(r), :] = total
        z = gate[chunk(r), :]
        gated = total * (z * sigmoid(z))
        up = grad[chunk(r), :] * coef[chunk(r), 0:1]
        squares, cross = sums
        return (
            squares + jnp.sum(gated * gated, axis=0, keepdims=True),
            cross + jnp.sum(gated * up, axis=0, keepdims=True),
        )

    nothing = jnp.zeros((1, SPAN), F32)
    squares, cross = lax.fori_loop(0, 8, forward, (nothing, nothing))
    factor = lax.rsqrt(squares * (1.0 / DI) + EPSILON)
    pull = factor * factor * cross * (1.0 / DI)
    grad_read[...] = jnp.zeros_like(grad_read)

    def backward(r, _):
        heads = by_head(entry, r)
        state = enter[0, chunk(r), :] + last[0, chunk(r), :]
        carried = nn(state, reads) * heads
        total = scan[chunk(r), :]
        z = gate[chunk(r), :]
        sig = sigmoid(z)
        soft = z * sig
        gated = total * soft
        scaled = gated * factor
        gain = coef[chunk(r), 0:1]
        given = grad[chunk(r), :]
        gated_low[chunk(r), :] = low(scaled * gain)
        share = given * scaled
        gain_sum[chunk(r), :] += share[:, :LANES] + share[:, LANES:]
        back = factor * (given * gain - gated * pull)
        grad_gate[chunk(r), :] = low(back * total * (sig * (1.0 + z * (1.0 - sig))))
        push = back * soft
        grad_scan[chunk(r), :] = push
        put_head_sums(carried_sum, r, push * carried)
        put_head_sums(skip_sum, r, push * signal[chunk(r), :])
        entering = low(push * heads)
        grad_state[0, chunk(r), :] = low(nt(entering, reads))
        grad_read[...] += tn(state, entering)
        return 0

    lax.fori_loop(0, 8, backward, 0)


def within_back_kernel(
    inflow, push, inside, maps, cum, cols, marks, grad_inflow, decay_sum, grad_maps, table, grad_table
):
    table[...] = mixing(maps, marks)
    grad_table[...] = jnp.zeros_like(grad_table)
    half = SPAN // 2

    def heads(g, _):
        x4, d4, results = inflow[chunk(g), :], low(push[chunk(g), :]), []
        above, below = 0.0, 0.0
        for h in range(4):
            rows = slice(h * HDIM, (h + 1) * HDIM)
            row, col = cum[pl.ds(4 * g + h, 1), :], cols[g, :, h : h + 1]
            upper = jnp.exp(jnp.minimum(row - col[:half], 0.0))
            lower = jnp.exp(jnp.minimum(row[:, half:] - col[half:], 0.0))
            x, d = x4[rows, :], d4[rows, :]
            above += upper * tn(x[:, :half], d)
            below += lower * tn(x[:, half:], d[:, half:])
            first = nt(d, low(upper * table[:half, :]))
            second = nt(d[:, half:], low(lower * table[half:, half:]))
            results.append(jnp.concatenate([first, second], axis=1))
        grad_table[:half, :] += above
        grad_table[half:, half:] += below
        back = jnp.concatenate(results, axis=0)
        grad_inflow[chunk(g), :] = back
        put_head_sums(decay_sum, g, real(d4) * inside[chunk(g), :] - real(x4) * back)
        return 0

    lax.fori_loop(0, GROUPS, heads, 0)
    spread = low(jnp.where(same_document(marks), grad_table[...], 0.0))
    grad_maps[0:LANES, :] = nt(low(maps[LANES:, :]), spread)
    grad_maps[LANES:, :] = nn(low(maps[0:LANES, :]), spread)


def state_back_kernel(
    leave, leave_last, enter, enter_last, conv, push, grad_inflow, maps, cum, step, raw, decay_sum, carried_sum, grad_maps, grad_read,
    steps, marks, coef, grad_conv, rim, grad_raw, bias_sum, rate_sum, tail, from_tail, from_step, crossing, grad_write
):
    ends = cum[:, SPAN - 1 : SPAN]
    tail[...] = marks[7:8, :] * jnp.exp(ends - cum[...])
    writes = low(maps[0:LANES, :])
    front = ((iota((16, SPAN), 1) == iota((16, SPAN), 0)) & (iota((16, SPAN), 0) < 3)).astype(jnp.bfloat16)
    grad_write[...] = grad_maps[0:LANES, :]

    def through_silu(r, c, sig, above):
        given = above * (sig * (1.0 + c * (1.0 - sig)))
        grad_conv[chunk(r), :] = given
        rim[0, :, chunk(r)] = low(nt(front, low(given)))

    def channels(r, _):
        c = conv[chunk(r), :]
        sig = sigmoid(c)
        signal = c * sig
        heads, tails = by_head(step, r), by_head(tail, r)
        x = signal * heads
        back = leave[0, chunk(r), :] + leave_last[0, chunk(r), :]
        ended = nn(back, writes) * tails
        whole = grad_inflow[chunk(r), :] + ended
        grad_write[...] += tn(back, low(x * tails))
        put_head_sums(from_tail, r, x * ended)
        put_head_sums(from_step, r, whole * signal)
        put_head_sums(crossing, r, real(back) * real(enter[0, chunk(r), :] + enter_last[0, chunk(r), :]))
        through_silu(r, c, sig, whole * heads + coef[chunk(r), 1:2] * push[chunk(r), :])
        return 0

    lax.fori_loop(0, 8, channels, 0)
    c = conv[chunk(8), :]
    through_silu(8, c, sigmoid(c), jnp.concatenate([grad_write[...], grad_maps[LANES:, :] + grad_read[...]], axis=0))
    last = iota((HEADS, SPAN), 1) == SPAN - 1
    passing = marks[8:9, 0:1] * jnp.exp(ends) * jnp.sum(crossing[...], axis=1, keepdims=True)
    tails = jnp.sum(from_tail[...], axis=1, keepdims=True)
    total = decay_sum[...] + carried_sum[...] - from_tail[...] + jnp.where(last, tails + passing, 0.0)
    onward = (iota((SPAN, SPAN), 0) >= iota((SPAN, SPAN), 1)).astype(F32)
    grad_decay = nn(total, onward, lax.Precision.HIGHEST)
    rate = steps[:, 1:2]
    rate_sum[...] = -grad_decay * step[...] * rate
    grad_step = (from_step[...] - grad_decay * rate) * sigmoid(raw[...] + steps[:, 0:1])
    bias_sum[...] = grad_step
    grad_raw[0:HEADS, :] = low(grad_step)
    grad_raw[HEADS:, :] = jnp.zeros((LANES - HEADS, SPAN), jnp.bfloat16)


def conv_back_kernel(grad_conv, ci, rim, taps, marks, grad_ci, sums, move, enter):
    @pl.when(pl.program_id(0) == 0)
    def _():
        for m in range(MICRO):
            here = marks[:, m * SPAN : (m + 1) * SPAN]
            move[m] = shifts(here, 3, SPAN, 1, 0)
            enter[m] = shifts(here, 3, 16, 1, -SPAN) * (iota((16, 3 * SPAN), 0) < 3).astype(jnp.bfloat16)

    totals = [0.0] * 5
    for m in range(MICRO):
        part = slice(m * SPAN, (m + 1) * SPAN)
        given, x = grad_conv[:, part], real(ci[:, part])
        moved = nn(low(given), move[m]) + tn(rim[m], enter[m])
        back = given * taps[:, 3:4]
        totals[3] += given * x
        totals[4] += given
        for d in range(1, 4):
            sooner = moved[:, (d - 1) * SPAN : d * SPAN]
            back += sooner * taps[:, 3 - d : 4 - d]
            totals[3 - d] += sooner * x
        grad_ci[:, part] = low(back)
    count = jnp.zeros((ROWS, LANES), F32)
    for k in range(5):
        pick = (iota((SPAN, LANES), 1) == k).astype(jnp.bfloat16)
        count += nn(low(totals[k]), pick)
    sums[...] = count[:, 0:8]


def call(kernel, grid, ins, outs, scratch, cost, name, mebibytes):
    return pl.pallas_call(
        kernel,
        grid=grid,
        in_specs=[pl.BlockSpec(block, where) for _, block, where in ins],
        out_specs=[pl.BlockSpec(block, where) for _, _, block, where in outs],
        out_shape=[jax.ShapeDtypeStruct(shape, dtype) for shape, dtype, _, _ in outs],
        scratch_shapes=scratch,
        compiler_params=pltpu.CompilerParams(
            vmem_limit_bytes=mebibytes * 2**20, dimension_semantics=("arbitrary",) * len(grid)
        ),
        cost_estimate=pl.CostEstimate(flops=cost, bytes_accessed=20_000_000, transcendentals=0),
        name=name,
    )(*[array for array, _, _ in ins])


def neighbours(value, source, target):
    return lax.ppermute(value, GROUP, [(source, target)])


def chained(local, through, order, beside):
    by_heads = (MICRO, HEADS, HDIM, STATE)

    def joined(arrived):
        total = through[:, :, None, :] * real(arrived).reshape(by_heads) + real(local).reshape(by_heads)
        return low(total).reshape(local.shape)

    one = neighbours(local, order[0], order[1])
    two = neighbours(joined(one), order[1], order[2])
    two, beside = lax.optimization_barrier((two, beside))
    three = neighbours(joined(two), order[2], order[3])
    return (one + two, three), beside


def shards(
    tokens, segments, cotangent, norm_gain, in_weight, conv_kernel, conv_bias, step_bias, decay_log,
    skip_gain, gate_gain, out_weight, master, moment_one, moment_two, step_count
):
    width = MICRO * SPAN
    bf16 = jnp.bfloat16
    spot = position()
    place = lax.axis_index(GROUP)
    one = (MICRO,)
    by_m = lambda m: (0, m)
    whole, first = lambda m: (0, 0), lambda m: (m, 0, 0)
    upstream = cotangent.reshape(width, D)
    turned_weight = in_weight.T
    conv_weight = turned_weight[DI : DI + CH]

    heads = jnp.stack([real(step_bias), real(decay_log), real(skip_gain)])
    heads = jnp.pad(heads, ((0, 5), (0, LANES - HEADS)))
    lines = [v.reshape(-1, LANES) for v in (norm_gain, conv_bias, gate_gain)]
    ins = [tokens.reshape(width, D), segments, lines[0], conv_kernel, lines[1], heads, lines[2]]
    outs = [((width, D), bf16), ((16, width), F32), ((CH, 8), F32), ((HEADS, 8), F32), ((DI, 8), F32)]
    at_start = lambda rank: lambda i: (0,) * rank
    normed_low, marks, taps, steps, coef = pl.pallas_call(
        set_up_kernel,
        grid=(1,),
        out_shape=[jax.ShapeDtypeStruct(*out) for out in outs],
        in_specs=[pl.BlockSpec(memory_space=pltpu.SMEM)] + [pl.BlockSpec(v.shape, at_start(v.ndim)) for v in ins],
        out_specs=[pl.BlockSpec(shape, at_start(len(shape))) for shape, _ in outs],
        scratch_shapes=[pltpu.VMEM((8, DI), F32)],
        compiler_params=pltpu.CompilerParams(vmem_limit_bytes=56 * 2**20),
        name="set_up",
    )(place.reshape(1), *ins)
    mark_in = (marks, (16, SPAN), by_m)
    rim_tokens, normed_low = lax.optimization_barrier((tokens[:, 0, SPAN - 16 :, :], normed_low))
    rim_tokens = lax.ppermute(rim_tokens, GROUP, [(0, 1), (1, 2), (2, 3)])

    whole1, head_rows = lambda r: (0, 0), lambda r: (jnp.maximum(r - 1, 0), 0)
    rows_of = lambda r: jnp.where(r == 0, GROUPS, r - 1)
    by_rows = lambda r: (rows_of(r), 0)
    lot = (HEADS, width)
    ci, conv, signal, inflow, maps, raw, cum, step, cols, local, through = call(
        prepare_kernel, (CH // ROWS,),
        [(turned_weight, (ROWS, D), lambda r: (GROUPS + rows_of(r), 0)),
         (turned_weight, (HEADS, D), lambda r: ((DI + CH) // HEADS, 0)), (normed_low, (width, D), whole1),
         (rim_tokens.reshape(-1, D), (32, D), whole1), (lines[0], lines[0].shape, whole1), (taps, (ROWS, 8), by_rows), (steps, (HEADS, 8), whole1),
         (marks, (16, width), whole1)],
        [((CH, width), bf16, (ROWS, width), by_rows), ((CH, width), F32, (ROWS, width), by_rows),
         ((DI, width), F32, (ROWS, width), head_rows), ((DI, width), bf16, (ROWS, width), head_rows),
         ((2 * STATE, width), F32, (2 * STATE, width), whole1), (lot, F32, lot, whole1), (lot, F32, lot, whole1),
         (lot, F32, lot, whole1), ((GROUPS, width, 4), F32, (GROUPS, width, 4), lambda r: (0, 0, 0)),
         ((MICRO, DI, STATE), bf16, (MICRO, ROWS, STATE), lambda r: (0, jnp.maximum(r - 1, 0), 0)),
         ((MICRO, HEADS, LANES), F32, (MICRO, HEADS, LANES), lambda r: (0, 0, 0))],
        [pltpu.VMEM(lot, F32), pltpu.VMEM((MICRO, SPAN, 3 * SPAN), bf16), pltpu.VMEM((MICRO, 16, 3 * SPAN), bf16),
         pltpu.VMEM((32, D), bf16)],
        10**9, "project_and_convolve", 56,
    )

    tiles = lambda r: (r, 0)
    gate, grad_mixed = call(
        products_kernel, (GROUPS // 2,),
        [(turned_weight, (2 * ROWS, D), tiles), (out_weight, (2 * ROWS, D), tiles), (normed_low, (width, D), whole1),
         (upstream, (width, D), whole1)],
        [((DI, width), F32, (2 * ROWS, width), tiles)] * 2, [], 4 * 10**9, "gate_products", 24,
    )
    tall, few = (DI, SPAN), (HEADS, SPAN)
    state_block = (1, DI, STATE)
    head_ins = [
        (maps, (2 * STATE, SPAN), by_m),
        (cum, few, by_m),
        (cols, (GROUPS, SPAN, 4), lambda m: (0, m, 0)),
        mark_in,
    ]
    table = pltpu.VMEM((SPAN, SPAN), F32)
    (inside,) = call(
        within_kernel, one, [(inflow, tall, by_m)] + head_ins, [((DI, width), F32, tall, by_m)], [table],
        4 * 10**9, "within_blocks", 24,
    )
    enter, (inside, gate, grad_mixed) = chained(local, through, (0, 1, 2, 3), (inside, gate, grad_mixed))

    gated_low, grad_gate, push, carried_sum, skip_sum, gain_sum, grad_state, grad_read = call(
        gate_kernel, one,
        [(inside, tall, by_m), (enter[0], state_block, first), (enter[1], state_block, first), (maps, (2 * STATE, SPAN), by_m), (signal, tall, by_m),
         (gate, tall, by_m), (grad_mixed, tall, by_m), (cum, (HEADS, SPAN), by_m), mark_in, (coef, (DI, 8), whole)],
        [((DI, width), bf16, tall, by_m), ((DI, width), bf16, tall, by_m), ((DI, width), F32, tall, by_m),
         ((HEADS, width), F32, (HEADS, SPAN), by_m), ((HEADS, width), F32, (HEADS, SPAN), by_m),
         ((DI, LANES), F32, (DI, LANES), whole), ((MICRO, DI, STATE), bf16, state_block, first),
         ((STATE, width), F32, (STATE, SPAN), by_m)],
        [pltpu.VMEM((DI, SPAN), F32), pltpu.VMEM((HEADS, SPAN), F32)], 2 * 10**9, "gate_and_back", 50,
    )
    grad_inflow, decay_sum, grad_maps = call(
        within_back_kernel, one, [(inflow, tall, by_m), (push, tall, by_m), (inside, tall, by_m)] + head_ins,
        [((DI, width), F32, tall, by_m), ((HEADS, width), F32, few, by_m),
         ((2 * STATE, width), F32, (2 * STATE, SPAN), by_m)],
        [table, table], 8 * 10**9, "within_blocks_back", 56,
    )
    left, cot = call(
        turn_kernel, (1,), [(normed_low, (width, D), whole), (upstream, (width, D), whole)],
        [((D, width), bf16, (D, width), whole), ((width, D), bf16, (width, D), whole)],
        [pltpu.VMEM((D, LANES), F32)], 10**6, "turn", 14,
    )
    leave, (grad_inflow, decay_sum, grad_maps, left, cot) = chained(
        grad_state, through, (3, 2, 1, 0), (grad_inflow, decay_sum, grad_maps, left, cot)
    )

    grad_conv, rim, grad_raw, bias_sum, rate_sum = call(
        state_back_kernel, one,
        [(leave[0], state_block, first), (leave[1], state_block, first), (enter[0], state_block, first),
         (enter[1], state_block, first), (conv, (CH, SPAN), by_m), (push, tall, by_m),
         (grad_inflow, tall, by_m), (maps, (2 * STATE, SPAN), by_m), (cum, few, by_m), (step, few, by_m), (raw, few, by_m),
         (decay_sum, few, by_m), (carried_sum, few, by_m), (grad_maps, (2 * STATE, SPAN), by_m),
         (grad_read, (STATE, SPAN), by_m), (steps, (HEADS, 8), whole), mark_in, (coef, (DI, 8), whole)],
        [((CH, width), F32, (CH, SPAN), by_m), ((MICRO, 16, CH), bf16, (1, 16, CH), first),
         ((LANES, width), bf16, (LANES, SPAN), by_m), ((HEADS, width), F32, few, by_m), ((HEADS, width), F32, few, by_m)],
        [pltpu.VMEM(few, F32), pltpu.VMEM(few, F32), pltpu.VMEM(few, F32), pltpu.VMEM((HEADS, LANES), F32),
         pltpu.VMEM((STATE, SPAN), F32)], 10**9, "state_and_silu_back", 56,
    )
    next_rim = lax.ppermute(rim, GROUP, [(1, 0), (2, 1), (3, 2)])
    early = tn(grad_gate, turned_weight[:DI])
    next_rim, early = lax.optimization_barrier((next_rim, early))

    by_r = lambda r: (r, 0)
    grad_ci, tap_sums = call(
        conv_back_kernel, (CH // ROWS,),
        [(grad_conv, (ROWS, width), by_r), (ci, (ROWS, width), by_r), (next_rim, (MICRO, 16, ROWS), lambda r: (0, 0, r)),
         (taps, (ROWS, 8), by_r), (marks, (16, width), lambda r: (0, 0))],
        [((CH, width), bf16, (ROWS, width), by_r), ((CH, 8), F32, (ROWS, 8), by_r)],
        [pltpu.VMEM((MICRO, SPAN, 3 * SPAN), bf16), pltpu.VMEM((MICRO, 16, 3 * SPAN), bf16)], 10**8, "convolution_back", 56,
    )

    middle = [tap_sums[:, :5].T.reshape(-1), jnp.sum(bias_sum, axis=1), jnp.sum(rate_sum, axis=1)]
    middle += [jnp.sum(skip_sum, axis=1), jnp.sum(gain_sum, axis=1), jnp.zeros((32 + 5 * LANES,), F32)]
    middle = jnp.concatenate(middle).reshape(-1, LANES)
    packed = pack(spot, left, grad_gate, grad_ci, grad_raw, gated_low, cot, middle)
    packed, late = lax.optimization_barrier((packed, (grad_gate, grad_ci, grad_raw)))
    rows_in = real(tokens.reshape(width, D))
    norm_back = jax.vjp(norm_piece, rows_in, real(norm_gain))[1]
    grad_normed = early + tn(late[1], conv_weight) + tn(late[2][:HEADS], turned_weight[DI + CH :])
    grad_rows, grad_norm_gain = norm_back(grad_normed)

    def finish(inputs):
        gated_low, grad_rows = inputs
        output = low(rows_in + tn(gated_low, out_weight)).reshape(tokens.shape)
        return output, low(real(upstream) + grad_rows).reshape(tokens.shape)

    piece, (output, input_grad) = reduce_pieces(
        packed[:2], packed[2:], grad_norm_gain.reshape(-1, LANES), finish, (gated_low, grad_rows)
    )

    skew = (12 * lax.axis_index("x")) % 16
    offset = PIECE * place - skew
    line = offset + iota((PIECE, 1), 0)
    own = jnp.where((line >= 0) & (line < SHARD_LINES), piece, 0.0)
    squares = sent_to_all(jnp.sum(own * own).reshape(1, 1), EVERY).reshape(1, -1)
    core, high = lax.axis_index("core") == 0, lax.axis_index("zh") == 0
    pair = [piece, swap_cores(piece)]
    pair = jnp.concatenate([jnp.where(core, *pair), jnp.where(core, *pair[::-1])])
    both = [pair, lax.ppermute(pair, "zh", [(0, 1), (1, 0)])]
    step_real = real(step_count[0])
    scales = jnp.stack([1.0 / (1.0 - jnp.power(BETA_ONE, step_real)), 1.0 / (1.0 - jnp.power(BETA_TWO, step_real))])
    both, squares = lax.optimization_barrier((both, squares))
    mine = own_update(offset, scales, squares, piece, master, moment_one, moment_two)

    def rest(inputs):
        both, squares, moments = inputs
        window = jnp.concatenate([jnp.where(high, *both), jnp.where(high, *both[::-1])])
        shard = lax.dynamic_slice(window, (skew, 0), (SHARD_LINES, LANES)).reshape(-1)
        clip_factor = MAX_NORM / jnp.maximum(jnp.sqrt(jnp.sum(squares)), MAX_NORM)
        return shard, adam_step(shard * clip_factor, *moments, scales[0], scales[1])

    moments = (master, moment_one, moment_two)
    pieces, (shard, results) = gather_pieces(mine, rest, (both, squares, moments))
    copies = unpack(spot, pieces).reshape(-1)
    return (output, input_grad, shard, *results, copies)


def solution(mesh):
    finer = Mesh(mesh.devices.reshape(4, 2, 4, 2, 2), ("y", "zl", "x", "zh", "core"))
    return jax.shard_map(
        shards,
        mesh=finer,
        in_specs=(
            P(None, DP, GROUP, None),
            P(None, DP, None),
            P(None, DP, GROUP, None),
            P(),
            P(),
            P(),
            P(),
            P(),
            P(),
            P(),
            P(),
            P(),
            P(DP),
            P(DP),
            P(DP),
            P(),
        ),
        out_specs=(
            P(None, DP, GROUP, None),
            P(None, DP, GROUP, None),
            P(DP),
            P(DP),
            P(DP),
            P(DP),
            P(),
        ),
        check_vma=False,
    )
```

```python
import functools

import jax
import jax.numpy as jnp
from jax import lax
from jax.experimental import pallas as pl
from jax.experimental.pallas import tpu as pltpu
from jax.sharding import Mesh
from jax.sharding import PartitionSpec as P

D = 1024
DI = 2048
HEADS = 32
HDIM = 64
STATE = 128
CH = 2304
DP = ("y", "zl", "x")
GROUP = ("zh", "core")
EVERY = DP + GROUP


EPSILON = 1e-05
BETA_ONE = 0.9
BETA_TWO = 0.95
ADAM_EPSILON = 1e-08
LEARN_RATE = 0.01
WEIGHT_DECAY = 0.1
MAX_NORM = 1.0


def sent_to_all(shard, axis):
    copies = jnp.broadcast_to(shard, (lax.axis_size(axis), *shard.shape))
    return lax.all_to_all(copies, axis, split_axis=0, concat_axis=0, tiled=True)


def norm_piece(values, scaling):
    factor = lax.rsqrt(jnp.mean(values * values, axis=-1, keepdims=True) + EPSILON)
    return values * factor * scaling


def adam_step(clipped, master, moment_one, moment_two, first_scale, second_scale):
    first_moment = BETA_ONE * moment_one + (1.0 - BETA_ONE) * clipped
    second_moment = BETA_TWO * moment_two + (1.0 - BETA_TWO) * clipped * clipped
    first_hat, second_hat = first_moment * first_scale, second_moment * second_scale
    updated = master - LEARN_RATE * (first_hat / (jnp.sqrt(second_hat) + ADAM_EPSILON) + WEIGHT_DECAY * master)
    return (first_moment, second_moment, updated)


LANES = 128
LINES = 51584
SHARD_LINES = 1612
IN_LINE = 8
MID_LINE = 35080
OUT_LINE = 35187
PIECE = 416
SLOTS = 16
PARTS = ((0, 208), (208, 208))
TAIL_LINES = 51632
GROUP_LINES = 137
RING = {"x": ("x",), "y": ("y",), "z": ("zl", "zh")}
ROUTES = (("x", "y", "z"), ("y", "x", "z"))


def ring_place(axis, i):
    i = i % 4
    return (i % 2) * 2 + i // 2 if axis == "z" else i


def from_offset(block, axis, distance):
    route = [(ring_place(axis, i + distance), ring_place(axis, i)) for i in range(4)]
    return lax.ppermute(block, RING[axis], route)


def swap_cores(block):
    return lax.ppermute(block, "core", [(0, 1), (1, 0)])


def position():
    z = 2 * lax.axis_index("zh") + lax.axis_index("zl")
    return jnp.stack([lax.axis_index("y"), z, lax.axis_index("x"), lax.axis_index("core")]).astype(jnp.int32)


def first_tile(shard):
    return (403 * shard) >> 2


def pack_kernel(pos, mid_part, *rest):
    sources, keep, send = rest[:6], rest[6], rest[7]
    flat, carry, edge, stage, sems = rest[8:13]
    left, grad_gate, grad_ci, grad_raw, gated, cot = held = rest[13:19]
    loads = [pltpu.make_async_copy(source, here, rest[19].at[k]) for k, (source, here) in enumerate(zip(sources, held))]
    for k in (4, 5, 0, 1, 2, 3):
        loads[k].start()
    lane = lax.broadcasted_iota(jnp.int32, (256, LANES), 1)

    flat[0:IN_LINE, :] = jnp.zeros((IN_LINE, LANES), jnp.float32)
    flat[MID_LINE : MID_LINE + 104, :] = mid_part[0:104, :]
    flat[MID_LINE + 104 : MID_LINE + 107, :] = mid_part[104:107, :]
    edge[0:8, :] = mid_part[99:107, :]

    def rows(b, _):
        block = gated[pl.ds(pl.multiple_of(b * 256, 256), 256), :]
        product = jnp.dot(block, cot[...], preferred_element_type=jnp.float32)
        start = OUT_LINE + 2048 * b
        for t in range(7):
            flat[pl.ds(start + t, 256, stride=8), :] = product[:, t * LANES : (t + 1) * LANES]
        last = product[:, 7 * LANES :]
        edge[8:264, :] = last
        flat[pl.ds(start - 1, 256, stride=8), :] = jnp.where(lane < 96, edge[7:263, :], last)
        edge[0:8, :] = edge[256:264, :]
        return 0

    loads[4].wait()
    loads[5].wait()
    lax.fori_loop(0, 8, rows, 0)
    low = lax.broadcasted_iota(jnp.int32, (1, LANES), 1) < 96
    flat[OUT_LINE + 16383 : TAIL_LINES, :] = jnp.zeros((TAIL_LINES - OUT_LINE - 16383, LANES), jnp.float32)
    flat[OUT_LINE + 16383 : OUT_LINE + 16384, :] = jnp.where(low, edge[7:8, :], 0.0)

    my_y, my_z, my_x, my_core = pos[0], pos[1], pos[2], pos[3]

    def drain(slot):
        pltpu.make_async_copy(stage.at[slot], keep.at[pl.ds(0, PIECE)], sems.at[slot]).wait()

    def ship(n, _):
        i = (n + 88) & 127
        slot = n & (SLOTS - 1)

        @pl.when(n >= SLOTS)
        def _():
            drain(slot)

        shard, quarter = i >> 2, i & 3
        line = 16 * first_tile(shard) + PIECE * quarter
        stage[slot] = flat[pl.ds(pl.multiple_of(line, 16), PIECE), :].astype(jnp.bfloat16)
        x, zl, y = shard & 3, (shard >> 2) & 1, shard >> 3
        core = quarter & 1
        z = 2 * (quarter >> 1) + zl
        off = {"y": (y - my_y) & 3, "z": (z - my_z) & 3, "x": (x - my_x) & 3}
        for p, (start, size) in enumerate(PARTS):
            a, b, c = (off[axis] for axis in ROUTES[p])
            to = pl.ds(pl.multiple_of((((4 * p + a) * 4 + b) * 4 + c) * size, 16), size)
            source = stage.at[slot, pl.ds(start, size)]

            @pl.when(core == my_core)
            def _():
                pltpu.make_async_copy(source, keep.at[to], sems.at[slot]).start()

            @pl.when(core != my_core)
            def _():
                pltpu.make_async_copy(source, send.at[to], sems.at[slot]).start()

        return 0

    lax.fori_loop(0, 40, ship, 0)

    def put(tile, k, line):
        moved = pltpu.roll(tile, 32 * k, 1) if k else tile
        whole = jnp.where(lane < 32 * k, carry[k], moved) if k else moved
        flat[pl.ds(IN_LINE + 34 * k + line, 256, stride=GROUP_LINES), :] = whole
        carry[k] = moved

    def columns(block, line, tiles):
        product = nt(left[...], block)
        for k in range(4):
            for t in range(tiles):
                put(product[256 * k : 256 * (k + 1), t * LANES : (t + 1) * LANES], k, line + t)

    def from_gate(j, _):
        columns(grad_gate[pl.ds(pl.multiple_of(j * 512, 512), 512), :], 4 * j, 4)
        return 0

    def from_conv(j, _):
        columns(grad_ci[pl.ds(pl.multiple_of(j * 512, 512), 512), :], 16 + 4 * j, 4)
        return 0

    loads[0].wait()
    loads[1].wait()
    lax.fori_loop(0, 4, from_gate, 0)
    loads[2].wait()
    loads[3].wait()
    lax.fori_loop(0, 4, from_conv, 0)
    heads = []
    for k in range(1, 4):
        heads.append(flat[pl.ds(IN_LINE + 34 * k, 256, stride=GROUP_LINES), :])
    columns(jnp.concatenate([grad_ci[2048:2304, :], grad_raw[...]], axis=0), 32, 3)
    for k in range(1, 4):
        at = pl.ds(IN_LINE + 34 * k, 256, stride=GROUP_LINES)
        flat[at, :] = jnp.where(lane < 32 * k, flat[at, :], heads[k - 1])

    lax.fori_loop(40, 128, ship, 0)
    for slot in range(SLOTS):
        drain(slot)


def pack(pos, left, grad_gate, grad_ci, grad_raw, gated, cot, mid_part):
    vmem, hbm = pl.BlockSpec(memory_space=pltpu.VMEM), pl.BlockSpec(memory_space=pl.ANY)
    shape = jax.ShapeDtypeStruct((64 * PIECE, LANES), jnp.bfloat16)
    return pl.pallas_call(
        pack_kernel,
        out_shape=[shape] * 2,
        in_specs=[pl.BlockSpec(memory_space=pltpu.SMEM)] + [vmem] + [hbm] * 6,
        out_specs=[hbm] * 2,
        scratch_shapes=[
            pltpu.VMEM((TAIL_LINES, LANES), jnp.float32),
            pltpu.VMEM((4, 256, LANES), jnp.float32),
            pltpu.VMEM((264, LANES), jnp.float32),
            pltpu.VMEM((SLOTS, PIECE, LANES), jnp.bfloat16),
            pltpu.SemaphoreType.DMA((SLOTS,)),
        ]
        + [pltpu.VMEM(v.shape, v.dtype) for v in (left, grad_gate, grad_ci, grad_raw, gated, cot)]
        + [pltpu.SemaphoreType.DMA((6,))],
        compiler_params=pltpu.CompilerParams(vmem_limit_bytes=60 * 2**20),
        cost_estimate=pl.CostEstimate(flops=7_000_000_000, bytes_accessed=25_000_000, transcendentals=0),
        name="pack_gradients",
    )(pos, mid_part, left, grad_gate, grad_ci, grad_raw, gated, cot)


def real(v):
    return v.astype(jnp.float32)


def low(v):
    return v.astype(jnp.bfloat16)


def to_offset(block, axis, distance):
    route = [(ring_place(axis, i), ring_place(axis, i + distance)) for i in range(4)]
    return lax.ppermute(block, RING[axis], route)


def quarters(block):
    return block.reshape(4, -1, LANES)


def ring_sum(block, axis):
    block = quarters(block)
    half = block.shape[1] // 32 * 16
    a, b = to_offset(block[2, :half], axis, 1), to_offset(block[2, half:], axis, 3)
    one = jnp.concatenate([low(real(block[1, :half]) + real(a)), block[1, half:]])
    three = jnp.concatenate([block[3, :half], low(real(block[3, half:]) + real(b))])
    return real(block[0]) + real(to_offset(one, axis, 1)) + real(to_offset(three, axis, 3))


def direct_sum(block, axis):
    block = quarters(block)
    moved = [to_offset(block[d], axis, d) for d in (1, 3, 2)]
    return real(block[0]) + real(moved[0]) + real(moved[1]) + real(moved[2])


def reduce_pieces(keep, send, gain_grad, beside, given):
    send, _ = lax.optimization_barrier((send, swap_cores(send[:16])))
    got = swap_cores(send)
    held = [low(real(mine) + real(other)) for mine, other in zip(jnp.split(keep, 2), jnp.split(got, 2))]
    gain_grad = low(gain_grad + swap_cores(gain_grad))
    x, y, z = lax.axis_index("x"), lax.axis_index("y"), 2 * lax.axis_index("zh") + lax.axis_index("zl")
    block = 16 * (-x & 3) + 4 * (-y & 3) + (-z & 3)
    lines = jnp.arange(16)[:, None]
    mine = (lines < IN_LINE) & (lax.axis_index("core") == 0)
    start = (block * PARTS[0][1], 0)
    tile = lax.dynamic_slice(held[0], start, (16, LANES))
    tile = jnp.where(mine, jnp.pad(gain_grad, ((0, 16 - IN_LINE), (0, 0))), tile)
    held[0] = lax.dynamic_update_slice(held[0], tile, start)
    held, given = lax.optimization_barrier((held, given))
    first, second = low(ring_sum(held[0], "x")), low(ring_sum(held[1], "y"))
    (first, second), done = lax.optimization_barrier(((first, second), beside(given)))
    first, second = low(direct_sum(first, "y")), low(direct_sum(second, "x"))
    both = jnp.concatenate([quarters(first), quarters(second)], axis=1).reshape(-1, LANES)
    return direct_sum(both, "z"), done


def join_kernel(*refs):
    *blocks, first, second = refs
    for out, parts in ((first, blocks[: len(blocks) // 2]), (second, blocks[len(blocks) // 2 :])):
        start = 0
        for block in parts:
            out[start : start + block.shape[0], :] = block[...]
            start += block.shape[0]


def join(first, second):
    vmem = pl.BlockSpec(memory_space=pltpu.VMEM)
    rows = [sum(block.shape[0] for block in parts) for parts in (first, second)]
    return pl.pallas_call(
        join_kernel,
        out_shape=[jax.ShapeDtypeStruct((n, LANES), jnp.bfloat16) for n in rows],
        in_specs=[vmem] * (len(first) + len(second)),
        out_specs=[vmem] * 2,
        compiler_params=pltpu.CompilerParams(vmem_limit_bytes=8 * 2**20),
        name="join",
    )(*first, *second)


def gather_pieces(piece, beside, given):
    def spread(block, axis):
        return [block] + [from_offset(block, axis, d) for d in (1, 3, 2)]

    def in_order(parts):
        return [parts[0], parts[1], parts[3], parts[2]]

    n = PARTS[0][1]
    both = spread(piece, "z")
    both = in_order(both)
    first = spread(jnp.concatenate([block[:n] for block in both]), "y")
    second = spread(jnp.concatenate([block[n:] for block in both]), "x")
    first, second = join(in_order(first), in_order(second))
    ends = [(first, "x"), (second, "y")]
    sides = [[from_offset(block, axis, d) for d in (1, 3)] for block, axis in ends]
    swapped = [swap_cores(block) for block, _ in ends]
    swapped, given = lax.optimization_barrier((swapped, given))
    sides, swapped, done = lax.optimization_barrier((sides, swapped, beside(given)))
    mine, other = [], []
    for (block, axis), (left, right), first in zip(ends, sides, swapped):
        half = block.shape[0] // 2
        halves = [from_offset(right[:half], axis, 3), from_offset(left[half:], axis, 1)]
        mine += [block, left, right, *halves]
        left, right, halves = lax.optimization_barrier((left, right, halves))
        other += [first] + [swap_cores(part) for part in (left, right, *halves)]
    return mine + other, done


def unpack_kernel(pos, *rest):
    sources, out = rest[:20], rest[20]
    whole, edges, sem = rest[21:]
    my_y, my_z, my_x, my_core = pos[0], pos[1], pos[2], pos[3]
    row = lax.broadcasted_iota(jnp.int32, (16, LANES), 0)

    def put(source, here, line, size):
        whole[pl.ds(pl.multiple_of(line, 16), size), :] = source[pl.ds(pl.multiple_of(here, 16), size), :]

    def at(far_y, z, x, core):
        shard = (((my_y + far_y) & 3) << 3) + ((z & 1) << 2) + x
        line = first_tile(shard) << 4
        return shard & 7, line, line + PIECE * (2 * (z >> 1) + core)

    rows_of_y = 8 * SHARD_LINES
    for far_y in range(4):
        for other in range(2):
            core = (my_core + other) & 1
            for array, far_x in enumerate((0, 1, 3, 2)):
                array = 4 if array == 3 and far_y >= 2 else array
                source = sources[10 * other + array]

                def first(i, _, source=source, far_x=far_x, far_y=far_y, core=core, array=array):
                    z, x = (my_z + i) & 3, (my_x + far_x) & 3
                    shard, start, line = at(far_y, z, x, core)
                    here = (4 * (far_y - 2 * (array == 4)) + i) * 208
                    put(source, here + 16, line + 16, 192)

                    @pl.when(line == start)
                    def _():
                        edges[0, shard] = source[pl.ds(pl.multiple_of(here, 16), 16), :]

                    @pl.when(line != start)
                    def _():
                        put(source, here, line, 16)

                    return 0

                lax.fori_loop(0, 4, first, 0, unroll=True)

            array = (0, 1, 3, 2)[far_y]
            for skip, array in ((0, array), (8, array)) if array < 3 else ((0, 3), (8, 4)):
                source = sources[10 * other + 5 + array]

                def second(i, _, source=source, far_y=far_y, core=core, skip=skip, array=array):
                    x, z = (my_x + ((i + skip) >> 2)) & 3, (my_z + (i & 3)) & 3
                    shard, start, line = at(far_y, z, x, core)
                    here = (i + (skip if array < 3 else 0)) * 208
                    put(source, here, line + 208, 160)

                    @pl.when(line == start + 3 * PIECE)
                    def _():
                        last = jnp.where((x == 1) | (x == 2), 160, 144)
                        edges[1, shard] = source[pl.ds(pl.multiple_of(here + last, 16), 16), :]

                    @pl.when(line != start + 3 * PIECE)
                    def _():
                        put(source, here + 160, line + 368, 48)

                    return 0

                lax.fori_loop(0, 8, second, 0, unroll=4)
        base = pl.multiple_of(rows_of_y * ((my_y + far_y) & 3), 16)
        for shard in range(8):
            x = shard % 4
            tile = real(edges[0, shard])
            if x:
                tile = jnp.where(row < (12 * x) % 16, real(edges[1, shard - 1]), tile)
            whole[pl.ds(pl.multiple_of(base + 16 * ((403 * shard) // 4), 16), 16), :] = low(tile)
        pltpu.make_async_copy(whole.at[pl.ds(base, rows_of_y)], out.at[pl.ds(base, rows_of_y)], sem.at[far_y]).start()
    for far_y in range(4):
        pltpu.make_async_copy(whole.at[pl.ds(0, rows_of_y)], out.at[pl.ds(0, rows_of_y)], sem.at[far_y]).wait()


def unpack(pos, pieces):
    hbm, vmem = pl.BlockSpec(memory_space=pl.ANY), pl.BlockSpec(memory_space=pltpu.VMEM)
    return pl.pallas_call(
        unpack_kernel,
        out_shape=jax.ShapeDtypeStruct((LINES, LANES), jnp.bfloat16),
        in_specs=[pl.BlockSpec(memory_space=pltpu.SMEM)] + [vmem] * 20,
        out_specs=hbm,
        scratch_shapes=[
            pltpu.VMEM((LINES, LANES), jnp.bfloat16),
            pltpu.VMEM((2, 8, 16, LANES), jnp.bfloat16),
            pltpu.SemaphoreType.DMA((4,)),
        ],
        compiler_params=pltpu.CompilerParams(vmem_limit_bytes=48 * 2**20),
        cost_estimate=pl.CostEstimate(flops=0, bytes_accessed=27_000_000, transcendentals=0),
        name="unpack_weights",
    )(pos, *pieces)


def own_update_kernel(where, scales, squares, piece, master, moment_one, moment_two, out):
    start, turn = where[0], where[1]
    total = jnp.sum(squares[...], axis=1, keepdims=True)
    clipped = piece[...] * (MAX_NORM / jnp.maximum(jnp.sqrt(total), MAX_NORM))

    def lines(ref):
        return pltpu.roll(ref[pl.ds(start, PIECE), :], turn, 0)

    out[...] = low(adam_step(clipped, lines(master), lines(moment_one), lines(moment_two), scales[0], scales[1])[2])


def own_update(offset, scales, squares, piece, master, moment_one, moment_two):
    start = jnp.clip(offset, 0, SHARD_LINES - PIECE)
    where = jnp.stack([start, (start - offset + PIECE) % PIECE]).astype(jnp.int32)
    smem, vmem = pl.BlockSpec(memory_space=pltpu.SMEM), pl.BlockSpec(memory_space=pltpu.VMEM)
    return pl.pallas_call(
        own_update_kernel,
        out_shape=jax.ShapeDtypeStruct((PIECE, LANES), jnp.bfloat16),
        in_specs=[smem, smem] + [vmem] * 5,
        out_specs=vmem,
        compiler_params=pltpu.CompilerParams(vmem_limit_bytes=16 * 2**20),
        name="own_update",
    )(where, scales, squares, piece, *[v.reshape(SHARD_LINES, LANES) for v in (master, moment_one, moment_two)])


SPAN = 256
MICRO = 2
GROUPS = 8
ROWS = 256
F32 = jnp.float32


def nt(left, right, precision=None):
    return lax.dot_general(left, right, (((1,), (1,)), ((), ())), precision=precision, preferred_element_type=F32)


def tn(left, right, precision=None):
    return lax.dot_general(left, right, (((0,), (0,)), ((), ())), precision=precision, preferred_element_type=F32)


def nn(left, right, precision=None):
    return lax.dot_general(left, right, (((1,), (0,)), ((), ())), precision=precision, preferred_element_type=F32)


def sigmoid(v):
    return 0.5 + 0.5 * jnp.tanh(0.5 * v)


def iota(shape, dim):
    return lax.broadcasted_iota(jnp.int32, shape, dim)


def shifts(marks, first, length, step, offset, columns=slice(0, SPAN)):
    parts = []
    for d in range(1, 4):
        hit = iota((length, SPAN), 0) == iota((length, SPAN), 1) + step * d + offset
        parts.append(jnp.where(hit, marks[first + d - 1 : first + d, :], 0.0)[:, columns])
    return low(jnp.concatenate(parts, axis=1))


def by_head(ref, r):
    rows = [jnp.broadcast_to(ref[pl.ds(4 * r + k, 1), :], (HDIM, ref.shape[1])) for k in range(4)]
    return jnp.concatenate(rows, axis=0)


def put_head_sums(ref, r, block):
    for k in range(4):
        ref[pl.ds(4 * r + k, 1), :] = jnp.sum(block[k * HDIM : (k + 1) * HDIM], axis=0, keepdims=True)


def chunk(r):
    return pl.ds(pl.multiple_of(r * ROWS, ROWS), ROWS)


def set_up_kernel(
    place, tokens, segments, gain, kernel, bias, heads, gate_gain, normed, marks, taps, steps, coef, table
):
    x = real(tokens[...])
    factor = lax.rsqrt(jnp.mean(x * x, axis=1, keepdims=True) + EPSILON)
    for t in range(D // LANES):
        part = slice(t * LANES, (t + 1) * LANES)
        normed[:, part] = low(x[:, part] * factor * real(gain[t : t + 1, :]))

    first = place[0] * SPAN
    lane = iota((1, SPAN), 1)
    for m in range(MICRO):
        part = slice(m * SPAN, (m + 1) * SPAN)
        here = segments[m, :, pl.ds(pl.multiple_of(first, SPAN), SPAN)]
        left = segments[m, :, pl.ds(pl.multiple_of(jnp.maximum(first - LANES, 0), LANES), LANES)]
        right = segments[m, :, pl.ds(pl.multiple_of(jnp.minimum(first + SPAN, 3 * SPAN), LANES), LANES)]
        here, left, right = real(here), real(left), real(right)
        left = jnp.where(place[0] > 0, left, -1.0)
        right = jnp.where(place[0] < 3, right, -1.0)
        left, right = jnp.concatenate([left, left], axis=1), jnp.concatenate([right, right], axis=1)
        rows = []
        for d in range(1, 4):
            before = jnp.where(lane < d, pltpu.roll(left, d, 1), pltpu.roll(here, d, 1))
            rows.append(before == here)
        for d in range(1, 4):
            after = pltpu.roll(here, SPAN - d, 1)
            rows.append(jnp.where(lane >= SPAN - d, pltpu.roll(right, SPAN - d, 1), after) == here)
        prior, final = left[:, LANES - 1 : LANES], here[:, SPAN - 1 :]
        rows += [here == prior, here == final, jnp.broadcast_to(final == prior, here.shape)]
        rows = [row.astype(F32) for row in rows] + [here] + [jnp.zeros((1, SPAN), F32)] * 6
        marks[:, part] = jnp.concatenate(rows, axis=0)

    def columns(rows):
        return jnp.transpose(jnp.concatenate(rows + [jnp.zeros((8 - len(rows), LANES), F32)], axis=0))

    for t in range(CH // LANES):
        part = slice(t * LANES, (t + 1) * LANES)
        rows = [real(kernel[k : k + 1, part]) for k in range(4)] + [real(bias[t : t + 1, :])]
        taps[part, :] = columns(rows)
    steps[...] = columns([heads[0:1, :], jnp.exp(heads[1:2, :])])[0:HEADS, :]
    pick = (iota((LANES, DI), 1) >> 6 == iota((LANES, DI), 0)).astype(F32)
    table[...] = nn(jnp.broadcast_to(heads[2:3, :], (8, LANES)), pick, lax.Precision.HIGHEST)
    for t in range(DI // LANES):
        part = slice(t * LANES, (t + 1) * LANES)
        coef[part, :] = columns([real(gate_gain[t : t + 1, :]), table[0:1, part]])


def products_kernel(gate_weight, out_weight, normed, cotangent, gate, grad_mixed):
    gate[...] = nt(gate_weight[...], normed[...])
    grad_mixed[...] = nt(out_weight[...], cotangent[...])


def prepare_kernel(
    weight, step_weight, normed, rim, gain, taps, steps, marks,
    ci, conv, signal, inflow, maps, raw, cum, step, cols, local, through, state, move, enter, edge
):
    r = pl.program_id(0)
    parts = [slice(m * SPAN, (m + 1) * SPAN) for m in range(MICRO)]

    @pl.when(r == 0)
    def _():
        x = real(rim[...])
        factor = lax.rsqrt(jnp.mean(x * x, axis=1, keepdims=True) + EPSILON)
        for t in range(D // LANES):
            part = slice(t * LANES, (t + 1) * LANES)
            edge[:, part] = low(x[:, part] * factor * real(gain[t : t + 1, :]))
        raw[...] = nt(step_weight[...], normed[...])
        step[...] = jax.nn.softplus(raw[...] + steps[:, 0:1])
        upto = (iota((SPAN, SPAN), 0) <= iota((SPAN, SPAN), 1)).astype(F32)
        for m, part in enumerate(parts):
            here = marks[:, part]
            move[m] = shifts(here, 0, SPAN, -1, 0)
            enter[m] = shifts(here, 0, 16, -1, 16, slice(0, LANES))
            decay = -step[:, part] * steps[:, 1:2]
            total = nn(decay, upto, lax.Precision.HIGHEST)
            cum[:, part] = total
            column = lax.dot_general(
                upto, decay, (((0,), (1,)), ((), ())), precision=lax.Precision.HIGHEST, preferred_element_type=F32
            )
            for g in range(GROUPS):
                cols[g, part, :] = column[:, 4 * g : 4 * g + 4]
            ends = total[:, SPAN - 1 :]
            state[:, part] = here[7:8, :] * jnp.exp(ends - total)
            through[m] = jnp.broadcast_to(here[8:9, 0:1] * jnp.exp(ends), (HEADS, LANES))

    x = low(nt(weight[...], normed[...]))
    ci[...] = x
    halo = low(nt(weight[...], edge[...]))
    flows = []
    for m, part in enumerate(parts):
        moved = nn(x[:, part], move[m])
        edges = nn(halo[:, 16 * m : 16 * m + 16], enter[m])
        total = taps[:, 4:5] + real(x[:, part]) * taps[:, 3:4]
        border = 0.0
        for d in range(1, 4):
            tap = taps[:, 3 - d : 4 - d]
            total = total + moved[:, (d - 1) * SPAN : d * SPAN] * tap
            border = border + edges[:, (d - 1) * LANES : d * LANES] * tap
        total = jnp.concatenate([total[:, :LANES] + border, total[:, LANES:]], axis=1)
        conv[:, part] = total
        flows.append(total * sigmoid(total))

    @pl.when(r == 0)
    def _():
        for flow, part in zip(flows, parts):
            maps[:, part] = flow

    @pl.when(r > 0)
    def _():
        for m, (flow, part) in enumerate(zip(flows, parts)):
            signal[:, part] = low(flow)
            heads = by_head(step, r - 1)[:, part]
            tails = by_head(state, r - 1)[:, part]
            flow = flow * heads
            inflow[:, part] = low(flow)
            local[m] = low(nt(low(flow * tails), low(maps[0:LANES, part])))


def turn_kernel(normed, upstream, left, cot, turned):
    for t in range(4):
        part = slice(t * LANES, (t + 1) * LANES)
        turned[...] = jnp.transpose(real(normed[part, :]))
        for k in range(4):
            left[256 * k : 256 * (k + 1), part] = low(turned[pl.ds(k, 256, stride=4), :])
    cot[...] = low(pltpu.roll(real(upstream[...]), D - 32, 1))


def same_document(marks):
    column = jnp.transpose(jnp.broadcast_to(marks[9:10, :], (8, SPAN)))[:, 0:1]
    return (column == marks[9:10, :]) & (iota((SPAN, SPAN), 0) <= iota((SPAN, SPAN), 1))


def mixing(maps, marks):
    products = tn(maps[0:LANES, :], maps[LANES:, :], lax.Precision.HIGHEST)
    return jnp.where(same_document(marks), products, 0.0)


def within_kernel(inflow, maps, cum, cols, marks, out, table):
    table[...] = mixing(maps, marks)
    half = SPAN // 2

    def heads(g, _):
        results = []
        x4 = inflow[chunk(g), :]
        for h in range(4):
            row, col = cum[pl.ds(4 * g + h, 1), :], cols[g, :, h : h + 1]
            upper = low(jnp.exp(jnp.minimum(row - col[:half], 0.0)) * table[:half, :])
            lower = low(jnp.exp(jnp.minimum(row[:, half:] - col[half:], 0.0)) * table[half:, half:])
            x = x4[h * HDIM : (h + 1) * HDIM, :]
            y = nn(x[:, :half], upper)
            results.append(jnp.concatenate([y[:, :half], y[:, half:] + nn(x[:, half:], lower)], axis=1))
        out[chunk(g), :] = jnp.concatenate(results, axis=0)
        return 0

    lax.fori_loop(0, GROUPS, heads, 0, unroll=4)


def gate_kernel(
    inside, enter, last, maps, signal, gate, grad, cum, marks, coef,
    gated_low, grad_gate, grad_scan, carried_sum, skip_sum, gain_sum, grad_state, grad_read, scan, entry
):
    entry[...] = marks[6:7, :] * jnp.exp(cum[...])
    reads = low(maps[LANES:, :])

    @pl.when(pl.program_id(0) == 0)
    def _():
        gain_sum[...] = jnp.zeros_like(gain_sum)

    def forward(r, sums):
        carried = nn(enter[0, chunk(r), :] + last[0, chunk(r), :], reads) * by_head(entry, r)
        total = inside[chunk(r), :] + carried + coef[chunk(r), 1:2] * real(signal[chunk(r), :])
        scan[chunk(r), :] = total
        z = gate[chunk(r), :]
        gated = total * (z * sigmoid(z))
        up = grad[chunk(r), :] * coef[chunk(r), 0:1]
        squares, cross = sums
        return (
            squares + jnp.sum(gated * gated, axis=0, keepdims=True),
            cross + jnp.sum(gated * up, axis=0, keepdims=True),
        )

    nothing = jnp.zeros((1, SPAN), F32)
    squares, cross = lax.fori_loop(0, 8, forward, (nothing, nothing), unroll=4)
    factor = lax.rsqrt(squares * (1.0 / DI) + EPSILON)
    pull = factor * factor * cross * (1.0 / DI)
    grad_read[...] = jnp.zeros_like(grad_read)

    def backward(r, _):
        heads = by_head(entry, r)
        state = enter[0, chunk(r), :] + last[0, chunk(r), :]
        carried = nn(state, reads) * heads
        total = scan[chunk(r), :]
        z = gate[chunk(r), :]
        sig = sigmoid(z)
        soft = z * sig
        gated = total * soft
        scaled = gated * factor
        gain = coef[chunk(r), 0:1]
        given = grad[chunk(r), :]
        gated_low[chunk(r), :] = low(scaled * gain)
        share = given * scaled
        gain_sum[chunk(r), :] += share[:, :LANES] + share[:, LANES:]
        back = factor * (given * gain - gated * pull)
        grad_gate[chunk(r), :] = low(back * total * (sig * (1.0 + z * (1.0 - sig))))
        push = back * soft
        grad_scan[chunk(r), :] = low(push)
        put_head_sums(carried_sum, r, push * carried)
        put_head_sums(skip_sum, r, push * real(signal[chunk(r), :]))
        entering = low(push * heads)
        grad_state[0, chunk(r), :] = low(nt(entering, reads))
        grad_read[...] += tn(state, entering)
        return 0

    lax.fori_loop(0, 8, backward, 0, unroll=4)


def within_back_kernel(
    inflow, push, inside, maps, cum, cols, marks, grad_inflow, decay_sum, grad_maps, table, grad_table
):
    table[...] = mixing(maps, marks)
    grad_table[...] = jnp.zeros_like(grad_table)
    half = SPAN // 2

    def heads(g, _):
        x4, d4, results = inflow[chunk(g), :], push[chunk(g), :], []
        above, below = 0.0, 0.0
        for h in range(4):
            rows = slice(h * HDIM, (h + 1) * HDIM)
            row, col = cum[pl.ds(4 * g + h, 1), :], cols[g, :, h : h + 1]
            upper = jnp.exp(jnp.minimum(row - col[:half], 0.0))
            lower = jnp.exp(jnp.minimum(row[:, half:] - col[half:], 0.0))
            x, d = x4[rows, :], d4[rows, :]
            above += upper * tn(x[:, :half], d)
            below += lower * tn(x[:, half:], d[:, half:])
            first = nt(d, low(upper * table[:half, :]))
            second = nt(d[:, half:], low(lower * table[half:, half:]))
            results.append(jnp.concatenate([first, second], axis=1))
        grad_table[:half, :] += above
        grad_table[half:, half:] += below
        back = jnp.concatenate(results, axis=0)
        grad_inflow[chunk(g), :] = low(back)
        put_head_sums(decay_sum, g, real(d4) * inside[chunk(g), :] - real(x4) * back)
        return 0

    lax.fori_loop(0, GROUPS, heads, 0, unroll=4)
    spread = low(jnp.where(same_document(marks), grad_table[...], 0.0))
    grad_maps[0:LANES, :] = nt(low(maps[LANES:, :]), spread)
    grad_maps[LANES:, :] = nn(low(maps[0:LANES, :]), spread)


def state_back_kernel(
    leave, leave_last, enter, enter_last, conv, push, grad_inflow, maps, cum, step, raw, decay_sum, carried_sum, grad_maps, grad_read,
    steps, marks, coef, grad_conv, rim, grad_raw, bias_sum, rate_sum, tail, from_tail, from_step, crossing, grad_write
):
    ends = cum[:, SPAN - 1 : SPAN]
    tail[...] = marks[7:8, :] * jnp.exp(ends - cum[...])
    writes = low(maps[0:LANES, :])
    front = ((iota((16, SPAN), 1) == iota((16, SPAN), 0)) & (iota((16, SPAN), 0) < 3)).astype(jnp.bfloat16)
    grad_write[...] = grad_maps[0:LANES, :]

    def through_silu(r, c, sig, above):
        given = above * (sig * (1.0 + c * (1.0 - sig)))
        given = low(given)
        grad_conv[chunk(r), :] = given
        rim[0, :, chunk(r)] = low(nt(front, given))

    def channels(r, _):
        c = conv[chunk(r), :]
        sig = sigmoid(c)
        signal = c * sig
        heads, tails = by_head(step, r), by_head(tail, r)
        x = signal * heads
        back = leave[0, chunk(r), :] + leave_last[0, chunk(r), :]
        ended = nn(back, writes) * tails
        whole = real(grad_inflow[chunk(r), :]) + ended
        grad_write[...] += tn(back, low(x * tails))
        put_head_sums(from_tail, r, x * ended)
        put_head_sums(from_step, r, whole * signal)
        put_head_sums(crossing, r, real(back) * real(enter[0, chunk(r), :] + enter_last[0, chunk(r), :]))
        through_silu(r, c, sig, whole * heads + coef[chunk(r), 1:2] * real(push[chunk(r), :]))
        return 0

    lax.fori_loop(0, 8, channels, 0, unroll=4)
    c = conv[chunk(8), :]
    through_silu(8, c, sigmoid(c), jnp.concatenate([grad_write[...], grad_maps[LANES:, :] + grad_read[...]], axis=0))
    last = iota((HEADS, SPAN), 1) == SPAN - 1
    passing = marks[8:9, 0:1] * jnp.exp(ends) * jnp.sum(crossing[...], axis=1, keepdims=True)
    tails = jnp.sum(from_tail[...], axis=1, keepdims=True)
    total = decay_sum[...] + carried_sum[...] - from_tail[...] + jnp.where(last, tails + passing, 0.0)
    onward = (iota((SPAN, SPAN), 0) >= iota((SPAN, SPAN), 1)).astype(F32)
    grad_decay = nn(total, onward, lax.Precision.HIGHEST)
    rate = steps[:, 1:2]
    rate_sum[...] = -grad_decay * step[...] * rate
    grad_step = (from_step[...] - grad_decay * rate) * sigmoid(raw[...] + steps[:, 0:1])
    bias_sum[...] = grad_step
    grad_raw[0:HEADS, :] = low(grad_step)
    grad_raw[HEADS:, :] = jnp.zeros((LANES - HEADS, SPAN), jnp.bfloat16)


def conv_back_kernel(grad_conv, ci, rim, taps, marks, grad_ci, sums, move, enter):
    @pl.when(pl.program_id(0) == 0)
    def _():
        for m in range(MICRO):
            here = marks[:, m * SPAN : (m + 1) * SPAN]
            move[m] = shifts(here, 3, SPAN, 1, 0)
            enter[m] = shifts(here, 3, 16, 1, -SPAN, slice(LANES, SPAN))

    totals = [0.0] * 5
    for m in range(MICRO):
        part = slice(m * SPAN, (m + 1) * SPAN)
        given, x = real(grad_conv[:, part]), real(ci[:, part])
        moved = nn(grad_conv[:, part], move[m])
        edges = tn(rim[m], enter[m])
        back = given * taps[:, 3:4]
        totals[3] += given * x
        totals[4] += given
        for d in range(1, 4):
            sooner = moved[:, (d - 1) * SPAN : d * SPAN]
            last = sooner[:, LANES:] + edges[:, (d - 1) * LANES : d * LANES]
            sooner = jnp.concatenate([sooner[:, :LANES], last], axis=1)
            back += sooner * taps[:, 3 - d : 4 - d]
            totals[3 - d] += sooner * x
        grad_ci[:, part] = low(back)
    count = jnp.zeros((ROWS, LANES), F32)
    for k in range(5):
        pick = (iota((LANES, LANES), 1) == k).astype(jnp.bfloat16)
        count += nn(low(totals[k][:, :LANES] + totals[k][:, LANES:]), pick)
    sums[...] = count[:, 0:8]


def call(kernel, grid, ins, outs, scratch, cost, name, mebibytes):
    return pl.pallas_call(
        kernel,
        grid=grid,
        in_specs=[pl.BlockSpec(block, where) for _, block, where in ins],
        out_specs=[pl.BlockSpec(block, where) for _, _, block, where in outs],
        out_shape=[jax.ShapeDtypeStruct(shape, dtype) for shape, dtype, _, _ in outs],
        scratch_shapes=scratch,
        compiler_params=pltpu.CompilerParams(
            vmem_limit_bytes=mebibytes * 2**20, dimension_semantics=("arbitrary",) * len(grid)
        ),
        cost_estimate=pl.CostEstimate(flops=cost, bytes_accessed=20_000_000, transcendentals=0),
        name=name,
    )(*[array for array, _, _ in ins])


def neighbours(value, source, target):
    return lax.ppermute(value, GROUP, [(source, target)])


def chained(local, through, order, beside):
    by_heads = (MICRO, HEADS, HDIM, STATE)

    def joined(arrived):
        total = through[:, :, None, :] * real(arrived).reshape(by_heads) + real(local).reshape(by_heads)
        return low(total).reshape(local.shape)

    one = neighbours(local, order[0], order[1])
    two = neighbours(joined(one), order[1], order[2])
    two, beside = lax.optimization_barrier((two, beside))
    three = neighbours(joined(two), order[2], order[3])
    return (one + two, three), beside


def shards(
    tokens, segments, cotangent, norm_gain, in_weight, conv_kernel, conv_bias, step_bias, decay_log,
    skip_gain, gate_gain, out_weight, master, moment_one, moment_two, step_count
):
    width = MICRO * SPAN
    bf16 = jnp.bfloat16
    spot = position()
    place = lax.axis_index(GROUP)
    one = (MICRO,)
    by_m = lambda m: (0, m)
    whole, first = lambda m: (0, 0), lambda m: (m, 0, 0)
    upstream = cotangent.reshape(width, D)
    turned_weight = in_weight.T
    conv_weight = turned_weight[DI : DI + CH]

    heads = jnp.stack([real(step_bias), real(decay_log), real(skip_gain)])
    heads = jnp.pad(heads, ((0, 5), (0, LANES - HEADS)))
    lines = [v.reshape(-1, LANES) for v in (norm_gain, conv_bias, gate_gain)]
    ins = [tokens.reshape(width, D), segments, lines[0], conv_kernel, lines[1], heads, lines[2]]
    outs = [((width, D), bf16), ((16, width), F32), ((CH, 8), F32), ((HEADS, 8), F32), ((DI, 8), F32)]
    at_start = lambda rank: lambda i: (0,) * rank
    normed_low, marks, taps, steps, coef = pl.pallas_call(
        set_up_kernel,
        grid=(1,),
        out_shape=[jax.ShapeDtypeStruct(*out) for out in outs],
        in_specs=[pl.BlockSpec(memory_space=pltpu.SMEM)] + [pl.BlockSpec(v.shape, at_start(v.ndim)) for v in ins],
        out_specs=[pl.BlockSpec(shape, at_start(len(shape))) for shape, _ in outs],
        scratch_shapes=[pltpu.VMEM((8, DI), F32)],
        compiler_params=pltpu.CompilerParams(vmem_limit_bytes=56 * 2**20),
        name="set_up",
    )(place.reshape(1), *ins)
    mark_in = (marks, (16, SPAN), by_m)
    rim_tokens, normed_low = lax.optimization_barrier((tokens[:, 0, SPAN - 16 :, :], normed_low))
    rim_tokens = lax.ppermute(rim_tokens, GROUP, [(0, 1), (1, 2), (2, 3)])

    whole1, head_rows = lambda r: (0, 0), lambda r: (jnp.maximum(r - 1, 0), 0)
    rows_of = lambda r: jnp.where(r == 0, GROUPS, r - 1)
    by_rows = lambda r: (rows_of(r), 0)
    lot = (HEADS, width)
    ci, conv, signal, inflow, maps, raw, cum, step, cols, local, through = call(
        prepare_kernel, (CH // ROWS,),
        [(turned_weight, (ROWS, D), lambda r: (GROUPS + rows_of(r), 0)),
         (turned_weight, (HEADS, D), lambda r: ((DI + CH) // HEADS, 0)), (normed_low, (width, D), whole1),
         (rim_tokens.reshape(-1, D), (32, D), whole1), (lines[0], lines[0].shape, whole1), (taps, (ROWS, 8), by_rows), (steps, (HEADS, 8), whole1),
         (marks, (16, width), whole1)],
        [((CH, width), bf16, (ROWS, width), by_rows), ((CH, width), F32, (ROWS, width), by_rows),
         ((DI, width), bf16, (ROWS, width), head_rows), ((DI, width), bf16, (ROWS, width), head_rows),
         ((2 * STATE, width), F32, (2 * STATE, width), whole1), (lot, F32, lot, whole1), (lot, F32, lot, whole1),
         (lot, F32, lot, whole1), ((GROUPS, width, 4), F32, (GROUPS, width, 4), lambda r: (0, 0, 0)),
         ((MICRO, DI, STATE), bf16, (MICRO, ROWS, STATE), lambda r: (0, jnp.maximum(r - 1, 0), 0)),
         ((MICRO, HEADS, LANES), F32, (MICRO, HEADS, LANES), lambda r: (0, 0, 0))],
        [pltpu.VMEM(lot, F32), pltpu.VMEM((MICRO, SPAN, 3 * SPAN), bf16), pltpu.VMEM((MICRO, 16, 3 * LANES), bf16),
         pltpu.VMEM((32, D), bf16)],
        10**9, "project_and_convolve", 56,
    )

    tiles = lambda r: (r, 0)
    gate, grad_mixed = call(
        products_kernel, (GROUPS // 2,),
        [(turned_weight, (2 * ROWS, D), tiles), (out_weight, (2 * ROWS, D), tiles), (normed_low, (width, D), whole1),
         (upstream, (width, D), whole1)],
        [((DI, width), F32, (2 * ROWS, width), tiles)] * 2, [], 4 * 10**9, "gate_products", 24,
    )
    tall, few = (DI, SPAN), (HEADS, SPAN)
    state_block = (1, DI, STATE)
    head_ins = [
        (maps, (2 * STATE, SPAN), by_m),
        (cum, few, by_m),
        (cols, (GROUPS, SPAN, 4), lambda m: (0, m, 0)),
        mark_in,
    ]
    table = pltpu.VMEM((SPAN, SPAN), F32)
    (inside,) = call(
        within_kernel, one, [(inflow, tall, by_m)] + head_ins, [((DI, width), F32, tall, by_m)], [table],
        4 * 10**9, "within_blocks", 24,
    )
    enter, (inside, gate, grad_mixed) = chained(local, through, (0, 1, 2, 3), (inside, gate, grad_mixed))

    gated_low, grad_gate, push, carried_sum, skip_sum, gain_sum, grad_state, grad_read = call(
        gate_kernel, one,
        [(inside, tall, by_m), (enter[0], state_block, first), (enter[1], state_block, first), (maps, (2 * STATE, SPAN), by_m), (signal, tall, by_m),
         (gate, tall, by_m), (grad_mixed, tall, by_m), (cum, (HEADS, SPAN), by_m), mark_in, (coef, (DI, 8), whole)],
        [((DI, width), bf16, tall, by_m), ((DI, width), bf16, tall, by_m), ((DI, width), bf16, tall, by_m),
         ((HEADS, width), F32, (HEADS, SPAN), by_m), ((HEADS, width), F32, (HEADS, SPAN), by_m),
         ((DI, LANES), F32, (DI, LANES), whole), ((MICRO, DI, STATE), bf16, state_block, first),
         ((STATE, width), F32, (STATE, SPAN), by_m)],
        [pltpu.VMEM((DI, SPAN), F32), pltpu.VMEM((HEADS, SPAN), F32)], 2 * 10**9, "gate_and_back", 50,
    )
    grad_inflow, decay_sum, grad_maps = call(
        within_back_kernel, one, [(inflow, tall, by_m), (push, tall, by_m), (inside, tall, by_m)] + head_ins,
        [((DI, width), bf16, tall, by_m), ((HEADS, width), F32, few, by_m),
         ((2 * STATE, width), F32, (2 * STATE, SPAN), by_m)],
        [table, table], 8 * 10**9, "within_blocks_back", 56,
    )
    left, cot = call(
        turn_kernel, (1,), [(normed_low, (width, D), whole), (upstream, (width, D), whole)],
        [((D, width), bf16, (D, width), whole), ((width, D), bf16, (width, D), whole)],
        [pltpu.VMEM((D, LANES), F32)], 10**6, "turn", 14,
    )
    leave, (grad_inflow, decay_sum, grad_maps, left, cot) = chained(
        grad_state, through, (3, 2, 1, 0), (grad_inflow, decay_sum, grad_maps, left, cot)
    )

    grad_conv, rim, grad_raw, bias_sum, rate_sum = call(
        state_back_kernel, one,
        [(leave[0], state_block, first), (leave[1], state_block, first), (enter[0], state_block, first),
         (enter[1], state_block, first), (conv, (CH, SPAN), by_m), (push, tall, by_m),
         (grad_inflow, tall, by_m), (maps, (2 * STATE, SPAN), by_m), (cum, few, by_m), (step, few, by_m), (raw, few, by_m),
         (decay_sum, few, by_m), (carried_sum, few, by_m), (grad_maps, (2 * STATE, SPAN), by_m),
         (grad_read, (STATE, SPAN), by_m), (steps, (HEADS, 8), whole), mark_in, (coef, (DI, 8), whole)],
        [((CH, width), bf16, (CH, SPAN), by_m), ((MICRO, 16, CH), bf16, (1, 16, CH), first),
         ((LANES, width), bf16, (LANES, SPAN), by_m), ((HEADS, width), F32, few, by_m), ((HEADS, width), F32, few, by_m)],
        [pltpu.VMEM(few, F32), pltpu.VMEM(few, F32), pltpu.VMEM(few, F32), pltpu.VMEM((HEADS, LANES), F32),
         pltpu.VMEM((STATE, SPAN), F32)], 10**9, "state_and_silu_back", 56,
    )
    next_rim = lax.ppermute(rim, GROUP, [(1, 0), (2, 1), (3, 2)])
    early = tn(grad_gate, turned_weight[:DI])
    next_rim, early = lax.optimization_barrier((next_rim, early))

    by_r = lambda r: (r, 0)
    grad_ci, tap_sums = call(
        conv_back_kernel, (CH // ROWS,),
        [(grad_conv, (ROWS, width), by_r), (ci, (ROWS, width), by_r), (next_rim, (MICRO, 16, ROWS), lambda r: (0, 0, r)),
         (taps, (ROWS, 8), by_r), (marks, (16, width), lambda r: (0, 0))],
        [((CH, width), bf16, (ROWS, width), by_r), ((CH, 8), F32, (ROWS, 8), by_r)],
        [pltpu.VMEM((MICRO, SPAN, 3 * SPAN), bf16), pltpu.VMEM((MICRO, 16, 3 * LANES), bf16)], 10**8, "convolution_back", 56,
    )

    middle = [tap_sums[:, :5].T.reshape(-1), jnp.sum(bias_sum, axis=1), jnp.sum(rate_sum, axis=1)]
    middle += [jnp.sum(skip_sum, axis=1), jnp.sum(gain_sum, axis=1), jnp.zeros((32 + 5 * LANES,), F32)]
    middle = jnp.concatenate(middle).reshape(-1, LANES)
    packed = pack(spot, left, grad_gate, grad_ci, grad_raw, gated_low, cot, middle)
    packed, late = lax.optimization_barrier((packed, (grad_gate, grad_ci, grad_raw)))
    rows_in = real(tokens.reshape(width, D))
    norm_back = jax.vjp(norm_piece, rows_in, real(norm_gain))[1]
    grad_normed = early + tn(late[1], conv_weight) + tn(late[2][:HEADS], turned_weight[DI + CH :])
    grad_rows, grad_norm_gain = norm_back(grad_normed)

    def finish(inputs):
        gated_low, grad_rows = inputs
        output = low(rows_in + tn(gated_low, out_weight)).reshape(tokens.shape)
        return output, low(real(upstream) + grad_rows).reshape(tokens.shape)

    piece, (output, input_grad) = reduce_pieces(
        *packed, grad_norm_gain.reshape(-1, LANES), finish, (gated_low, grad_rows)
    )

    skew = (12 * lax.axis_index("x")) % 16
    offset = PIECE * place - skew
    line = offset + iota((PIECE, 1), 0)
    own = jnp.where((line >= 0) & (line < SHARD_LINES), piece, 0.0)
    squares = sent_to_all(jnp.sum(own * own).reshape(1, 1), EVERY).reshape(1, -1)
    core, high = lax.axis_index("core") == 0, lax.axis_index("zh") == 0
    pair = [piece, swap_cores(piece)]
    pair = jnp.concatenate([jnp.where(core, *pair), jnp.where(core, *pair[::-1])])
    both = [pair, lax.ppermute(pair, "zh", [(0, 1), (1, 0)])]
    step_real = real(step_count[0])
    scales = jnp.stack([1.0 / (1.0 - jnp.power(BETA_ONE, step_real)), 1.0 / (1.0 - jnp.power(BETA_TWO, step_real))])
    both, squares = lax.optimization_barrier((both, squares))
    mine = own_update(offset, scales, squares, piece, master, moment_one, moment_two)

    def rest(inputs):
        both, squares, moments = inputs
        window = jnp.concatenate([jnp.where(high, *both), jnp.where(high, *both[::-1])])
        shard = lax.dynamic_slice(window, (skew, 0), (SHARD_LINES, LANES)).reshape(-1)
        clip_factor = MAX_NORM / jnp.maximum(jnp.sqrt(jnp.sum(squares)), MAX_NORM)
        return shard, adam_step(shard * clip_factor, *moments, scales[0], scales[1])

    moments = (master, moment_one, moment_two)
    pieces, (shard, results) = gather_pieces(mine, rest, (both, squares, moments))
    copies = unpack(spot, pieces).reshape(-1)
    return (output, input_grad, shard, *results, copies)


def solution(mesh):
    finer = Mesh(mesh.devices.reshape(4, 2, 4, 2, 2), ("y", "zl", "x", "zh", "core"))
    return jax.shard_map(
        shards,
        mesh=finer,
        in_specs=(
            P(None, DP, GROUP, None),
            P(None, DP, None),
            P(None, DP, GROUP, None),
            P(),
            P(),
            P(),
            P(),
            P(),
            P(),
            P(),
            P(),
            P(),
            P(DP),
            P(DP),
            P(DP),
            P(),
        ),
        out_specs=(
            P(None, DP, GROUP, None),
            P(None, DP, GROUP, None),
            P(DP),
            P(DP),
            P(DP),
            P(DP),
            P(),
        ),
        check_vma=False,
    )
```

```python
import functools

import jax
import jax.numpy as jnp
from jax import lax
from jax.experimental import pallas as pl
from jax.experimental.pallas import tpu as pltpu
from jax.sharding import Mesh
from jax.sharding import PartitionSpec as P

D = 1024
DI = 2048
HEADS = 32
HDIM = 64
STATE = 128
CH = 2304
DP = ("y", "zl", "x")
GROUP = ("zh", "core")
EVERY = DP + GROUP


EPSILON = 1e-05
BETA_ONE = 0.9
BETA_TWO = 0.95
ADAM_EPSILON = 1e-08
LEARN_RATE = 0.01
WEIGHT_DECAY = 0.1
MAX_NORM = 1.0


def sent_to_all(shard, axis):
    copies = jnp.broadcast_to(shard, (lax.axis_size(axis), *shard.shape))
    return lax.all_to_all(copies, axis, split_axis=0, concat_axis=0, tiled=True)


def norm_piece(values, scaling):
    factor = lax.rsqrt(jnp.mean(values * values, axis=-1, keepdims=True) + EPSILON)
    return values * factor * scaling


def adam_step(clipped, master, moment_one, moment_two, first_scale, second_scale):
    first_moment = BETA_ONE * moment_one + (1.0 - BETA_ONE) * clipped
    second_moment = BETA_TWO * moment_two + (1.0 - BETA_TWO) * clipped * clipped
    first_hat, second_hat = first_moment * first_scale, second_moment * second_scale
    updated = master - LEARN_RATE * (first_hat / (jnp.sqrt(second_hat) + ADAM_EPSILON) + WEIGHT_DECAY * master)
    return (first_moment, second_moment, updated)


LANES = 128
LINES = 51584
SHARD_LINES = 1612
IN_LINE = 8
MID_LINE = 35080
OUT_LINE = 35187
PIECE = 416
SLOTS = 16
PARTS = ((0, 208), (208, 208))
TAIL_LINES = 51632
GROUP_LINES = 137
RING = {"x": ("x",), "y": ("y",), "z": ("zl", "zh")}
ROUTES = (("x", "y", "z"), ("y", "x", "z"))


def ring_place(axis, i):
    i = i % 4
    return (i % 2) * 2 + i // 2 if axis == "z" else i


def from_offset(block, axis, distance):
    route = [(ring_place(axis, i + distance), ring_place(axis, i)) for i in range(4)]
    return lax.ppermute(block, RING[axis], route)


def swap_cores(block):
    return lax.ppermute(block, "core", [(0, 1), (1, 0)])


def position():
    z = 2 * lax.axis_index("zh") + lax.axis_index("zl")
    return jnp.stack([lax.axis_index("y"), z, lax.axis_index("x"), lax.axis_index("core")]).astype(jnp.int32)


def first_tile(shard):
    return (403 * shard) >> 2


def pack_kernel(pos, mid_part, *rest):
    sources, keep, send = rest[:6], rest[6], rest[7]
    flat, carry, edge, stage, sems = rest[8:13]
    left, grad_gate, grad_ci, grad_raw, gated, cot = held = rest[13:19]
    loads = [pltpu.make_async_copy(source, here, rest[19].at[k]) for k, (source, here) in enumerate(zip(sources, held))]
    for k in (4, 5, 0, 1, 2, 3):
        loads[k].start()
    lane = lax.broadcasted_iota(jnp.int32, (256, LANES), 1)

    flat[0:IN_LINE, :] = jnp.zeros((IN_LINE, LANES), jnp.float32)
    flat[MID_LINE : MID_LINE + 104, :] = mid_part[0:104, :]
    flat[MID_LINE + 104 : MID_LINE + 107, :] = mid_part[104:107, :]
    edge[0:8, :] = mid_part[99:107, :]

    def rows(b, _):
        block = gated[pl.ds(pl.multiple_of(b * 256, 256), 256), :]
        product = jnp.dot(block, cot[...], preferred_element_type=jnp.float32)
        start = OUT_LINE + 2048 * b
        for t in range(7):
            flat[pl.ds(start + t, 256, stride=8), :] = product[:, t * LANES : (t + 1) * LANES]
        last = product[:, 7 * LANES :]
        edge[8:264, :] = last
        flat[pl.ds(start - 1, 256, stride=8), :] = jnp.where(lane < 96, edge[7:263, :], last)
        edge[0:8, :] = edge[256:264, :]
        return 0

    loads[4].wait()
    loads[5].wait()
    lax.fori_loop(0, 8, rows, 0)
    low = lax.broadcasted_iota(jnp.int32, (1, LANES), 1) < 96
    flat[OUT_LINE + 16383 : TAIL_LINES, :] = jnp.zeros((TAIL_LINES - OUT_LINE - 16383, LANES), jnp.float32)
    flat[OUT_LINE + 16383 : OUT_LINE + 16384, :] = jnp.where(low, edge[7:8, :], 0.0)

    my_y, my_z, my_x, my_core = pos[0], pos[1], pos[2], pos[3]

    def drain(slot):
        pltpu.make_async_copy(stage.at[slot], keep.at[pl.ds(0, PIECE)], sems.at[slot]).wait()

    def ship(n, _):
        i = (n + 88) & 127
        slot = n & (SLOTS - 1)

        @pl.when(n >= SLOTS)
        def _():
            drain(slot)

        shard, quarter = i >> 2, i & 3
        line = 16 * first_tile(shard) + PIECE * quarter
        stage[slot] = flat[pl.ds(pl.multiple_of(line, 16), PIECE), :].astype(jnp.bfloat16)
        x, zl, y = shard & 3, (shard >> 2) & 1, shard >> 3
        core = quarter & 1
        z = 2 * (quarter >> 1) + zl
        off = {"y": (y - my_y) & 3, "z": (z - my_z) & 3, "x": (x - my_x) & 3}
        for p, (start, size) in enumerate(PARTS):
            a, b, c = (off[axis] for axis in ROUTES[p])
            to = pl.ds(pl.multiple_of((((4 * p + a) * 4 + b) * 4 + c) * size, 16), size)
            source = stage.at[slot, pl.ds(start, size)]

            @pl.when(core == my_core)
            def _():
                pltpu.make_async_copy(source, keep.at[to], sems.at[slot]).start()

            @pl.when(core != my_core)
            def _():
                pltpu.make_async_copy(source, send.at[to], sems.at[slot]).start()

        return 0

    lax.fori_loop(0, 40, ship, 0)

    def put(tile, k, line):
        moved = pltpu.roll(tile, 32 * k, 1) if k else tile
        whole = jnp.where(lane < 32 * k, carry[k], moved) if k else moved
        flat[pl.ds(IN_LINE + 34 * k + line, 256, stride=GROUP_LINES), :] = whole
        carry[k] = moved

    def columns(block, line, tiles):
        product = nt(left[...], block)
        for k in range(4):
            for t in range(tiles):
                put(product[256 * k : 256 * (k + 1), t * LANES : (t + 1) * LANES], k, line + t)

    def from_gate(j, _):
        columns(grad_gate[pl.ds(pl.multiple_of(j * 512, 512), 512), :], 4 * j, 4)
        return 0

    def from_conv(j, _):
        columns(grad_ci[pl.ds(pl.multiple_of(j * 512, 512), 512), :], 16 + 4 * j, 4)
        return 0

    loads[0].wait()
    loads[1].wait()
    lax.fori_loop(0, 4, from_gate, 0, unroll=2)
    loads[2].wait()
    loads[3].wait()
    lax.fori_loop(0, 4, from_conv, 0, unroll=2)
    heads = []
    for k in range(1, 4):
        heads.append(flat[pl.ds(IN_LINE + 34 * k, 256, stride=GROUP_LINES), :])
    columns(jnp.concatenate([grad_ci[2048:2304, :], grad_raw[...]], axis=0), 32, 3)
    for k in range(1, 4):
        at = pl.ds(IN_LINE + 34 * k, 256, stride=GROUP_LINES)
        flat[at, :] = jnp.where(lane < 32 * k, flat[at, :], heads[k - 1])

    lax.fori_loop(40, 128, ship, 0)
    for slot in range(SLOTS):
        drain(slot)


def pack(pos, left, grad_gate, grad_ci, grad_raw, gated, cot, mid_part):
    vmem, hbm = pl.BlockSpec(memory_space=pltpu.VMEM), pl.BlockSpec(memory_space=pl.ANY)
    shape = jax.ShapeDtypeStruct((64 * PIECE, LANES), jnp.bfloat16)
    return pl.pallas_call(
        pack_kernel,
        out_shape=[shape] * 2,
        in_specs=[pl.BlockSpec(memory_space=pltpu.SMEM)] + [vmem] + [hbm] * 6,
        out_specs=[hbm] * 2,
        scratch_shapes=[
            pltpu.VMEM((TAIL_LINES, LANES), jnp.float32),
            pltpu.VMEM((4, 256, LANES), jnp.float32),
            pltpu.VMEM((264, LANES), jnp.float32),
            pltpu.VMEM((SLOTS, PIECE, LANES), jnp.bfloat16),
            pltpu.SemaphoreType.DMA((SLOTS,)),
        ]
        + [pltpu.VMEM(v.shape, v.dtype) for v in (left, grad_gate, grad_ci, grad_raw, gated, cot)]
        + [pltpu.SemaphoreType.DMA((6,))],
        compiler_params=pltpu.CompilerParams(vmem_limit_bytes=60 * 2**20),
        cost_estimate=pl.CostEstimate(flops=7_000_000_000, bytes_accessed=25_000_000, transcendentals=0),
        name="pack_gradients",
    )(pos, mid_part, left, grad_gate, grad_ci, grad_raw, gated, cot)


def real(v):
    return v.astype(jnp.float32)


def low(v):
    return v.astype(jnp.bfloat16)


def to_offset(block, axis, distance):
    route = [(ring_place(axis, i), ring_place(axis, i + distance)) for i in range(4)]
    return lax.ppermute(block, RING[axis], route)


def quarters(block):
    return block.reshape(4, -1, LANES)


def ring_sum(block, axis):
    block = quarters(block)
    half = block.shape[1] // 32 * 16
    a, b = to_offset(block[2, :half], axis, 1), to_offset(block[2, half:], axis, 3)
    one = jnp.concatenate([low(real(block[1, :half]) + real(a)), block[1, half:]])
    three = jnp.concatenate([block[3, :half], low(real(block[3, half:]) + real(b))])
    return real(block[0]) + real(to_offset(one, axis, 1)) + real(to_offset(three, axis, 3))


def direct_sum(block, axis):
    block = quarters(block)
    moved = [to_offset(block[d], axis, d) for d in (1, 3, 2)]
    return real(block[0]) + real(moved[0]) + real(moved[1]) + real(moved[2])


def reduce_pieces(keep, send, gain_grad, beside, given):
    got = swap_cores(send)
    held = [low(real(mine) + real(other)) for mine, other in zip(jnp.split(keep, 2), jnp.split(got, 2))]
    gain_grad = low(gain_grad + swap_cores(gain_grad))
    x, y, z = lax.axis_index("x"), lax.axis_index("y"), 2 * lax.axis_index("zh") + lax.axis_index("zl")
    block = 16 * (-x & 3) + 4 * (-y & 3) + (-z & 3)
    lines = jnp.arange(16)[:, None]
    mine = (lines < IN_LINE) & (lax.axis_index("core") == 0)
    start = (block * PARTS[0][1], 0)
    tile = lax.dynamic_slice(held[0], start, (16, LANES))
    tile = jnp.where(mine, jnp.pad(gain_grad, ((0, 16 - IN_LINE), (0, 0))), tile)
    held[0] = lax.dynamic_update_slice(held[0], tile, start)
    held, given = lax.optimization_barrier((held, given))
    first, second = low(ring_sum(held[0], "x")), low(ring_sum(held[1], "y"))
    (first, second), done = lax.optimization_barrier(((first, second), beside(given)))
    first, second = low(direct_sum(first, "y")), low(direct_sum(second, "x"))
    both = jnp.concatenate([quarters(first), quarters(second)], axis=1).reshape(-1, LANES)
    return direct_sum(both, "z"), done


def join_kernel(*refs):
    *blocks, first, second = refs
    for out, parts in ((first, blocks[: len(blocks) // 2]), (second, blocks[len(blocks) // 2 :])):
        start = 0
        for block in parts:
            out[start : start + block.shape[0], :] = block[...]
            start += block.shape[0]


def join(first, second):
    vmem = pl.BlockSpec(memory_space=pltpu.VMEM)
    rows = [sum(block.shape[0] for block in parts) for parts in (first, second)]
    return pl.pallas_call(
        join_kernel,
        out_shape=[jax.ShapeDtypeStruct((n, LANES), jnp.bfloat16) for n in rows],
        in_specs=[vmem] * (len(first) + len(second)),
        out_specs=[vmem] * 2,
        compiler_params=pltpu.CompilerParams(vmem_limit_bytes=8 * 2**20),
        name="join",
    )(*first, *second)


def gather_pieces(piece, beside, given):
    def spread(block, axis):
        return [block] + [from_offset(block, axis, d) for d in (1, 3, 2)]

    def in_order(parts):
        return [parts[0], parts[1], parts[3], parts[2]]

    n = PARTS[0][1]
    both = spread(piece, "z")
    both = in_order(both)
    first = spread(jnp.concatenate([block[:n] for block in both]), "y")
    second = spread(jnp.concatenate([block[n:] for block in both]), "x")
    first, second = join(in_order(first), in_order(second))
    ends = [(first, "x"), (second, "y")]
    sides = [[from_offset(block, axis, d) for d in (1, 3)] for block, axis in ends]
    swapped = [swap_cores(block) for block, _ in ends]
    swapped, given = lax.optimization_barrier((swapped, given))
    sides, swapped, done = lax.optimization_barrier((sides, swapped, beside(given)))
    mine, other = [], []
    for (block, axis), (left, right), first in zip(ends, sides, swapped):
        half = block.shape[0] // 2
        halves = [from_offset(right[:half], axis, 3), from_offset(left[half:], axis, 1)]
        mine += [block, left, right, *halves]
        left, right, halves = lax.optimization_barrier((left, right, halves))
        other += [first] + [swap_cores(part) for part in (left, right, *halves)]
    return mine + other, done


def unpack_kernel(pos, *rest):
    sources, out = rest[:20], rest[20]
    whole, edges, sem = rest[21:]
    my_y, my_z, my_x, my_core = pos[0], pos[1], pos[2], pos[3]
    row = lax.broadcasted_iota(jnp.int32, (16, LANES), 0)

    def put(source, here, line, size):
        whole[pl.ds(pl.multiple_of(line, 16), size), :] = source[pl.ds(pl.multiple_of(here, 16), size), :]

    def at(far_y, z, x, core):
        shard = (((my_y + far_y) & 3) << 3) + ((z & 1) << 2) + x
        line = first_tile(shard) << 4
        return shard & 7, line, line + PIECE * (2 * (z >> 1) + core)

    rows_of_y = 8 * SHARD_LINES
    for far_y in range(4):
        for other in range(2):
            core = (my_core + other) & 1
            for array, far_x in enumerate((0, 1, 3, 2)):
                array = 4 if array == 3 and far_y >= 2 else array
                source = sources[10 * other + array]

                def first(i, _, source=source, far_x=far_x, far_y=far_y, core=core, array=array):
                    z, x = (my_z + i) & 3, (my_x + far_x) & 3
                    shard, start, line = at(far_y, z, x, core)
                    here = (4 * (far_y - 2 * (array == 4)) + i) * 208
                    put(source, here + 16, line + 16, 192)

                    @pl.when(line == start)
                    def _():
                        edges[0, shard] = source[pl.ds(pl.multiple_of(here, 16), 16), :]

                    @pl.when(line != start)
                    def _():
                        put(source, here, line, 16)

                    return 0

                lax.fori_loop(0, 4, first, 0, unroll=True)

            array = (0, 1, 3, 2)[far_y]
            for skip, array in ((0, array), (8, array)) if array < 3 else ((0, 3), (8, 4)):
                source = sources[10 * other + 5 + array]

                def second(i, _, source=source, far_y=far_y, core=core, skip=skip, array=array):
                    x, z = (my_x + ((i + skip) >> 2)) & 3, (my_z + (i & 3)) & 3
                    shard, start, line = at(far_y, z, x, core)
                    here = (i + (skip if array < 3 else 0)) * 208
                    put(source, here, line + 208, 160)

                    @pl.when(line == start + 3 * PIECE)
                    def _():
                        last = jnp.where((x == 1) | (x == 2), 160, 144)
                        edges[1, shard] = source[pl.ds(pl.multiple_of(here + last, 16), 16), :]

                    @pl.when(line != start + 3 * PIECE)
                    def _():
                        put(source, here + 160, line + 368, 48)

                    return 0

                lax.fori_loop(0, 8, second, 0, unroll=4)
        base = pl.multiple_of(rows_of_y * ((my_y + far_y) & 3), 16)
        for shard in range(8):
            x = shard % 4
            tile = real(edges[0, shard])
            if x:
                tile = jnp.where(row < (12 * x) % 16, real(edges[1, shard - 1]), tile)
            whole[pl.ds(pl.multiple_of(base + 16 * ((403 * shard) // 4), 16), 16), :] = low(tile)
        pltpu.make_async_copy(whole.at[pl.ds(base, rows_of_y)], out.at[pl.ds(base, rows_of_y)], sem.at[far_y]).start()
    for far_y in range(4):
        pltpu.make_async_copy(whole.at[pl.ds(0, rows_of_y)], out.at[pl.ds(0, rows_of_y)], sem.at[far_y]).wait()


def unpack(pos, pieces):
    hbm, vmem = pl.BlockSpec(memory_space=pl.ANY), pl.BlockSpec(memory_space=pltpu.VMEM)
    return pl.pallas_call(
        unpack_kernel,
        out_shape=jax.ShapeDtypeStruct((LINES, LANES), jnp.bfloat16),
        in_specs=[pl.BlockSpec(memory_space=pltpu.SMEM)] + [vmem] * 20,
        out_specs=hbm,
        scratch_shapes=[
            pltpu.VMEM((LINES, LANES), jnp.bfloat16),
            pltpu.VMEM((2, 8, 16, LANES), jnp.bfloat16),
            pltpu.SemaphoreType.DMA((4,)),
        ],
        compiler_params=pltpu.CompilerParams(vmem_limit_bytes=30 * 2**20),
        cost_estimate=pl.CostEstimate(flops=0, bytes_accessed=27_000_000, transcendentals=0),
        name="unpack_weights",
    )(pos, *pieces)


def own_update_kernel(where, scales, squares, piece, master, moment_one, moment_two, out):
    start, turn = where[0], where[1]
    total = jnp.sum(squares[...], axis=1, keepdims=True)
    clipped = piece[...] * (MAX_NORM / jnp.maximum(jnp.sqrt(total), MAX_NORM))

    def lines(ref):
        return pltpu.roll(ref[pl.ds(start, PIECE), :], turn, 0)

    out[...] = low(adam_step(clipped, lines(master), lines(moment_one), lines(moment_two), scales[0], scales[1])[2])


def own_update(offset, scales, squares, piece, master, moment_one, moment_two):
    start = jnp.clip(offset, 0, SHARD_LINES - PIECE)
    where = jnp.stack([start, (start - offset + PIECE) % PIECE]).astype(jnp.int32)
    smem, vmem = pl.BlockSpec(memory_space=pltpu.SMEM), pl.BlockSpec(memory_space=pltpu.VMEM)
    return pl.pallas_call(
        own_update_kernel,
        out_shape=jax.ShapeDtypeStruct((PIECE, LANES), jnp.bfloat16),
        in_specs=[smem, smem] + [vmem] * 5,
        out_specs=vmem,
        compiler_params=pltpu.CompilerParams(vmem_limit_bytes=16 * 2**20),
        name="own_update",
    )(where, scales, squares, piece, *[v.reshape(SHARD_LINES, LANES) for v in (master, moment_one, moment_two)])


SPAN = 256
MICRO = 2
GROUPS = 8
ROWS = 256
F32 = jnp.float32


def nt(left, right, precision=None):
    return lax.dot_general(left, right, (((1,), (1,)), ((), ())), precision=precision, preferred_element_type=F32)


def tn(left, right, precision=None):
    return lax.dot_general(left, right, (((0,), (0,)), ((), ())), precision=precision, preferred_element_type=F32)


def nn(left, right, precision=None):
    return lax.dot_general(left, right, (((1,), (0,)), ((), ())), precision=precision, preferred_element_type=F32)


def sigmoid(v):
    return 0.5 + 0.5 * jnp.tanh(0.5 * v)


def iota(shape, dim):
    return lax.broadcasted_iota(jnp.int32, shape, dim)


def shifts(marks, first, length, step, offset, columns=slice(0, SPAN)):
    parts = []
    for d in range(1, 4):
        hit = iota((length, SPAN), 0) == iota((length, SPAN), 1) + step * d + offset
        parts.append(jnp.where(hit, marks[first + d - 1 : first + d, :], 0.0)[:, columns])
    return low(jnp.concatenate(parts, axis=1))


def by_head(ref, r):
    rows = [jnp.broadcast_to(ref[pl.ds(4 * r + k, 1), :], (HDIM, ref.shape[1])) for k in range(4)]
    return jnp.concatenate(rows, axis=0)


def put_head_sums(ref, r, block):
    for k in range(4):
        ref[pl.ds(4 * r + k, 1), :] = jnp.sum(block[k * HDIM : (k + 1) * HDIM], axis=0, keepdims=True)


def chunk(r):
    return pl.ds(pl.multiple_of(r * ROWS, ROWS), ROWS)


def set_up_kernel(
    place, tokens, segments, gain, kernel, bias, heads, gate_gain, normed, marks, taps, steps, coef, table
):
    x = real(tokens[...])
    factor = lax.rsqrt(jnp.mean(x * x, axis=1, keepdims=True) + EPSILON)
    for t in range(D // LANES):
        part = slice(t * LANES, (t + 1) * LANES)
        normed[:, part] = low(x[:, part] * factor * real(gain[t : t + 1, :]))

    first = place[0] * SPAN
    lane = iota((1, SPAN), 1)
    for m in range(MICRO):
        part = slice(m * SPAN, (m + 1) * SPAN)
        here = segments[m, :, pl.ds(pl.multiple_of(first, SPAN), SPAN)]
        left = segments[m, :, pl.ds(pl.multiple_of(jnp.maximum(first - LANES, 0), LANES), LANES)]
        right = segments[m, :, pl.ds(pl.multiple_of(jnp.minimum(first + SPAN, 3 * SPAN), LANES), LANES)]
        here, left, right = real(here), real(left), real(right)
        left = jnp.where(place[0] > 0, left, -1.0)
        right = jnp.where(place[0] < 3, right, -1.0)
        left, right = jnp.concatenate([left, left], axis=1), jnp.concatenate([right, right], axis=1)
        rows = []
        for d in range(1, 4):
            before = jnp.where(lane < d, pltpu.roll(left, d, 1), pltpu.roll(here, d, 1))
            rows.append(before == here)
        for d in range(1, 4):
            after = pltpu.roll(here, SPAN - d, 1)
            rows.append(jnp.where(lane >= SPAN - d, pltpu.roll(right, SPAN - d, 1), after) == here)
        prior, final = left[:, LANES - 1 : LANES], here[:, SPAN - 1 :]
        rows += [here == prior, here == final, jnp.broadcast_to(final == prior, here.shape)]
        rows = [row.astype(F32) for row in rows] + [here] + [jnp.zeros((1, SPAN), F32)] * 6
        marks[:, part] = jnp.concatenate(rows, axis=0)

    def columns(rows):
        return jnp.transpose(jnp.concatenate(rows + [jnp.zeros((8 - len(rows), LANES), F32)], axis=0))

    for t in range(CH // LANES):
        part = slice(t * LANES, (t + 1) * LANES)
        rows = [real(kernel[k : k + 1, part]) for k in range(4)] + [real(bias[t : t + 1, :])]
        taps[part, :] = columns(rows)
    steps[...] = columns([heads[0:1, :], jnp.exp(heads[1:2, :])])[0:HEADS, :]
    pick = (iota((LANES, DI), 1) >> 6 == iota((LANES, DI), 0)).astype(F32)
    table[...] = nn(jnp.broadcast_to(heads[2:3, :], (8, LANES)), pick, lax.Precision.HIGHEST)
    for t in range(DI // LANES):
        part = slice(t * LANES, (t + 1) * LANES)
        coef[part, :] = columns([real(gate_gain[t : t + 1, :]), table[0:1, part]])


def products_kernel(gate_weight, out_weight, normed, cotangent, gate, grad_mixed):
    gate[...] = nt(gate_weight[...], normed[...])
    grad_mixed[...] = nt(out_weight[...], cotangent[...])


def prepare_kernel(
    weight, step_weight, normed, rim, gain, taps, steps, marks,
    ci, conv, signal, inflow, maps, raw, cum, step, cols, local, through, state, move, enter, edge
):
    r = pl.program_id(0)
    parts = [slice(m * SPAN, (m + 1) * SPAN) for m in range(MICRO)]

    @pl.when(r == 0)
    def _():
        x = real(rim[...])
        factor = lax.rsqrt(jnp.mean(x * x, axis=1, keepdims=True) + EPSILON)
        for t in range(D // LANES):
            part = slice(t * LANES, (t + 1) * LANES)
            edge[:, part] = low(x[:, part] * factor * real(gain[t : t + 1, :]))
        raw[...] = nt(step_weight[...], normed[...])
        step[...] = jax.nn.softplus(raw[...] + steps[:, 0:1])
        upto = (iota((SPAN, SPAN), 0) <= iota((SPAN, SPAN), 1)).astype(F32)
        for m, part in enumerate(parts):
            here = marks[:, part]
            move[m] = shifts(here, 0, SPAN, -1, 0)
            enter[m] = shifts(here, 0, 16, -1, 16, slice(0, LANES))
            decay = -step[:, part] * steps[:, 1:2]
            total = nn(decay, upto, lax.Precision.HIGHEST)
            cum[:, part] = total
            column = lax.dot_general(
                upto, decay, (((0,), (1,)), ((), ())), precision=lax.Precision.HIGHEST, preferred_element_type=F32
            )
            for g in range(GROUPS):
                cols[g, part, :] = column[:, 4 * g : 4 * g + 4]
            ends = total[:, SPAN - 1 :]
            state[:, part] = here[7:8, :] * jnp.exp(ends - total)
            through[m] = jnp.broadcast_to(here[8:9, 0:1] * jnp.exp(ends), (HEADS, LANES))

    x = low(nt(weight[...], normed[...]))
    ci[...] = x
    halo = low(nt(weight[...], edge[...]))
    flows = []
    for m, part in enumerate(parts):
        moved = nn(x[:, part], move[m])
        edges = nn(halo[:, 16 * m : 16 * m + 16], enter[m])
        total = taps[:, 4:5] + real(x[:, part]) * taps[:, 3:4]
        border = 0.0
        for d in range(1, 4):
            tap = taps[:, 3 - d : 4 - d]
            total = total + moved[:, (d - 1) * SPAN : d * SPAN] * tap
            border = border + edges[:, (d - 1) * LANES : d * LANES] * tap
        total = jnp.concatenate([total[:, :LANES] + border, total[:, LANES:]], axis=1)
        conv[:, part] = total
        flows.append(total * sigmoid(total))

    @pl.when(r == 0)
    def _():
        for flow, part in zip(flows, parts):
            maps[:, part] = flow

    @pl.when(r > 0)
    def _():
        for m, (flow, part) in enumerate(zip(flows, parts)):
            signal[:, part] = low(flow)
            heads = by_head(step, r - 1)[:, part]
            tails = by_head(state, r - 1)[:, part]
            flow = flow * heads
            inflow[:, part] = low(flow)
            local[m] = low(nt(low(flow * tails), low(maps[0:LANES, part])))


def turn_kernel(normed, upstream, left, cot, turned):
    for t in range(4):
        part = slice(t * LANES, (t + 1) * LANES)
        turned[...] = jnp.transpose(real(normed[part, :]))
        for k in range(4):
            left[256 * k : 256 * (k + 1), part] = low(turned[pl.ds(k, 256, stride=4), :])
    cot[...] = low(pltpu.roll(real(upstream[...]), D - 32, 1))


def same_document(marks):
    column = jnp.transpose(jnp.broadcast_to(marks[9:10, :], (8, SPAN)))[:, 0:1]
    return (column == marks[9:10, :]) & (iota((SPAN, SPAN), 0) <= iota((SPAN, SPAN), 1))


def mixing(maps, marks):
    products = tn(maps[0:LANES, :], maps[LANES:, :], lax.Precision.HIGHEST)
    return jnp.where(same_document(marks), products, 0.0)


def within_kernel(inflow, maps, cum, cols, marks, out, table):
    table[...] = mixing(maps, marks)
    half = SPAN // 2

    def heads(g, _):
        results = []
        x4 = inflow[chunk(g), :]
        for h in range(4):
            row, col = cum[pl.ds(4 * g + h, 1), :], cols[g, :, h : h + 1]
            upper = low(jnp.exp(jnp.minimum(row - col[:half], 0.0)) * table[:half, :])
            lower = low(jnp.exp(jnp.minimum(row[:, half:] - col[half:], 0.0)) * table[half:, half:])
            x = x4[h * HDIM : (h + 1) * HDIM, :]
            y = nn(x[:, :half], upper)
            results.append(jnp.concatenate([y[:, :half], y[:, half:] + nn(x[:, half:], lower)], axis=1))
        out[chunk(g), :] = jnp.concatenate(results, axis=0)
        return 0

    lax.fori_loop(0, GROUPS, heads, 0, unroll=4)


def gate_kernel(
    inside, enter, last, maps, signal, gate, grad, cum, marks, coef,
    gated_low, grad_gate, grad_scan, carried_sum, skip_sum, gain_sum, grad_state, grad_read, scan, entry
):
    entry[...] = marks[6:7, :] * jnp.exp(cum[...])
    reads = low(maps[LANES:, :])

    @pl.when(pl.program_id(0) == 0)
    def _():
        gain_sum[...] = jnp.zeros_like(gain_sum)

    def forward(r, sums):
        carried = nn(enter[0, chunk(r), :] + last[0, chunk(r), :], reads) * by_head(entry, r)
        total = inside[chunk(r), :] + carried + coef[chunk(r), 1:2] * real(signal[chunk(r), :])
        scan[chunk(r), :] = total
        z = gate[chunk(r), :]
        gated = total * (z * sigmoid(z))
        up = grad[chunk(r), :] * coef[chunk(r), 0:1]
        squares, cross = sums
        return (
            squares + jnp.sum(gated * gated, axis=0, keepdims=True),
            cross + jnp.sum(gated * up, axis=0, keepdims=True),
        )

    nothing = jnp.zeros((1, SPAN), F32)
    squares, cross = lax.fori_loop(0, 8, forward, (nothing, nothing), unroll=4)
    factor = lax.rsqrt(squares * (1.0 / DI) + EPSILON)
    pull = factor * factor * cross * (1.0 / DI)
    grad_read[...] = jnp.zeros_like(grad_read)

    def backward(r, _):
        heads = by_head(entry, r)
        state = enter[0, chunk(r), :] + last[0, chunk(r), :]
        carried = nn(state, reads) * heads
        total = scan[chunk(r), :]
        z = gate[chunk(r), :]
        sig = sigmoid(z)
        soft = z * sig
        gated = total * soft
        scaled = gated * factor
        gain = coef[chunk(r), 0:1]
        given = grad[chunk(r), :]
        gated_low[chunk(r), :] = low(scaled * gain)
        share = given * scaled
        gain_sum[chunk(r), :] += share[:, :LANES] + share[:, LANES:]
        back = factor * (given * gain - gated * pull)
        grad_gate[chunk(r), :] = low(back * total * (sig * (1.0 + z * (1.0 - sig))))
        push = back * soft
        grad_scan[chunk(r), :] = low(push)
        put_head_sums(carried_sum, r, push * carried)
        put_head_sums(skip_sum, r, push * real(signal[chunk(r), :]))
        entering = low(push * heads)
        grad_state[0, chunk(r), :] = low(nt(entering, reads))
        grad_read[...] += tn(state, entering)
        return 0

    lax.fori_loop(0, 8, backward, 0, unroll=4)


def within_back_kernel(
    inflow, push, inside, maps, cum, cols, marks, grad_inflow, decay_sum, grad_maps, table, grad_table
):
    table[...] = mixing(maps, marks)
    grad_table[...] = jnp.zeros_like(grad_table)
    half = SPAN // 2

    def heads(g, _):
        x4, d4, results = inflow[chunk(g), :], push[chunk(g), :], []
        above, below = 0.0, 0.0
        for h in range(4):
            rows = slice(h * HDIM, (h + 1) * HDIM)
            row, col = cum[pl.ds(4 * g + h, 1), :], cols[g, :, h : h + 1]
            upper = jnp.exp(jnp.minimum(row - col[:half], 0.0))
            lower = jnp.exp(jnp.minimum(row[:, half:] - col[half:], 0.0))
            x, d = x4[rows, :], d4[rows, :]
            above += upper * tn(x[:, :half], d)
            below += lower * tn(x[:, half:], d[:, half:])
            first = nt(d, low(upper * table[:half, :]))
            second = nt(d[:, half:], low(lower * table[half:, half:]))
            results.append(jnp.concatenate([first, second], axis=1))
        grad_table[:half, :] += above
        grad_table[half:, half:] += below
        back = jnp.concatenate(results, axis=0)
        grad_inflow[chunk(g), :] = low(back)
        put_head_sums(decay_sum, g, real(d4) * inside[chunk(g), :] - real(x4) * back)
        return 0

    lax.fori_loop(0, GROUPS, heads, 0, unroll=4)
    spread = low(jnp.where(same_document(marks), grad_table[...], 0.0))
    grad_maps[0:LANES, :] = nt(low(maps[LANES:, :]), spread)
    grad_maps[LANES:, :] = nn(low(maps[0:LANES, :]), spread)


def state_back_kernel(
    leave, leave_last, enter, enter_last, conv, push, grad_inflow, maps, cum, step, raw, decay_sum, carried_sum, grad_maps, grad_read,
    steps, marks, coef, grad_conv, rim, grad_raw, bias_sum, rate_sum, tail, from_tail, from_step, crossing, grad_write
):
    ends = cum[:, SPAN - 1 : SPAN]
    tail[...] = marks[7:8, :] * jnp.exp(ends - cum[...])
    writes = low(maps[0:LANES, :])
    front = ((iota((16, SPAN), 1) == iota((16, SPAN), 0)) & (iota((16, SPAN), 0) < 3)).astype(jnp.bfloat16)
    grad_write[...] = grad_maps[0:LANES, :]

    def through_silu(r, c, sig, above):
        given = above * (sig * (1.0 + c * (1.0 - sig)))
        given = low(given)
        grad_conv[chunk(r), :] = given
        rim[0, :, chunk(r)] = low(nt(front, given))

    def channels(r, _):
        c = conv[chunk(r), :]
        sig = sigmoid(c)
        signal = c * sig
        heads, tails = by_head(step, r), by_head(tail, r)
        x = signal * heads
        back = leave[0, chunk(r), :] + leave_last[0, chunk(r), :]
        ended = nn(back, writes) * tails
        whole = real(grad_inflow[chunk(r), :]) + ended
        grad_write[...] += tn(back, low(x * tails))
        put_head_sums(from_tail, r, x * ended)
        put_head_sums(from_step, r, whole * signal)
        put_head_sums(crossing, r, real(back) * real(enter[0, chunk(r), :] + enter_last[0, chunk(r), :]))
        through_silu(r, c, sig, whole * heads + coef[chunk(r), 1:2] * real(push[chunk(r), :]))
        return 0

    lax.fori_loop(0, 8, channels, 0, unroll=4)
    c = conv[chunk(8), :]
    through_silu(8, c, sigmoid(c), jnp.concatenate([grad_write[...], grad_maps[LANES:, :] + grad_read[...]], axis=0))
    last = iota((HEADS, SPAN), 1) == SPAN - 1
    passing = marks[8:9, 0:1] * jnp.exp(ends) * jnp.sum(crossing[...], axis=1, keepdims=True)
    tails = jnp.sum(from_tail[...], axis=1, keepdims=True)
    total = decay_sum[...] + carried_sum[...] - from_tail[...] + jnp.where(last, tails + passing, 0.0)
    onward = (iota((SPAN, SPAN), 0) >= iota((SPAN, SPAN), 1)).astype(F32)
    grad_decay = nn(total, onward, lax.Precision.HIGHEST)
    rate = steps[:, 1:2]
    rate_sum[...] = -grad_decay * step[...] * rate
    grad_step = (from_step[...] - grad_decay * rate) * sigmoid(raw[...] + steps[:, 0:1])
    bias_sum[...] = grad_step
    grad_raw[0:HEADS, :] = low(grad_step)
    grad_raw[HEADS:, :] = jnp.zeros((LANES - HEADS, SPAN), jnp.bfloat16)


def conv_back_kernel(grad_conv, ci, rim, taps, marks, grad_ci, sums, move, enter):
    @pl.when(pl.program_id(0) == 0)
    def _():
        for m in range(MICRO):
            here = marks[:, m * SPAN : (m + 1) * SPAN]
            move[m] = shifts(here, 3, SPAN, 1, 0)
            enter[m] = shifts(here, 3, 16, 1, -SPAN, slice(LANES, SPAN))

    totals = [0.0] * 5
    for m in range(MICRO):
        part = slice(m * SPAN, (m + 1) * SPAN)
        given, x = real(grad_conv[:, part]), real(ci[:, part])
        moved = nn(grad_conv[:, part], move[m])
        edges = tn(rim[m], enter[m])
        back = given * taps[:, 3:4]
        totals[3] += given * x
        totals[4] += given
        for d in range(1, 4):
            sooner = moved[:, (d - 1) * SPAN : d * SPAN]
            last = sooner[:, LANES:] + edges[:, (d - 1) * LANES : d * LANES]
            sooner = jnp.concatenate([sooner[:, :LANES], last], axis=1)
            back += sooner * taps[:, 3 - d : 4 - d]
            totals[3 - d] += sooner * x
        grad_ci[:, part] = low(back)
    count = jnp.zeros((ROWS, LANES), F32)
    for k in range(5):
        pick = (iota((LANES, LANES), 1) == k).astype(jnp.bfloat16)
        count += nn(low(totals[k][:, :LANES] + totals[k][:, LANES:]), pick)
    sums[...] = count[:, 0:8]


def call(kernel, grid, ins, outs, scratch, cost, name, mebibytes):
    return pl.pallas_call(
        kernel,
        grid=grid,
        in_specs=[pl.BlockSpec(block, where) for _, block, where in ins],
        out_specs=[pl.BlockSpec(block, where) for _, _, block, where in outs],
        out_shape=[jax.ShapeDtypeStruct(shape, dtype) for shape, dtype, _, _ in outs],
        scratch_shapes=scratch,
        compiler_params=pltpu.CompilerParams(
            vmem_limit_bytes=mebibytes * 2**20, dimension_semantics=("arbitrary",) * len(grid)
        ),
        cost_estimate=pl.CostEstimate(flops=cost, bytes_accessed=20_000_000, transcendentals=0),
        name=name,
    )(*[array for array, _, _ in ins])


def neighbours(value, source, target):
    return lax.ppermute(value, GROUP, [(source, target)])


def chained(local, through, order, beside):
    by_heads = (MICRO, HEADS, HDIM, STATE)

    def joined(arrived):
        total = through[:, :, None, :] * real(arrived).reshape(by_heads) + real(local).reshape(by_heads)
        return low(total).reshape(local.shape)

    one = neighbours(local, order[0], order[1])
    two = neighbours(joined(one), order[1], order[2])
    two, beside = lax.optimization_barrier((two, beside))
    three = neighbours(joined(two), order[2], order[3])
    return (one + two, three), beside


def shards(
    tokens, segments, cotangent, norm_gain, in_weight, conv_kernel, conv_bias, step_bias, decay_log,
    skip_gain, gate_gain, out_weight, master, moment_one, moment_two, step_count
):
    width = MICRO * SPAN
    bf16 = jnp.bfloat16
    spot = position()
    place = lax.axis_index(GROUP)
    one = (MICRO,)
    by_m = lambda m: (0, m)
    whole, first = lambda m: (0, 0), lambda m: (m, 0, 0)
    upstream = cotangent.reshape(width, D)
    turned_weight = in_weight.T
    conv_weight = turned_weight[DI : DI + CH]

    heads = jnp.stack([real(step_bias), real(decay_log), real(skip_gain)])
    heads = jnp.pad(heads, ((0, 5), (0, LANES - HEADS)))
    lines = [v.reshape(-1, LANES) for v in (norm_gain, conv_bias, gate_gain)]
    ins = [tokens.reshape(width, D), segments, lines[0], conv_kernel, lines[1], heads, lines[2]]
    outs = [((width, D), bf16), ((16, width), F32), ((CH, 8), F32), ((HEADS, 8), F32), ((DI, 8), F32)]
    at_start = lambda rank: lambda i: (0,) * rank
    normed_low, marks, taps, steps, coef = pl.pallas_call(
        set_up_kernel,
        grid=(1,),
        out_shape=[jax.ShapeDtypeStruct(*out) for out in outs],
        in_specs=[pl.BlockSpec(memory_space=pltpu.SMEM)] + [pl.BlockSpec(v.shape, at_start(v.ndim)) for v in ins],
        out_specs=[pl.BlockSpec(shape, at_start(len(shape))) for shape, _ in outs],
        scratch_shapes=[pltpu.VMEM((8, DI), F32)],
        compiler_params=pltpu.CompilerParams(vmem_limit_bytes=56 * 2**20),
        name="set_up",
    )(place.reshape(1), *ins)
    mark_in = (marks, (16, SPAN), by_m)
    rim_tokens, normed_low = lax.optimization_barrier((tokens[:, 0, SPAN - 16 :, :], normed_low))
    rim_tokens = lax.ppermute(rim_tokens, GROUP, [(0, 1), (1, 2), (2, 3)])

    whole1, head_rows = lambda r: (0, 0), lambda r: (jnp.maximum(r - 1, 0), 0)
    rows_of = lambda r: jnp.where(r == 0, GROUPS, r - 1)
    by_rows = lambda r: (rows_of(r), 0)
    lot = (HEADS, width)
    ci, conv, signal, inflow, maps, raw, cum, step, cols, local, through = call(
        prepare_kernel, (CH // ROWS,),
        [(turned_weight, (ROWS, D), lambda r: (GROUPS + rows_of(r), 0)),
         (turned_weight, (HEADS, D), lambda r: ((DI + CH) // HEADS, 0)), (normed_low, (width, D), whole1),
         (rim_tokens.reshape(-1, D), (32, D), whole1), (lines[0], lines[0].shape, whole1), (taps, (ROWS, 8), by_rows), (steps, (HEADS, 8), whole1),
         (marks, (16, width), whole1)],
        [((CH, width), bf16, (ROWS, width), by_rows), ((CH, width), F32, (ROWS, width), by_rows),
         ((DI, width), bf16, (ROWS, width), head_rows), ((DI, width), bf16, (ROWS, width), head_rows),
         ((2 * STATE, width), F32, (2 * STATE, width), whole1), (lot, F32, lot, whole1), (lot, F32, lot, whole1),
         (lot, F32, lot, whole1), ((GROUPS, width, 4), F32, (GROUPS, width, 4), lambda r: (0, 0, 0)),
         ((MICRO, DI, STATE), bf16, (MICRO, ROWS, STATE), lambda r: (0, jnp.maximum(r - 1, 0), 0)),
         ((MICRO, HEADS, LANES), F32, (MICRO, HEADS, LANES), lambda r: (0, 0, 0))],
        [pltpu.VMEM(lot, F32), pltpu.VMEM((MICRO, SPAN, 3 * SPAN), bf16), pltpu.VMEM((MICRO, 16, 3 * LANES), bf16),
         pltpu.VMEM((32, D), bf16)],
        10**9, "project_and_convolve", 56,
    )

    tiles = lambda r: (r, 0)
    gate, grad_mixed = call(
        products_kernel, (GROUPS // 2,),
        [(turned_weight, (2 * ROWS, D), tiles), (out_weight, (2 * ROWS, D), tiles), (normed_low, (width, D), whole1),
         (upstream, (width, D), whole1)],
        [((DI, width), F32, (2 * ROWS, width), tiles)] * 2, [], 4 * 10**9, "gate_products", 24,
    )
    tall, few = (DI, SPAN), (HEADS, SPAN)
    state_block = (1, DI, STATE)
    head_ins = [
        (maps, (2 * STATE, SPAN), by_m),
        (cum, few, by_m),
        (cols, (GROUPS, SPAN, 4), lambda m: (0, m, 0)),
        mark_in,
    ]
    table = pltpu.VMEM((SPAN, SPAN), F32)
    (inside,) = call(
        within_kernel, one, [(inflow, tall, by_m)] + head_ins, [((DI, width), F32, tall, by_m)], [table],
        4 * 10**9, "within_blocks", 24,
    )
    enter, (inside, gate, grad_mixed) = chained(local, through, (0, 1, 2, 3), (inside, gate, grad_mixed))

    gated_low, grad_gate, push, carried_sum, skip_sum, gain_sum, grad_state, grad_read = call(
        gate_kernel, one,
        [(inside, tall, by_m), (enter[0], state_block, first), (enter[1], state_block, first), (maps, (2 * STATE, SPAN), by_m), (signal, tall, by_m),
         (gate, tall, by_m), (grad_mixed, tall, by_m), (cum, (HEADS, SPAN), by_m), mark_in, (coef, (DI, 8), whole)],
        [((DI, width), bf16, tall, by_m), ((DI, width), bf16, tall, by_m), ((DI, width), bf16, tall, by_m),
         ((HEADS, width), F32, (HEADS, SPAN), by_m), ((HEADS, width), F32, (HEADS, SPAN), by_m),
         ((DI, LANES), F32, (DI, LANES), whole), ((MICRO, DI, STATE), bf16, state_block, first),
         ((STATE, width), F32, (STATE, SPAN), by_m)],
        [pltpu.VMEM((DI, SPAN), F32), pltpu.VMEM((HEADS, SPAN), F32)], 2 * 10**9, "gate_and_back", 50,
    )
    grad_inflow, decay_sum, grad_maps = call(
        within_back_kernel, one, [(inflow, tall, by_m), (push, tall, by_m), (inside, tall, by_m)] + head_ins,
        [((DI, width), bf16, tall, by_m), ((HEADS, width), F32, few, by_m),
         ((2 * STATE, width), F32, (2 * STATE, SPAN), by_m)],
        [table, table], 8 * 10**9, "within_blocks_back", 56,
    )
    left, cot = call(
        turn_kernel, (1,), [(normed_low, (width, D), whole), (upstream, (width, D), whole)],
        [((D, width), bf16, (D, width), whole), ((width, D), bf16, (width, D), whole)],
        [pltpu.VMEM((D, LANES), F32)], 10**6, "turn", 14,
    )
    leave, (grad_inflow, decay_sum, grad_maps, left, cot) = chained(
        grad_state, through, (3, 2, 1, 0), (grad_inflow, decay_sum, grad_maps, left, cot)
    )

    grad_conv, rim, grad_raw, bias_sum, rate_sum = call(
        state_back_kernel, one,
        [(leave[0], state_block, first), (leave[1], state_block, first), (enter[0], state_block, first),
         (enter[1], state_block, first), (conv, (CH, SPAN), by_m), (push, tall, by_m),
         (grad_inflow, tall, by_m), (maps, (2 * STATE, SPAN), by_m), (cum, few, by_m), (step, few, by_m), (raw, few, by_m),
         (decay_sum, few, by_m), (carried_sum, few, by_m), (grad_maps, (2 * STATE, SPAN), by_m),
         (grad_read, (STATE, SPAN), by_m), (steps, (HEADS, 8), whole), mark_in, (coef, (DI, 8), whole)],
        [((CH, width), bf16, (CH, SPAN), by_m), ((MICRO, 16, CH), bf16, (1, 16, CH), first),
         ((LANES, width), bf16, (LANES, SPAN), by_m), ((HEADS, width), F32, few, by_m), ((HEADS, width), F32, few, by_m)],
        [pltpu.VMEM(few, F32), pltpu.VMEM(few, F32), pltpu.VMEM(few, F32), pltpu.VMEM((HEADS, LANES), F32),
         pltpu.VMEM((STATE, SPAN), F32)], 10**9, "state_and_silu_back", 56,
    )
    next_rim = lax.ppermute(rim, GROUP, [(1, 0), (2, 1), (3, 2)])
    early = tn(grad_gate, turned_weight[:DI])
    next_rim, early = lax.optimization_barrier((next_rim, early))

    by_r = lambda r: (r, 0)
    grad_ci, tap_sums = call(
        conv_back_kernel, (CH // ROWS,),
        [(grad_conv, (ROWS, width), by_r), (ci, (ROWS, width), by_r), (next_rim, (MICRO, 16, ROWS), lambda r: (0, 0, r)),
         (taps, (ROWS, 8), by_r), (marks, (16, width), lambda r: (0, 0))],
        [((CH, width), bf16, (ROWS, width), by_r), ((CH, 8), F32, (ROWS, 8), by_r)],
        [pltpu.VMEM((MICRO, SPAN, 3 * SPAN), bf16), pltpu.VMEM((MICRO, 16, 3 * LANES), bf16)], 10**8, "convolution_back", 56,
    )

    middle = [tap_sums[:, :5].T.reshape(-1), jnp.sum(bias_sum, axis=1), jnp.sum(rate_sum, axis=1)]
    middle += [jnp.sum(skip_sum, axis=1), jnp.sum(gain_sum, axis=1), jnp.zeros((32 + 5 * LANES,), F32)]
    middle = jnp.concatenate(middle).reshape(-1, LANES)
    packed = pack(spot, left, grad_gate, grad_ci, grad_raw, gated_low, cot, middle)
    packed, late = lax.optimization_barrier((packed, (grad_gate, grad_ci, grad_raw)))
    rows_in = real(tokens.reshape(width, D))
    norm_back = jax.vjp(norm_piece, rows_in, real(norm_gain))[1]
    grad_normed = early + tn(late[1], conv_weight) + tn(late[2][:HEADS], turned_weight[DI + CH :])
    grad_rows, grad_norm_gain = norm_back(grad_normed)

    def finish(inputs):
        gated_low, grad_rows = inputs
        output = low(rows_in + tn(gated_low, out_weight)).reshape(tokens.shape)
        return output, low(real(upstream) + grad_rows).reshape(tokens.shape)

    piece, (output, input_grad) = reduce_pieces(
        *packed, grad_norm_gain.reshape(-1, LANES), finish, (gated_low, grad_rows)
    )

    skew = (12 * lax.axis_index("x")) % 16
    offset = PIECE * place - skew
    line = offset + iota((PIECE, 1), 0)
    own = jnp.where((line >= 0) & (line < SHARD_LINES), piece, 0.0)
    squares = sent_to_all(jnp.sum(own * own).reshape(1, 1), EVERY).reshape(1, -1)
    core, high = lax.axis_index("core") == 0, lax.axis_index("zh") == 0
    pair = [piece, swap_cores(piece)]
    pair = jnp.concatenate([jnp.where(core, *pair), jnp.where(core, *pair[::-1])])
    both = [pair, lax.ppermute(pair, "zh", [(0, 1), (1, 0)])]
    step_real = real(step_count[0])
    scales = jnp.stack([1.0 / (1.0 - jnp.power(BETA_ONE, step_real)), 1.0 / (1.0 - jnp.power(BETA_TWO, step_real))])
    both, squares = lax.optimization_barrier((both, squares))
    mine = own_update(offset, scales, squares, piece, master, moment_one, moment_two)

    def rest(inputs):
        both, squares, moments = inputs
        window = jnp.concatenate([jnp.where(high, *both), jnp.where(high, *both[::-1])])
        shard = lax.dynamic_slice(window, (skew, 0), (SHARD_LINES, LANES)).reshape(-1)
        clip_factor = MAX_NORM / jnp.maximum(jnp.sqrt(jnp.sum(squares)), MAX_NORM)
        return shard, adam_step(shard * clip_factor, *moments, scales[0], scales[1])

    moments = (master, moment_one, moment_two)
    pieces, (shard, results) = gather_pieces(mine, rest, (both, squares, moments))
    copies = unpack(spot, pieces).reshape(-1)
    return (output, input_grad, shard, *results, copies)


def solution(mesh):
    finer = Mesh(mesh.devices.reshape(4, 2, 4, 2, 2), ("y", "zl", "x", "zh", "core"))
    return jax.shard_map(
        shards,
        mesh=finer,
        in_specs=(
            P(None, DP, GROUP, None),
            P(None, DP, None),
            P(None, DP, GROUP, None),
            P(),
            P(),
            P(),
            P(),
            P(),
            P(),
            P(),
            P(),
            P(),
            P(DP),
            P(DP),
            P(DP),
            P(),
        ),
        out_specs=(
            P(None, DP, GROUP, None),
            P(None, DP, GROUP, None),
            P(DP),
            P(DP),
            P(DP),
            P(DP),
            P(),
        ),
        check_vma=False,
    )
```

```python
import functools

import jax
import jax.numpy as jnp
from jax import lax
from jax.experimental import pallas as pl
from jax.experimental.pallas import tpu as pltpu
from jax.sharding import Mesh
from jax.sharding import PartitionSpec as P

D = 1024
DI = 2048
HEADS = 32
HDIM = 64
STATE = 128
CH = 2304
DP = ("y", "zl", "x")
GROUP = ("zh", "core")
EVERY = DP + GROUP


EPSILON = 1e-05
BETA_ONE = 0.9
BETA_TWO = 0.95
ADAM_EPSILON = 1e-08
LEARN_RATE = 0.01
WEIGHT_DECAY = 0.1
MAX_NORM = 1.0


def sent_to_all(shard, axis):
    copies = jnp.broadcast_to(shard, (lax.axis_size(axis), *shard.shape))
    return lax.all_to_all(copies, axis, split_axis=0, concat_axis=0, tiled=True)


def norm_piece(values, scaling):
    factor = lax.rsqrt(jnp.mean(values * values, axis=-1, keepdims=True) + EPSILON)
    return values * factor * scaling


def adam_step(clipped, master, moment_one, moment_two, first_scale, second_scale):
    first_moment = BETA_ONE * moment_one + (1.0 - BETA_ONE) * clipped
    second_moment = BETA_TWO * moment_two + (1.0 - BETA_TWO) * clipped * clipped
    first_hat, second_hat = first_moment * first_scale, second_moment * second_scale
    updated = master - LEARN_RATE * (first_hat / (jnp.sqrt(second_hat) + ADAM_EPSILON) + WEIGHT_DECAY * master)
    return (first_moment, second_moment, updated)


LANES = 128
LINES = 51584
SHARD_LINES = 1612
IN_LINE = 8
MID_LINE = 35080
OUT_LINE = 35187
PIECE = 416
SLOTS = 16
PARTS = ((0, 208), (208, 208))
TAIL_LINES = 51632
GROUP_LINES = 137
RING = {"x": ("x",), "y": ("y",), "z": ("zl", "zh")}
ROUTES = (("x", "y", "z"), ("y", "x", "z"))


def ring_place(axis, i):
    i = i % 4
    return (i % 2) * 2 + i // 2 if axis == "z" else i


def from_offset(block, axis, distance):
    route = [(ring_place(axis, i + distance), ring_place(axis, i)) for i in range(4)]
    return lax.ppermute(block, RING[axis], route)


def swap_cores(block):
    return lax.ppermute(block, "core", [(0, 1), (1, 0)])


def position():
    z = 2 * lax.axis_index("zh") + lax.axis_index("zl")
    return jnp.stack([lax.axis_index("y"), z, lax.axis_index("x"), lax.axis_index("core")]).astype(jnp.int32)


def first_tile(shard):
    return (403 * shard) >> 2


def pack_kernel(pos, mid_part, *rest):
    sources, keep, send = rest[:6], rest[6], rest[7]
    flat, carry, edge, stage, sems = rest[8:13]
    left, grad_gate, grad_ci, grad_raw, gated, cot = held = rest[13:19]
    loads = [pltpu.make_async_copy(source, here, rest[19].at[k]) for k, (source, here) in enumerate(zip(sources, held))]
    for k in (4, 5, 0, 1, 2, 3):
        loads[k].start()
    lane = lax.broadcasted_iota(jnp.int32, (256, LANES), 1)

    flat[0:IN_LINE, :] = jnp.zeros((IN_LINE, LANES), jnp.float32)
    flat[MID_LINE : MID_LINE + 104, :] = mid_part[0:104, :]
    flat[MID_LINE + 104 : MID_LINE + 107, :] = mid_part[104:107, :]
    edge[0:8, :] = mid_part[99:107, :]

    def rows(b, _):
        block = gated[pl.ds(pl.multiple_of(b * 256, 256), 256), :]
        product = jnp.dot(block, cot[...], preferred_element_type=jnp.float32)
        start = OUT_LINE + 2048 * b
        for t in range(7):
            flat[pl.ds(start + t, 256, stride=8), :] = product[:, t * LANES : (t + 1) * LANES]
        last = product[:, 7 * LANES :]
        edge[8:264, :] = last
        flat[pl.ds(start - 1, 256, stride=8), :] = jnp.where(lane < 96, edge[7:263, :], last)
        edge[0:8, :] = edge[256:264, :]
        return 0

    loads[4].wait()
    loads[5].wait()
    lax.fori_loop(0, 8, rows, 0, unroll=2)
    low = lax.broadcasted_iota(jnp.int32, (1, LANES), 1) < 96
    flat[OUT_LINE + 16383 : TAIL_LINES, :] = jnp.zeros((TAIL_LINES - OUT_LINE - 16383, LANES), jnp.float32)
    flat[OUT_LINE + 16383 : OUT_LINE + 16384, :] = jnp.where(low, edge[7:8, :], 0.0)

    my_y, my_z, my_x, my_core = pos[0], pos[1], pos[2], pos[3]

    def drain(slot):
        pltpu.make_async_copy(stage.at[slot], keep.at[pl.ds(0, PIECE)], sems.at[slot]).wait()

    def ship(n, _):
        i = (n + 88) & 127
        slot = n & (SLOTS - 1)

        @pl.when(n >= SLOTS)
        def _():
            drain(slot)

        shard, quarter = i >> 2, i & 3
        line = 16 * first_tile(shard) + PIECE * quarter
        stage[slot] = flat[pl.ds(pl.multiple_of(line, 16), PIECE), :].astype(jnp.bfloat16)
        x, zl, y = shard & 3, (shard >> 2) & 1, shard >> 3
        core = quarter & 1
        z = 2 * (quarter >> 1) + zl
        off = {"y": (y - my_y) & 3, "z": (z - my_z) & 3, "x": (x - my_x) & 3}
        for p, (start, size) in enumerate(PARTS):
            a, b, c = (off[axis] for axis in ROUTES[p])
            to = pl.ds(pl.multiple_of((((4 * p + a) * 4 + b) * 4 + c) * size, 16), size)
            source = stage.at[slot, pl.ds(start, size)]

            @pl.when(core == my_core)
            def _():
                pltpu.make_async_copy(source, keep.at[to], sems.at[slot]).start()

            @pl.when(core != my_core)
            def _():
                pltpu.make_async_copy(source, send.at[to], sems.at[slot]).start()

        return 0

    lax.fori_loop(0, 40, ship, 0)

    def put(tile, k, line):
        moved = pltpu.roll(tile, 32 * k, 1) if k else tile
        whole = jnp.where(lane < 32 * k, carry[k], moved) if k else moved
        flat[pl.ds(IN_LINE + 34 * k + line, 256, stride=GROUP_LINES), :] = whole
        carry[k] = moved

    def columns(block, line, tiles):
        product = nt(left[...], block)
        for k in range(4):
            for t in range(tiles):
                put(product[256 * k : 256 * (k + 1), t * LANES : (t + 1) * LANES], k, line + t)

    def from_gate(j, _):
        columns(grad_gate[pl.ds(pl.multiple_of(j * 512, 512), 512), :], 4 * j, 4)
        return 0

    def from_conv(j, _):
        columns(grad_ci[pl.ds(pl.multiple_of(j * 512, 512), 512), :], 16 + 4 * j, 4)
        return 0

    loads[0].wait()
    loads[1].wait()
    lax.fori_loop(0, 4, from_gate, 0, unroll=2)
    loads[2].wait()
    loads[3].wait()
    lax.fori_loop(0, 4, from_conv, 0, unroll=2)
    heads = []
    for k in range(1, 4):
        heads.append(flat[pl.ds(IN_LINE + 34 * k, 256, stride=GROUP_LINES), :])
    columns(jnp.concatenate([grad_ci[2048:2304, :], grad_raw[...]], axis=0), 32, 3)
    for k in range(1, 4):
        at = pl.ds(IN_LINE + 34 * k, 256, stride=GROUP_LINES)
        flat[at, :] = jnp.where(lane < 32 * k, flat[at, :], heads[k - 1])

    lax.fori_loop(40, 128, ship, 0)
    for slot in range(SLOTS):
        drain(slot)


def pack(pos, left, grad_gate, grad_ci, grad_raw, gated, cot, mid_part):
    vmem, hbm = pl.BlockSpec(memory_space=pltpu.VMEM), pl.BlockSpec(memory_space=pl.ANY)
    shape = jax.ShapeDtypeStruct((64 * PIECE, LANES), jnp.bfloat16)
    return pl.pallas_call(
        pack_kernel,
        out_shape=[shape] * 2,
        in_specs=[pl.BlockSpec(memory_space=pltpu.SMEM)] + [vmem] + [hbm] * 6,
        out_specs=[hbm] * 2,
        scratch_shapes=[
            pltpu.VMEM((TAIL_LINES, LANES), jnp.float32),
            pltpu.VMEM((4, 256, LANES), jnp.float32),
            pltpu.VMEM((264, LANES), jnp.float32),
            pltpu.VMEM((SLOTS, PIECE, LANES), jnp.bfloat16),
            pltpu.SemaphoreType.DMA((SLOTS,)),
        ]
        + [pltpu.VMEM(v.shape, v.dtype) for v in (left, grad_gate, grad_ci, grad_raw, gated, cot)]
        + [pltpu.SemaphoreType.DMA((6,))],
        compiler_params=pltpu.CompilerParams(vmem_limit_bytes=60 * 2**20),
        cost_estimate=pl.CostEstimate(flops=7_000_000_000, bytes_accessed=25_000_000, transcendentals=0),
        name="pack_gradients",
    )(pos, mid_part, left, grad_gate, grad_ci, grad_raw, gated, cot)


def real(v):
    return v.astype(jnp.float32)


def low(v):
    return v.astype(jnp.bfloat16)


def to_offset(block, axis, distance):
    route = [(ring_place(axis, i), ring_place(axis, i + distance)) for i in range(4)]
    return lax.ppermute(block, RING[axis], route)


def quarters(block):
    return block.reshape(4, -1, LANES)


def ring_sum(block, axis):
    block = quarters(block)
    half = block.shape[1] // 32 * 16
    a, b = to_offset(block[2, :half], axis, 1), to_offset(block[2, half:], axis, 3)
    one = jnp.concatenate([low(real(block[1, :half]) + real(a)), block[1, half:]])
    three = jnp.concatenate([block[3, :half], low(real(block[3, half:]) + real(b))])
    return real(block[0]) + real(to_offset(one, axis, 1)) + real(to_offset(three, axis, 3))


def direct_sum(block, axis):
    block = quarters(block)
    moved = [to_offset(block[d], axis, d) for d in (1, 3, 2)]
    return real(block[0]) + real(moved[0]) + real(moved[1]) + real(moved[2])


def reduce_pieces(keep, send, gain_grad, beside, given):
    got = swap_cores(send)
    held = [low(real(mine) + real(other)) for mine, other in zip(jnp.split(keep, 2), jnp.split(got, 2))]
    gain_grad = low(gain_grad + swap_cores(gain_grad))
    x, y, z = lax.axis_index("x"), lax.axis_index("y"), 2 * lax.axis_index("zh") + lax.axis_index("zl")
    block = 16 * (-x & 3) + 4 * (-y & 3) + (-z & 3)
    lines = jnp.arange(16)[:, None]
    mine = (lines < IN_LINE) & (lax.axis_index("core") == 0)
    start = (block * PARTS[0][1], 0)
    tile = lax.dynamic_slice(held[0], start, (16, LANES))
    tile = jnp.where(mine, jnp.pad(gain_grad, ((0, 16 - IN_LINE), (0, 0))), tile)
    held[0] = lax.dynamic_update_slice(held[0], tile, start)
    held, given = lax.optimization_barrier((held, given))
    first, second = low(ring_sum(held[0], "x")), low(ring_sum(held[1], "y"))
    (first, second), done = lax.optimization_barrier(((first, second), beside(given)))
    first, second = low(direct_sum(first, "y")), low(direct_sum(second, "x"))
    both = jnp.concatenate([quarters(first), quarters(second)], axis=1).reshape(-1, LANES)
    return direct_sum(both, "z"), done


def join_kernel(*refs):
    *blocks, first, second = refs
    for out, parts in ((first, blocks[: len(blocks) // 2]), (second, blocks[len(blocks) // 2 :])):
        start = 0
        for block in parts:
            out[start : start + block.shape[0], :] = block[...]
            start += block.shape[0]


def join(first, second):
    vmem = pl.BlockSpec(memory_space=pltpu.VMEM)
    rows = [sum(block.shape[0] for block in parts) for parts in (first, second)]
    return pl.pallas_call(
        join_kernel,
        out_shape=[jax.ShapeDtypeStruct((n, LANES), jnp.bfloat16) for n in rows],
        in_specs=[vmem] * (len(first) + len(second)),
        out_specs=[vmem] * 2,
        compiler_params=pltpu.CompilerParams(vmem_limit_bytes=8 * 2**20),
        name="join",
    )(*first, *second)


def gather_pieces(piece, beside, given):
    def spread(block, axis):
        return [block] + [from_offset(block, axis, d) for d in (1, 3, 2)]

    def in_order(parts):
        return [parts[0], parts[1], parts[3], parts[2]]

    n = PARTS[0][1]
    both = spread(piece, "z")
    both = in_order(both)
    first = spread(jnp.concatenate([block[:n] for block in both]), "y")
    second = spread(jnp.concatenate([block[n:] for block in both]), "x")
    first, second = join(in_order(first), in_order(second))
    ends = [(first, "x"), (second, "y")]
    sides = [[from_offset(block, axis, d) for d in (1, 3)] for block, axis in ends]
    swapped = [swap_cores(block) for block, _ in ends]
    swapped, given = lax.optimization_barrier((swapped, given))
    sides, swapped, done = lax.optimization_barrier((sides, swapped, beside(given)))
    mine, other = [], []
    for (block, axis), (left, right), first in zip(ends, sides, swapped):
        half = block.shape[0] // 2
        halves = [from_offset(right[:half], axis, 3), from_offset(left[half:], axis, 1)]
        mine += [block, left, right, *halves]
        left, right, halves = lax.optimization_barrier((left, right, halves))
        other += [first] + [swap_cores(part) for part in (left, right, *halves)]
    return mine + other, done


def unpack_kernel(pos, *rest):
    sources, out = rest[:20], rest[20]
    whole, edges, sem = rest[21:]
    my_y, my_z, my_x, my_core = pos[0], pos[1], pos[2], pos[3]
    row = lax.broadcasted_iota(jnp.int32, (16, LANES), 0)

    def put(source, here, line, size):
        whole[pl.ds(pl.multiple_of(line, 16), size), :] = source[pl.ds(pl.multiple_of(here, 16), size), :]

    def at(far_y, z, x, core):
        shard = (((my_y + far_y) & 3) << 3) + ((z & 1) << 2) + x
        line = first_tile(shard) << 4
        return shard & 7, line, line + PIECE * (2 * (z >> 1) + core)

    rows_of_y = 8 * SHARD_LINES
    for far_y in range(4):
        for other in range(2):
            core = (my_core + other) & 1
            for array, far_x in enumerate((0, 1, 3, 2)):
                array = 4 if array == 3 and far_y >= 2 else array
                source = sources[10 * other + array]

                def first(i, _, source=source, far_x=far_x, far_y=far_y, core=core, array=array):
                    z, x = (my_z + i) & 3, (my_x + far_x) & 3
                    shard, start, line = at(far_y, z, x, core)
                    here = (4 * (far_y - 2 * (array == 4)) + i) * 208
                    put(source, here + 16, line + 16, 192)

                    @pl.when(line == start)
                    def _():
                        edges[0, shard] = source[pl.ds(pl.multiple_of(here, 16), 16), :]

                    @pl.when(line != start)
                    def _():
                        put(source, here, line, 16)

                    return 0

                lax.fori_loop(0, 4, first, 0, unroll=True)

            array = (0, 1, 3, 2)[far_y]
            for skip, array in ((0, array), (8, array)) if array < 3 else ((0, 3), (8, 4)):
                source = sources[10 * other + 5 + array]

                def second(i, _, source=source, far_y=far_y, core=core, skip=skip, array=array):
                    x, z = (my_x + ((i + skip) >> 2)) & 3, (my_z + (i & 3)) & 3
                    shard, start, line = at(far_y, z, x, core)
                    here = (i + (skip if array < 3 else 0)) * 208
                    put(source, here, line + 208, 160)

                    @pl.when(line == start + 3 * PIECE)
                    def _():
                        last = jnp.where((x == 1) | (x == 2), 160, 144)
                        edges[1, shard] = source[pl.ds(pl.multiple_of(here + last, 16), 16), :]

                    @pl.when(line != start + 3 * PIECE)
                    def _():
                        put(source, here + 160, line + 368, 48)

                    return 0

                lax.fori_loop(0, 8, second, 0, unroll=4)
        base = pl.multiple_of(rows_of_y * ((my_y + far_y) & 3), 16)
        for shard in range(8):
            x = shard % 4
            tile = real(edges[0, shard])
            if x:
                tile = jnp.where(row < (12 * x) % 16, real(edges[1, shard - 1]), tile)
            whole[pl.ds(pl.multiple_of(base + 16 * ((403 * shard) // 4), 16), 16), :] = low(tile)
        pltpu.make_async_copy(whole.at[pl.ds(base, rows_of_y)], out.at[pl.ds(base, rows_of_y)], sem.at[far_y]).start()
    for far_y in range(4):
        pltpu.make_async_copy(whole.at[pl.ds(0, rows_of_y)], out.at[pl.ds(0, rows_of_y)], sem.at[far_y]).wait()


def unpack(pos, pieces):
    hbm, vmem = pl.BlockSpec(memory_space=pl.ANY), pl.BlockSpec(memory_space=pltpu.VMEM)
    return pl.pallas_call(
        unpack_kernel,
        out_shape=jax.ShapeDtypeStruct((LINES, LANES), jnp.bfloat16),
        in_specs=[pl.BlockSpec(memory_space=pltpu.SMEM)] + [vmem] * 20,
        out_specs=hbm,
        scratch_shapes=[
            pltpu.VMEM((LINES, LANES), jnp.bfloat16),
            pltpu.VMEM((2, 8, 16, LANES), jnp.bfloat16),
            pltpu.SemaphoreType.DMA((4,)),
        ],
        compiler_params=pltpu.CompilerParams(vmem_limit_bytes=30 * 2**20),
        cost_estimate=pl.CostEstimate(flops=0, bytes_accessed=27_000_000, transcendentals=0),
        name="unpack_weights",
    )(pos, *pieces)


def own_update_kernel(where, scales, squares, piece, master, moment_one, moment_two, out):
    start, turn = where[0], where[1]
    total = jnp.sum(squares[...], axis=1, keepdims=True)
    clipped = piece[...] * (MAX_NORM / jnp.maximum(jnp.sqrt(total), MAX_NORM))

    def lines(ref):
        return pltpu.roll(ref[pl.ds(start, PIECE), :], turn, 0)

    out[...] = low(adam_step(clipped, lines(master), lines(moment_one), lines(moment_two), scales[0], scales[1])[2])


def own_update(offset, scales, squares, piece, master, moment_one, moment_two):
    start = jnp.clip(offset, 0, SHARD_LINES - PIECE)
    where = jnp.stack([start, (start - offset + PIECE) % PIECE]).astype(jnp.int32)
    smem, vmem = pl.BlockSpec(memory_space=pltpu.SMEM), pl.BlockSpec(memory_space=pltpu.VMEM)
    return pl.pallas_call(
        own_update_kernel,
        out_shape=jax.ShapeDtypeStruct((PIECE, LANES), jnp.bfloat16),
        in_specs=[smem, smem] + [vmem] * 5,
        out_specs=vmem,
        compiler_params=pltpu.CompilerParams(vmem_limit_bytes=16 * 2**20),
        name="own_update",
    )(where, scales, squares, piece, *[v.reshape(SHARD_LINES, LANES) for v in (master, moment_one, moment_two)])


SPAN = 256
MICRO = 2
GROUPS = 8
ROWS = 256
F32 = jnp.float32


def nt(left, right, precision=None):
    return lax.dot_general(left, right, (((1,), (1,)), ((), ())), precision=precision, preferred_element_type=F32)


def tn(left, right, precision=None):
    return lax.dot_general(left, right, (((0,), (0,)), ((), ())), precision=precision, preferred_element_type=F32)


def nn(left, right, precision=None):
    return lax.dot_general(left, right, (((1,), (0,)), ((), ())), precision=precision, preferred_element_type=F32)


def sigmoid(v):
    return 0.5 + 0.5 * jnp.tanh(0.5 * v)


def iota(shape, dim):
    return lax.broadcasted_iota(jnp.int32, shape, dim)


def shifts(marks, first, length, step, offset, columns=slice(0, SPAN)):
    parts = []
    for d in range(1, 4):
        hit = iota((length, SPAN), 0) == iota((length, SPAN), 1) + step * d + offset
        parts.append(jnp.where(hit, marks[first + d - 1 : first + d, :], 0.0)[:, columns])
    return low(jnp.concatenate(parts, axis=1))


def by_head(ref, r):
    rows = [jnp.broadcast_to(ref[pl.ds(4 * r + k, 1), :], (HDIM, ref.shape[1])) for k in range(4)]
    return jnp.concatenate(rows, axis=0)


def put_head_sums(ref, r, block):
    for k in range(4):
        ref[pl.ds(4 * r + k, 1), :] = jnp.sum(block[k * HDIM : (k + 1) * HDIM], axis=0, keepdims=True)


def chunk(r):
    return pl.ds(pl.multiple_of(r * ROWS, ROWS), ROWS)


def set_up_kernel(
    place, tokens, segments, gain, kernel, bias, heads, gate_gain, normed, marks, taps, steps, coef, table
):
    x = real(tokens[...])
    factor = lax.rsqrt(jnp.mean(x * x, axis=1, keepdims=True) + EPSILON)
    for t in range(D // LANES):
        part = slice(t * LANES, (t + 1) * LANES)
        normed[:, part] = low(x[:, part] * factor * real(gain[t : t + 1, :]))

    first = place[0] * SPAN
    lane = iota((1, SPAN), 1)
    for m in range(MICRO):
        part = slice(m * SPAN, (m + 1) * SPAN)
        here = segments[m, :, pl.ds(pl.multiple_of(first, SPAN), SPAN)]
        left = segments[m, :, pl.ds(pl.multiple_of(jnp.maximum(first - LANES, 0), LANES), LANES)]
        right = segments[m, :, pl.ds(pl.multiple_of(jnp.minimum(first + SPAN, 3 * SPAN), LANES), LANES)]
        here, left, right = real(here), real(left), real(right)
        left = jnp.where(place[0] > 0, left, -1.0)
        right = jnp.where(place[0] < 3, right, -1.0)
        left, right = jnp.concatenate([left, left], axis=1), jnp.concatenate([right, right], axis=1)
        rows = []
        for d in range(1, 4):
            before = jnp.where(lane < d, pltpu.roll(left, d, 1), pltpu.roll(here, d, 1))
            rows.append(before == here)
        for d in range(1, 4):
            after = pltpu.roll(here, SPAN - d, 1)
            rows.append(jnp.where(lane >= SPAN - d, pltpu.roll(right, SPAN - d, 1), after) == here)
        prior, final = left[:, LANES - 1 : LANES], here[:, SPAN - 1 :]
        rows += [here == prior, here == final, jnp.broadcast_to(final == prior, here.shape)]
        rows = [row.astype(F32) for row in rows] + [here] + [jnp.zeros((1, SPAN), F32)] * 6
        marks[:, part] = jnp.concatenate(rows, axis=0)

    def columns(rows):
        return jnp.transpose(jnp.concatenate(rows + [jnp.zeros((8 - len(rows), LANES), F32)], axis=0))

    for t in range(CH // LANES):
        part = slice(t * LANES, (t + 1) * LANES)
        rows = [real(kernel[k : k + 1, part]) for k in range(4)] + [real(bias[t : t + 1, :])]
        taps[part, :] = columns(rows)
    steps[...] = columns([heads[0:1, :], jnp.exp(heads[1:2, :])])[0:HEADS, :]
    pick = (iota((LANES, DI), 1) >> 6 == iota((LANES, DI), 0)).astype(F32)
    table[...] = nn(jnp.broadcast_to(heads[2:3, :], (8, LANES)), pick, lax.Precision.HIGHEST)
    for t in range(DI // LANES):
        part = slice(t * LANES, (t + 1) * LANES)
        coef[part, :] = columns([real(gate_gain[t : t + 1, :]), table[0:1, part]])


def products_kernel(gate_weight, out_weight, normed, cotangent, gate, grad_mixed):
    gate[...] = nt(gate_weight[...], normed[...])
    grad_mixed[...] = nt(out_weight[...], cotangent[...])


def prepare_kernel(
    weight, step_weight, normed, rim, gain, taps, steps, marks,
    ci, conv, signal, inflow, maps, raw, cum, step, cols, local, through, state, move, enter, edge
):
    r = pl.program_id(0)
    parts = [slice(m * SPAN, (m + 1) * SPAN) for m in range(MICRO)]

    @pl.when(r == 0)
    def _():
        x = real(rim[...])
        factor = lax.rsqrt(jnp.mean(x * x, axis=1, keepdims=True) + EPSILON)
        for t in range(D // LANES):
            part = slice(t * LANES, (t + 1) * LANES)
            edge[:, part] = low(x[:, part] * factor * real(gain[t : t + 1, :]))
        raw[...] = nt(step_weight[...], normed[...])
        step[...] = jax.nn.softplus(raw[...] + steps[:, 0:1])
        upto = (iota((SPAN, SPAN), 0) <= iota((SPAN, SPAN), 1)).astype(F32)
        for m, part in enumerate(parts):
            here = marks[:, part]
            move[m] = shifts(here, 0, SPAN, -1, 0)
            enter[m] = shifts(here, 0, 16, -1, 16, slice(0, LANES))
            decay = -step[:, part] * steps[:, 1:2]
            total = nn(decay, upto, lax.Precision.HIGHEST)
            cum[:, part] = total
            column = lax.dot_general(
                upto, decay, (((0,), (1,)), ((), ())), precision=lax.Precision.HIGHEST, preferred_element_type=F32
            )
            for g in range(GROUPS):
                cols[g, part, :] = column[:, 4 * g : 4 * g + 4]
            ends = total[:, SPAN - 1 :]
            state[:, part] = here[7:8, :] * jnp.exp(ends - total)
            through[m] = jnp.broadcast_to(here[8:9, 0:1] * jnp.exp(ends), (HEADS, LANES))

    x = low(nt(weight[...], normed[...]))
    ci[...] = x
    halo = low(nt(weight[...], edge[...]))
    flows = []
    for m, part in enumerate(parts):
        moved = nn(x[:, part], move[m])
        edges = nn(halo[:, 16 * m : 16 * m + 16], enter[m])
        total = taps[:, 4:5] + real(x[:, part]) * taps[:, 3:4]
        border = 0.0
        for d in range(1, 4):
            tap = taps[:, 3 - d : 4 - d]
            total = total + moved[:, (d - 1) * SPAN : d * SPAN] * tap
            border = border + edges[:, (d - 1) * LANES : d * LANES] * tap
        total = jnp.concatenate([total[:, :LANES] + border, total[:, LANES:]], axis=1)
        conv[:, part] = total
        flows.append(total * sigmoid(total))

    @pl.when(r == 0)
    def _():
        for flow, part in zip(flows, parts):
            maps[:, part] = flow

    @pl.when(r > 0)
    def _():
        for m, (flow, part) in enumerate(zip(flows, parts)):
            signal[:, part] = low(flow)
            heads = by_head(step, r - 1)[:, part]
            tails = by_head(state, r - 1)[:, part]
            flow = flow * heads
            inflow[:, part] = low(flow)
            local[m] = low(nt(low(flow * tails), low(maps[0:LANES, part])))


def turn_kernel(normed, upstream, left, cot, turned):
    for t in range(4):
        part = slice(t * LANES, (t + 1) * LANES)
        turned[...] = jnp.transpose(real(normed[part, :]))
        for k in range(4):
            left[256 * k : 256 * (k + 1), part] = low(turned[pl.ds(k, 256, stride=4), :])
    cot[...] = low(pltpu.roll(real(upstream[...]), D - 32, 1))


def same_document(marks):
    column = jnp.transpose(jnp.broadcast_to(marks[9:10, :], (8, SPAN)))[:, 0:1]
    return (column == marks[9:10, :]) & (iota((SPAN, SPAN), 0) <= iota((SPAN, SPAN), 1))


def mixing(maps, marks):
    products = tn(maps[0:LANES, :], maps[LANES:, :], lax.Precision.HIGHEST)
    return jnp.where(same_document(marks), products, 0.0)


def within_kernel(inflow, maps, cum, cols, marks, out, table):
    table[...] = mixing(maps, marks)
    half = SPAN // 2

    def heads(g, _):
        results = []
        x4 = inflow[chunk(g), :]
        for h in range(4):
            row, col = cum[pl.ds(4 * g + h, 1), :], cols[g, :, h : h + 1]
            upper = low(jnp.exp(jnp.minimum(row - col[:half], 0.0)) * table[:half, :])
            lower = low(jnp.exp(jnp.minimum(row[:, half:] - col[half:], 0.0)) * table[half:, half:])
            x = x4[h * HDIM : (h + 1) * HDIM, :]
            y = nn(x[:, :half], upper)
            results.append(jnp.concatenate([y[:, :half], y[:, half:] + nn(x[:, half:], lower)], axis=1))
        out[chunk(g), :] = jnp.concatenate(results, axis=0)
        return 0

    lax.fori_loop(0, GROUPS, heads, 0, unroll=4)


def gate_kernel(
    inside, enter, last, maps, signal, gate, grad, cum, marks, coef,
    gated_low, grad_gate, grad_scan, carried_sum, skip_sum, gain_sum, grad_state, grad_read, scan, entry
):
    entry[...] = marks[6:7, :] * jnp.exp(cum[...])
    reads = low(maps[LANES:, :])

    @pl.when(pl.program_id(0) == 0)
    def _():
        gain_sum[...] = jnp.zeros_like(gain_sum)

    def forward(r, sums):
        carried = nn(enter[0, chunk(r), :] + last[0, chunk(r), :], reads) * by_head(entry, r)
        total = inside[chunk(r), :] + carried + coef[chunk(r), 1:2] * real(signal[chunk(r), :])
        scan[chunk(r), :] = total
        z = gate[chunk(r), :]
        gated = total * (z * sigmoid(z))
        up = grad[chunk(r), :] * coef[chunk(r), 0:1]
        squares, cross = sums
        return (
            squares + jnp.sum(gated * gated, axis=0, keepdims=True),
            cross + jnp.sum(gated * up, axis=0, keepdims=True),
        )

    nothing = jnp.zeros((1, SPAN), F32)
    squares, cross = lax.fori_loop(0, 8, forward, (nothing, nothing), unroll=8)
    factor = lax.rsqrt(squares * (1.0 / DI) + EPSILON)
    pull = factor * factor * cross * (1.0 / DI)
    grad_read[...] = jnp.zeros_like(grad_read)

    def backward(r, _):
        heads = by_head(entry, r)
        state = enter[0, chunk(r), :] + last[0, chunk(r), :]
        carried = nn(state, reads) * heads
        total = scan[chunk(r), :]
        z = gate[chunk(r), :]
        sig = sigmoid(z)
        soft = z * sig
        gated = total * soft
        scaled = gated * factor
        gain = coef[chunk(r), 0:1]
        given = grad[chunk(r), :]
        gated_low[chunk(r), :] = low(scaled * gain)
        share = given * scaled
        gain_sum[chunk(r), :] += share[:, :LANES] + share[:, LANES:]
        back = factor * (given * gain - gated * pull)
        grad_gate[chunk(r), :] = low(back * total * (sig * (1.0 + z * (1.0 - sig))))
        push = back * soft
        grad_scan[chunk(r), :] = low(push)
        put_head_sums(carried_sum, r, push * carried)
        put_head_sums(skip_sum, r, push * real(signal[chunk(r), :]))
        entering = low(push * heads)
        grad_state[0, chunk(r), :] = low(nt(entering, reads))
        grad_read[...] += tn(state, entering)
        return 0

    lax.fori_loop(0, 8, backward, 0, unroll=4)


def within_back_kernel(
    inflow, push, inside, maps, cum, cols, marks, grad_inflow, decay_sum, grad_maps, table, grad_table
):
    table[...] = mixing(maps, marks)
    grad_table[...] = jnp.zeros_like(grad_table)
    half = SPAN // 2

    def heads(g, _):
        x4, d4, results = inflow[chunk(g), :], push[chunk(g), :], []
        above, below = 0.0, 0.0
        for h in range(4):
            rows = slice(h * HDIM, (h + 1) * HDIM)
            row, col = cum[pl.ds(4 * g + h, 1), :], cols[g, :, h : h + 1]
            upper = jnp.exp(jnp.minimum(row - col[:half], 0.0))
            lower = jnp.exp(jnp.minimum(row[:, half:] - col[half:], 0.0))
            x, d = x4[rows, :], d4[rows, :]
            above += upper * tn(x[:, :half], d)
            below += lower * tn(x[:, half:], d[:, half:])
            first = nt(d, low(upper * table[:half, :]))
            second = nt(d[:, half:], low(lower * table[half:, half:]))
            results.append(jnp.concatenate([first, second], axis=1))
        grad_table[:half, :] += above
        grad_table[half:, half:] += below
        back = jnp.concatenate(results, axis=0)
        grad_inflow[chunk(g), :] = low(back)
        put_head_sums(decay_sum, g, real(d4) * inside[chunk(g), :] - real(x4) * back)
        return 0

    lax.fori_loop(0, GROUPS, heads, 0, unroll=4)
    spread = low(jnp.where(same_document(marks), grad_table[...], 0.0))
    grad_maps[0:LANES, :] = nt(low(maps[LANES:, :]), spread)
    grad_maps[LANES:, :] = nn(low(maps[0:LANES, :]), spread)


def state_back_kernel(
    leave, leave_last, enter, enter_last, conv, push, grad_inflow, maps, cum, step, raw, decay_sum, carried_sum, grad_maps, grad_read,
    steps, marks, coef, grad_conv, rim, grad_raw, bias_sum, rate_sum, tail, from_tail, from_step, crossing, grad_write
):
    ends = cum[:, SPAN - 1 : SPAN]
    tail[...] = marks[7:8, :] * jnp.exp(ends - cum[...])
    writes = low(maps[0:LANES, :])
    front = ((iota((16, SPAN), 1) == iota((16, SPAN), 0)) & (iota((16, SPAN), 0) < 3)).astype(jnp.bfloat16)
    grad_write[...] = grad_maps[0:LANES, :]

    def through_silu(r, c, sig, above):
        given = above * (sig * (1.0 + c * (1.0 - sig)))
        given = low(given)
        grad_conv[chunk(r), :] = given
        rim[0, :, chunk(r)] = low(nt(front, given))

    def channels(r, _):
        c = conv[chunk(r), :]
        sig = sigmoid(c)
        signal = c * sig
        heads, tails = by_head(step, r), by_head(tail, r)
        x = signal * heads
        back = leave[0, chunk(r), :] + leave_last[0, chunk(r), :]
        ended = nn(back, writes) * tails
        whole = real(grad_inflow[chunk(r), :]) + ended
        grad_write[...] += tn(back, low(x * tails))
        put_head_sums(from_tail, r, x * ended)
        put_head_sums(from_step, r, whole * signal)
        put_head_sums(crossing, r, real(back) * real(enter[0, chunk(r), :] + enter_last[0, chunk(r), :]))
        through_silu(r, c, sig, whole * heads + coef[chunk(r), 1:2] * real(push[chunk(r), :]))
        return 0

    lax.fori_loop(0, 8, channels, 0, unroll=4)
    c = conv[chunk(8), :]
    through_silu(8, c, sigmoid(c), jnp.concatenate([grad_write[...], grad_maps[LANES:, :] + grad_read[...]], axis=0))
    last = iota((HEADS, SPAN), 1) == SPAN - 1
    passing = marks[8:9, 0:1] * jnp.exp(ends) * jnp.sum(crossing[...], axis=1, keepdims=True)
    tails = jnp.sum(from_tail[...], axis=1, keepdims=True)
    total = decay_sum[...] + carried_sum[...] - from_tail[...] + jnp.where(last, tails + passing, 0.0)
    onward = (iota((SPAN, SPAN), 0) >= iota((SPAN, SPAN), 1)).astype(F32)
    grad_decay = nn(total, onward, lax.Precision.HIGHEST)
    rate = steps[:, 1:2]
    rate_sum[...] = -grad_decay * step[...] * rate
    grad_step = (from_step[...] - grad_decay * rate) * sigmoid(raw[...] + steps[:, 0:1])
    bias_sum[...] = grad_step
    grad_raw[0:HEADS, :] = low(grad_step)
    grad_raw[HEADS:, :] = jnp.zeros((LANES - HEADS, SPAN), jnp.bfloat16)


def conv_back_kernel(grad_conv, ci, rim, taps, marks, grad_ci, sums, move, enter):
    @pl.when(pl.program_id(0) == 0)
    def _():
        for m in range(MICRO):
            here = marks[:, m * SPAN : (m + 1) * SPAN]
            move[m] = shifts(here, 3, SPAN, 1, 0)
            enter[m] = shifts(here, 3, 16, 1, -SPAN, slice(LANES, SPAN))

    totals = [0.0] * 5
    for m in range(MICRO):
        part = slice(m * SPAN, (m + 1) * SPAN)
        given, x = real(grad_conv[:, part]), real(ci[:, part])
        moved = nn(grad_conv[:, part], move[m])
        edges = tn(rim[m], enter[m])
        back = given * taps[:, 3:4]
        totals[3] += given * x
        totals[4] += given
        for d in range(1, 4):
            sooner = moved[:, (d - 1) * SPAN : d * SPAN]
            last = sooner[:, LANES:] + edges[:, (d - 1) * LANES : d * LANES]
            sooner = jnp.concatenate([sooner[:, :LANES], last], axis=1)
            back += sooner * taps[:, 3 - d : 4 - d]
            totals[3 - d] += sooner * x
        grad_ci[:, part] = low(back)
    count = jnp.zeros((ROWS, LANES), F32)
    for k in range(5):
        pick = (iota((LANES, LANES), 1) == k).astype(jnp.bfloat16)
        count += nn(low(totals[k][:, :LANES] + totals[k][:, LANES:]), pick)
    sums[...] = count[:, 0:8]


def call(kernel, grid, ins, outs, scratch, cost, name, mebibytes):
    return pl.pallas_call(
        kernel,
        grid=grid,
        in_specs=[pl.BlockSpec(block, where) for _, block, where in ins],
        out_specs=[pl.BlockSpec(block, where) for _, _, block, where in outs],
        out_shape=[jax.ShapeDtypeStruct(shape, dtype) for shape, dtype, _, _ in outs],
        scratch_shapes=scratch,
        compiler_params=pltpu.CompilerParams(
            vmem_limit_bytes=mebibytes * 2**20, dimension_semantics=("arbitrary",) * len(grid)
        ),
        cost_estimate=pl.CostEstimate(flops=cost, bytes_accessed=20_000_000, transcendentals=0),
        name=name,
    )(*[array for array, _, _ in ins])


def neighbours(value, source, target):
    return lax.ppermute(value, GROUP, [(source, target)])


def chained(local, through, order, beside):
    by_heads = (MICRO, HEADS, HDIM, STATE)

    def joined(arrived):
        total = through[:, :, None, :] * real(arrived).reshape(by_heads) + real(local).reshape(by_heads)
        return low(total).reshape(local.shape)

    one = neighbours(local, order[0], order[1])
    two = neighbours(joined(one), order[1], order[2])
    two, beside = lax.optimization_barrier((two, beside))
    three = neighbours(joined(two), order[2], order[3])
    return (one + two, three), beside


def shards(
    tokens, segments, cotangent, norm_gain, in_weight, conv_kernel, conv_bias, step_bias, decay_log,
    skip_gain, gate_gain, out_weight, master, moment_one, moment_two, step_count
):
    width = MICRO * SPAN
    bf16 = jnp.bfloat16
    spot = position()
    place = lax.axis_index(GROUP)
    one = (MICRO,)
    by_m = lambda m: (0, m)
    whole, first = lambda m: (0, 0), lambda m: (m, 0, 0)
    upstream = cotangent.reshape(width, D)
    turned_weight = in_weight.T
    conv_weight = turned_weight[DI : DI + CH]

    heads = jnp.stack([real(step_bias), real(decay_log), real(skip_gain)])
    heads = jnp.pad(heads, ((0, 5), (0, LANES - HEADS)))
    lines = [v.reshape(-1, LANES) for v in (norm_gain, conv_bias, gate_gain)]
    ins = [tokens.reshape(width, D), segments, lines[0], conv_kernel, lines[1], heads, lines[2]]
    outs = [((width, D), bf16), ((16, width), F32), ((CH, 8), F32), ((HEADS, 8), F32), ((DI, 8), F32)]
    at_start = lambda rank: lambda i: (0,) * rank
    normed_low, marks, taps, steps, coef = pl.pallas_call(
        set_up_kernel,
        grid=(1,),
        out_shape=[jax.ShapeDtypeStruct(*out) for out in outs],
        in_specs=[pl.BlockSpec(memory_space=pltpu.SMEM)] + [pl.BlockSpec(v.shape, at_start(v.ndim)) for v in ins],
        out_specs=[pl.BlockSpec(shape, at_start(len(shape))) for shape, _ in outs],
        scratch_shapes=[pltpu.VMEM((8, DI), F32)],
        compiler_params=pltpu.CompilerParams(vmem_limit_bytes=56 * 2**20),
        name="set_up",
    )(place.reshape(1), *ins)
    mark_in = (marks, (16, SPAN), by_m)
    rim_tokens, normed_low = lax.optimization_barrier((tokens[:, 0, SPAN - 16 :, :], normed_low))
    rim_tokens = lax.ppermute(rim_tokens, GROUP, [(0, 1), (1, 2), (2, 3)])

    whole1, head_rows = lambda r: (0, 0), lambda r: (jnp.maximum(r - 1, 0), 0)
    rows_of = lambda r: jnp.where(r == 0, GROUPS, r - 1)
    by_rows = lambda r: (rows_of(r), 0)
    lot = (HEADS, width)
    ci, conv, signal, inflow, maps, raw, cum, step, cols, local, through = call(
        prepare_kernel, (CH // ROWS,),
        [(turned_weight, (ROWS, D), lambda r: (GROUPS + rows_of(r), 0)),
         (turned_weight, (HEADS, D), lambda r: ((DI + CH) // HEADS, 0)), (normed_low, (width, D), whole1),
         (rim_tokens.reshape(-1, D), (32, D), whole1), (lines[0], lines[0].shape, whole1), (taps, (ROWS, 8), by_rows), (steps, (HEADS, 8), whole1),
         (marks, (16, width), whole1)],
        [((CH, width), bf16, (ROWS, width), by_rows), ((CH, width), F32, (ROWS, width), by_rows),
         ((DI, width), bf16, (ROWS, width), head_rows), ((DI, width), bf16, (ROWS, width), head_rows),
         ((2 * STATE, width), F32, (2 * STATE, width), whole1), (lot, F32, lot, whole1), (lot, F32, lot, whole1),
         (lot, F32, lot, whole1), ((GROUPS, width, 4), F32, (GROUPS, width, 4), lambda r: (0, 0, 0)),
         ((MICRO, DI, STATE), bf16, (MICRO, ROWS, STATE), lambda r: (0, jnp.maximum(r - 1, 0), 0)),
         ((MICRO, HEADS, LANES), F32, (MICRO, HEADS, LANES), lambda r: (0, 0, 0))],
        [pltpu.VMEM(lot, F32), pltpu.VMEM((MICRO, SPAN, 3 * SPAN), bf16), pltpu.VMEM((MICRO, 16, 3 * LANES), bf16),
         pltpu.VMEM((32, D), bf16)],
        10**9, "project_and_convolve", 56,
    )

    tiles = lambda r: (r, 0)
    gate, grad_mixed = call(
        products_kernel, (GROUPS // 2,),
        [(turned_weight, (2 * ROWS, D), tiles), (out_weight, (2 * ROWS, D), tiles), (normed_low, (width, D), whole1),
         (upstream, (width, D), whole1)],
        [((DI, width), F32, (2 * ROWS, width), tiles)] * 2, [], 4 * 10**9, "gate_products", 24,
    )
    tall, few = (DI, SPAN), (HEADS, SPAN)
    state_block = (1, DI, STATE)
    head_ins = [
        (maps, (2 * STATE, SPAN), by_m),
        (cum, few, by_m),
        (cols, (GROUPS, SPAN, 4), lambda m: (0, m, 0)),
        mark_in,
    ]
    table = pltpu.VMEM((SPAN, SPAN), F32)
    (inside,) = call(
        within_kernel, one, [(inflow, tall, by_m)] + head_ins, [((DI, width), F32, tall, by_m)], [table],
        4 * 10**9, "within_blocks", 24,
    )
    enter, (inside, gate, grad_mixed) = chained(local, through, (0, 1, 2, 3), (inside, gate, grad_mixed))

    gated_low, grad_gate, push, carried_sum, skip_sum, gain_sum, grad_state, grad_read = call(
        gate_kernel, one,
        [(inside, tall, by_m), (enter[0], state_block, first), (enter[1], state_block, first), (maps, (2 * STATE, SPAN), by_m), (signal, tall, by_m),
         (gate, tall, by_m), (grad_mixed, tall, by_m), (cum, (HEADS, SPAN), by_m), mark_in, (coef, (DI, 8), whole)],
        [((DI, width), bf16, tall, by_m), ((DI, width), bf16, tall, by_m), ((DI, width), bf16, tall, by_m),
         ((HEADS, width), F32, (HEADS, SPAN), by_m), ((HEADS, width), F32, (HEADS, SPAN), by_m),
         ((DI, LANES), F32, (DI, LANES), whole), ((MICRO, DI, STATE), bf16, state_block, first),
         ((STATE, width), F32, (STATE, SPAN), by_m)],
        [pltpu.VMEM((DI, SPAN), F32), pltpu.VMEM((HEADS, SPAN), F32)], 2 * 10**9, "gate_and_back", 50,
    )
    grad_inflow, decay_sum, grad_maps = call(
        within_back_kernel, one, [(inflow, tall, by_m), (push, tall, by_m), (inside, tall, by_m)] + head_ins,
        [((DI, width), bf16, tall, by_m), ((HEADS, width), F32, few, by_m),
         ((2 * STATE, width), F32, (2 * STATE, SPAN), by_m)],
        [table, table], 8 * 10**9, "within_blocks_back", 56,
    )
    left, cot = call(
        turn_kernel, (1,), [(normed_low, (width, D), whole), (upstream, (width, D), whole)],
        [((D, width), bf16, (D, width), whole), ((width, D), bf16, (width, D), whole)],
        [pltpu.VMEM((D, LANES), F32)], 10**6, "turn", 14,
    )
    leave, (grad_inflow, decay_sum, grad_maps, left, cot) = chained(
        grad_state, through, (3, 2, 1, 0), (grad_inflow, decay_sum, grad_maps, left, cot)
    )

    grad_conv, rim, grad_raw, bias_sum, rate_sum = call(
        state_back_kernel, one,
        [(leave[0], state_block, first), (leave[1], state_block, first), (enter[0], state_block, first),
         (enter[1], state_block, first), (conv, (CH, SPAN), by_m), (push, tall, by_m),
         (grad_inflow, tall, by_m), (maps, (2 * STATE, SPAN), by_m), (cum, few, by_m), (step, few, by_m), (raw, few, by_m),
         (decay_sum, few, by_m), (carried_sum, few, by_m), (grad_maps, (2 * STATE, SPAN), by_m),
         (grad_read, (STATE, SPAN), by_m), (steps, (HEADS, 8), whole), mark_in, (coef, (DI, 8), whole)],
        [((CH, width), bf16, (CH, SPAN), by_m), ((MICRO, 16, CH), bf16, (1, 16, CH), first),
         ((LANES, width), bf16, (LANES, SPAN), by_m), ((HEADS, width), F32, few, by_m), ((HEADS, width), F32, few, by_m)],
        [pltpu.VMEM(few, F32), pltpu.VMEM(few, F32), pltpu.VMEM(few, F32), pltpu.VMEM((HEADS, LANES), F32),
         pltpu.VMEM((STATE, SPAN), F32)], 10**9, "state_and_silu_back", 56,
    )
    next_rim = lax.ppermute(rim, GROUP, [(1, 0), (2, 1), (3, 2)])
    early = tn(grad_gate, turned_weight[:DI])
    next_rim, early = lax.optimization_barrier((next_rim, early))

    by_r = lambda r: (r, 0)
    grad_ci, tap_sums = call(
        conv_back_kernel, (CH // ROWS,),
        [(grad_conv, (ROWS, width), by_r), (ci, (ROWS, width), by_r), (next_rim, (MICRO, 16, ROWS), lambda r: (0, 0, r)),
         (taps, (ROWS, 8), by_r), (marks, (16, width), lambda r: (0, 0))],
        [((CH, width), bf16, (ROWS, width), by_r), ((CH, 8), F32, (ROWS, 8), by_r)],
        [pltpu.VMEM((MICRO, SPAN, 3 * SPAN), bf16), pltpu.VMEM((MICRO, 16, 3 * LANES), bf16)], 10**8, "convolution_back", 56,
    )

    middle = [tap_sums[:, :5].T.reshape(-1), jnp.sum(bias_sum, axis=1), jnp.sum(rate_sum, axis=1)]
    middle += [jnp.sum(skip_sum, axis=1), jnp.sum(gain_sum, axis=1), jnp.zeros((32 + 5 * LANES,), F32)]
    middle = jnp.concatenate(middle).reshape(-1, LANES)
    packed = pack(spot, left, grad_gate, grad_ci, grad_raw, gated_low, cot, middle)
    packed, late = lax.optimization_barrier((packed, (grad_gate, grad_ci, grad_raw)))
    rows_in = real(tokens.reshape(width, D))
    norm_back = jax.vjp(norm_piece, rows_in, real(norm_gain))[1]
    grad_normed = early + tn(late[1], conv_weight) + tn(late[2][:HEADS], turned_weight[DI + CH :])
    grad_rows, grad_norm_gain = norm_back(grad_normed)

    def finish(inputs):
        gated_low, grad_rows = inputs
        output = low(rows_in + tn(gated_low, out_weight)).reshape(tokens.shape)
        return output, low(real(upstream) + grad_rows).reshape(tokens.shape)

    piece, (output, input_grad) = reduce_pieces(
        *packed, grad_norm_gain.reshape(-1, LANES), finish, (gated_low, grad_rows)
    )

    skew = (12 * lax.axis_index("x")) % 16
    offset = PIECE * place - skew
    line = offset + iota((PIECE, 1), 0)
    own = jnp.where((line >= 0) & (line < SHARD_LINES), piece, 0.0)
    squares = sent_to_all(jnp.sum(own * own).reshape(1, 1), EVERY).reshape(1, -1)
    core, high = lax.axis_index("core") == 0, lax.axis_index("zh") == 0
    pair = [piece, swap_cores(piece)]
    pair = jnp.concatenate([jnp.where(core, *pair), jnp.where(core, *pair[::-1])])
    both = [pair, lax.ppermute(pair, "zh", [(0, 1), (1, 0)])]
    step_real = real(step_count[0])
    scales = jnp.stack([1.0 / (1.0 - jnp.power(BETA_ONE, step_real)), 1.0 / (1.0 - jnp.power(BETA_TWO, step_real))])
    both, squares = lax.optimization_barrier((both, squares))
    mine = own_update(offset, scales, squares, piece, master, moment_one, moment_two)

    def rest(inputs):
        both, squares, moments = inputs
        window = jnp.concatenate([jnp.where(high, *both), jnp.where(high, *both[::-1])])
        shard = lax.dynamic_slice(window, (skew, 0), (SHARD_LINES, LANES)).reshape(-1)
        clip_factor = MAX_NORM / jnp.maximum(jnp.sqrt(jnp.sum(squares)), MAX_NORM)
        return shard, adam_step(shard * clip_factor, *moments, scales[0], scales[1])

    moments = (master, moment_one, moment_two)
    pieces, (shard, results) = gather_pieces(mine, rest, (both, squares, moments))
    copies = unpack(spot, pieces).reshape(-1)
    return (output, input_grad, shard, *results, copies)


def solution(mesh):
    finer = Mesh(mesh.devices.reshape(4, 2, 4, 2, 2), ("y", "zl", "x", "zh", "core"))
    return jax.shard_map(
        shards,
        mesh=finer,
        in_specs=(
            P(None, DP, GROUP, None),
            P(None, DP, None),
            P(None, DP, GROUP, None),
            P(),
            P(),
            P(),
            P(),
            P(),
            P(),
            P(),
            P(),
            P(),
            P(DP),
            P(DP),
            P(DP),
            P(),
        ),
        out_specs=(
            P(None, DP, GROUP, None),
            P(None, DP, GROUP, None),
            P(DP),
            P(DP),
            P(DP),
            P(DP),
            P(),
        ),
        check_vma=False,
    )
```
